32 devices in a mesh: row: 8 (over z, core), col: 4 (over y, x).
Axes of the slice: x: 2, y: 2, z: 4, core: 2. Of those that a mesh axis runs over, the one named last changes fastest.
Arguments:
- hidden_in: bfloat16 [16384, 1024], P(('row', 'col')), may hold values from -7.2 to 7.2
- out_cotangent: bfloat16 [16384, 1024], P(('row', 'col')), may hold values from -6 to 6
- query_weight: bfloat16 [1024, 1024], P(('row', 'col')), may hold values from -0.046875 to 0.046875
- key_weight: bfloat16 [1024, 1024], P(('row', 'col')), may hold values from -0.1875 to 0.1875
- value_weight: bfloat16 [1024, 1024], P(('row', 'col')), may hold values from -0.1875 to 0.1875
- output_weight: bfloat16 [1024, 1024], P(('row', 'col')), may hold values from -0.75 to 0.75
- attn_gain: bfloat16 [1024], P(('row', 'col')), may hold values from 0.5 to 1.5
- relative_table: bfloat16 [512], P(('row', 'col')), may hold values from -3.1875 to 3.1875
- horiz_table: bfloat16 [512], P(('row', 'col')), may hold values from -3.1875 to 3.1875
- vert_table: bfloat16 [512], P(('row', 'col')), may hold values from -3.1875 to 3.1875
- ffn_gain: bfloat16 [1024], P(('row', 'col')), may hold values from 0.5 to 1.5
- gate_weight: bfloat16 [1024, 2816], P(('row', 'col')), may hold values from -0.1875 to 0.1875
- up_weight: bfloat16 [1024, 2816], P(('row', 'col')), may hold values from -0.1875 to 0.1875
- down_weight: bfloat16 [2816, 1024], P(('row', 'col')), may hold values from -0.109375 to 0.109375
- key_keep: int32 [16384], replicated, may hold values from 0 to 1, as said below
- halo_rows: int32 [32, 4, 128], replicated, may hold values from 0 to 511, as said below
- relative_bucket: int32 [16384, 1024], P(('row', 'col')), may hold values from 0 to 31
- horiz_bucket: int32 [16384, 1024], P(('row', 'col')), may hold values from 0 to 31
- vert_bucket: int32 [16384, 1024], P(('row', 'col')), may hold values from 0 to 31
Outputs:
- layer_out: bfloat16 [16384, 1024], P(('row', 'col'))
- input_grad: bfloat16 [16384, 1024], P(('row', 'col'))
- query_grad: float32 [1024, 1024], P(('row', 'col'))
- key_grad: float32 [1024, 1024], P(('row', 'col'))
- value_grad: float32 [1024, 1024], P(('row', 'col'))
- output_grad: float32 [1024, 1024], P(('row', 'col'))
- attn_gain_grad: float32 [1024], P(('row', 'col'))
- relative_grad: float32 [512], P(('row', 'col'))
- horiz_grad: float32 [512], P(('row', 'col'))
- vert_grad: float32 [512], P(('row', 'col'))
- ffn_gain_grad: float32 [1024], P(('row', 'col'))
- gate_grad: float32 [1024, 2816], P(('row', 'col'))
- up_grad: float32 [1024, 2816], P(('row', 'col'))
- down_grad: float32 [2816, 1024], P(('row', 'col'))
- residual_rms: float32 [3], replicated
The draws below stay inside these ranges and needn't reach their ends.
Inputs may be any that keep to these rules, and one draw needn't show every extreme that they name: `key_keep`: the first token of every region is kept; about a quarter of the other tokens are kept. `halo_rows`: each list holds 128 distinct rows of its region, counted from the region's first row; direction 0 is lent to the region above, 1 below, 2 to the left, 3 to the right.
All inputs are finite; a program needn't handle non-finite values.
Results may differ from the reference program's by a relative error of at most 0.015.
The reference program's roundings to bfloat16 on the way count: a program that leaves them out, or rounds other values in their place, can miss the bound.
Values may be sent and summed in bfloat16 or wider, within the bound.
No kernel may reach another device: no remote copies, remote signals or barrier semaphores. Data moves between devices by JAX's collectives and lax.ppermute only.
A program may use at most 320 MiB of HBM per device.

```python
import jax
import jax.numpy as jnp
from jax import lax

D = 1024
FF = 2816
HEADS = 16
HEAD_DIM = 64
BUCKETS = 32
TOK_DEV = 512
HALO = 128
KEYS = 1024
REGIONS = 32
TOKENS = 16384
N_ROW = 8
N_COL = 4


def draw_hidden_in(key, part):
    key = jax.random.fold_in(key, 11)
    position = jnp.arange(TOKENS, dtype=jnp.float32)[:, None] / TOKENS
    base = jnp.clip(jax.random.normal(key, (TOKENS, D), jnp.float32), -4.0, 4.0)
    scale = 0.6 + 1.2 * position
    return (base * scale).astype(jnp.bfloat16)


def draw_key_keep(key, part):
    key = jax.random.fold_in(key, 23)
    visible = (jax.random.randint(key, (TOKENS,), 0, 4) == 0).astype(jnp.int32)
    leading = (jnp.arange(TOKENS, dtype=jnp.int32) % TOK_DEV == 0).astype(jnp.int32)
    return jnp.maximum(visible, leading)


def draw_halo_rows(key, part):
    key = jax.random.fold_in(key, 37)
    subkeys = jax.random.split(key, REGIONS * 4)
    chosen = jax.vmap(lambda subkey: jax.random.permutation(subkey, TOK_DEV)[:HALO])(subkeys)
    return chosen.reshape(REGIONS, 4, HALO).astype(jnp.int32)


def plant(values, rng, smallest, top_value):
    index_at = [jax.random.randint(jax.random.fold_in(rng, axis), (), 0, length) for axis, length in enumerate(values.shape)]
    longest = values.shape.index(max(values.shape))
    beside = index_at[:longest] + [(index_at[longest] + 1) % values.shape[longest]] + index_at[longest + 1:]
    return values.at[tuple(index_at)].set(smallest).at[tuple(beside)].set(top_value)


def shard_levels(key, dims, cuts, least, largest):
    factor_of, own = 1.0, jax.random.fold_in(key, 6)
    for dim, shards_of in cuts:
        steps = jnp.exp(jax.random.uniform(jax.random.fold_in(own, dim), (shards_of,), jnp.float32, least / len(cuts), largest / len(cuts)))
        factor_of = factor_of * jnp.repeat(steps, dims[dim] // shards_of).reshape([-1 if axis == dim else 1 for axis in range(len(dims))])
    return factor_of


def bell_draw(own_key, extent, spread, limit, cuts=(), held_as=jnp.bfloat16):
    level = shard_levels(own_key, extent, cuts, -0.22, 0.18) if cuts else 1.0
    result = jax.random.normal(own_key, extent, jnp.float32) * spread * level
    return jnp.minimum(jnp.maximum(result, -limit), limit).astype(held_as)


def setup_inputs(seed: int = 0) -> dict:
    arg_keys = jax.random.split(jax.random.key(seed), 20)
    hidden_in = draw_hidden_in(jax.random.fold_in(arg_keys[19], 71), 0)
    out_cotangent = bell_draw(arg_keys[1], (TOKENS, D), 1.0, 6.0, ((0, 32),))
    query_weight = bell_draw(arg_keys[2], (D, D), (16 * D) ** -0.5, 0.046875, ((0, 32),))
    key_weight = bell_draw(arg_keys[3], (D, D), D ** -0.5, 0.1875, ((0, 32),))
    value_weight = bell_draw(arg_keys[4], (D, D), D ** -0.5, 0.1875, ((0, 32),))
    output_weight = bell_draw(arg_keys[5], (D, D), (D // 16) ** -0.5, 0.75, ((0, 32),))
    attn_gain = jnp.clip(1.0 + 0.1 * jax.random.normal(arg_keys[6], (D,), jnp.float32), 0.5, 1.5).astype(jnp.bfloat16)
    relative_table = bell_draw(arg_keys[7], (BUCKETS * HEADS,), 0.8, 3.1875, ((0, 32),))
    horiz_table = bell_draw(arg_keys[8], (BUCKETS * HEADS,), 0.8, 3.1875, ((0, 32),))
    vert_table = bell_draw(arg_keys[9], (BUCKETS * HEADS,), 0.8, 3.1875, ((0, 32),))
    ffn_gain = jnp.clip(1.0 + 0.1 * jax.random.normal(arg_keys[10], (D,), jnp.float32), 0.5, 1.5).astype(jnp.bfloat16)
    gate_weight = bell_draw(arg_keys[11], (D, FF), D ** -0.5, 0.1875, ((0, 32),))
    up_weight = bell_draw(arg_keys[12], (D, FF), D ** -0.5, 0.1875, ((0, 32),))
    down_weight = bell_draw(arg_keys[13], (FF, D), FF ** -0.5, 0.109375, ((0, 32),))
    key_keep = draw_key_keep(jax.random.fold_in(arg_keys[19], 71), 0)
    halo_rows = draw_halo_rows(jax.random.fold_in(arg_keys[19], 71), 0)
    relative_bucket = plant(jax.random.randint(arg_keys[16], (TOKENS, KEYS), 0, BUCKETS), jax.random.fold_in(arg_keys[16], 1), 0, BUCKETS - 1).astype(jnp.int32)
    horiz_bucket = plant(jax.random.randint(arg_keys[17], (TOKENS, KEYS), 0, BUCKETS), jax.random.fold_in(arg_keys[17], 1), 0, BUCKETS - 1).astype(jnp.int32)
    vert_bucket = plant(jax.random.randint(arg_keys[18], (TOKENS, KEYS), 0, BUCKETS), jax.random.fold_in(arg_keys[18], 1), 0, BUCKETS - 1).astype(jnp.int32)
    return {"hidden_in": hidden_in, "out_cotangent": out_cotangent, "query_weight": query_weight, "key_weight": key_weight, "value_weight": value_weight, "output_weight": output_weight, "attn_gain": attn_gain, "relative_table": relative_table, "horiz_table": horiz_table, "vert_table": vert_table, "ffn_gain": ffn_gain, "gate_weight": gate_weight, "up_weight": up_weight, "down_weight": down_weight, "key_keep": key_keep, "halo_rows": halo_rows, "relative_bucket": relative_bucket, "horiz_bucket": horiz_bucket, "vert_bucket": vert_bucket}


@jax.custom_vjp
def low(v):
    return lax.optimization_barrier(v.astype(jnp.bfloat16)).astype(jnp.float32)

@jax.custom_vjp
def low_back(v):
    return v

def low_keep(v):
    return (low(v), None)

def low_pass(kept, grad):
    return (grad,)

def back_keep(v):
    return (v, None)

def back_low(kept, grad):
    return (low(grad),)
low.defvjp(low_keep, low_pass)
low_back.defvjp(back_keep, back_low)
EPS = 1e-06
masked_score = -1e+30

def matmul_hi(left, right):
    return jnp.dot(left, right, precision=lax.Precision.HIGHEST, preferred_element_type=jnp.float32)

def norm_rows(values, gain_row):
    return values * lax.rsqrt(lax.optimization_barrier(jnp.mean(values * values, -1, keepdims=True)) + EPS) * gain_row

def region_keys(halo_rows, key_keep):
    region_ids = jnp.arange(REGIONS, dtype=jnp.int32)
    grid_row = region_ids // N_COL
    grid_col = region_ids % N_COL
    neighbours = jnp.stack([region_ids - N_COL, region_ids + N_COL, region_ids - 1, region_ids + 1], 1)
    present = jnp.stack([grid_row > 0, grid_row < N_ROW - 1, grid_col > 0, grid_col < N_COL - 1], 1).astype(jnp.int32)
    list_ids = jnp.array([1, 0, 3, 2], dtype=jnp.int32)
    clipped = jnp.clip(neighbours, 0, REGIONS - 1).astype(jnp.int32)
    their_lists = halo_rows[clipped, list_ids[None, :]]
    global_rows = (clipped[:, :, None] * TOK_DEV + their_lists).astype(jnp.int32)
    halo_keep = key_keep[global_rows] * present[:, :, None]
    own_keep = key_keep.reshape(REGIONS, TOK_DEV)
    key_valid = jnp.concatenate([own_keep, halo_keep.reshape(REGIONS, 4 * HALO)], 1)
    return (global_rows.reshape(REGIONS, 4 * HALO), key_valid)

def forward(x_input, params, key_rows, key_valid, relative_bucket, horiz_bucket, vert_bucket):
    w_query, w_key, w_value, w_output, gain_attn, table_rel, table_hor, table_ver, gain_ffn, w_gate, w_up, w_down = params
    tables = (table_rel.reshape(BUCKETS, HEADS), table_hor.reshape(BUCKETS, HEADS), table_ver.reshape(BUCKETS, HEADS))
    normed_one = low(norm_rows(x_input, gain_attn))
    queries = low_back(low(matmul_hi(normed_one, w_query)))
    key_all = low_back(low(matmul_hi(normed_one, w_key)))
    value_all = low_back(low(matmul_hi(normed_one, w_value)))
    region_k = jnp.concatenate([key_all.reshape(REGIONS, TOK_DEV, D), key_all[key_rows]], 1)
    region_v = jnp.concatenate([value_all.reshape(REGIONS, TOK_DEV, D), value_all[key_rows]], 1)

    def attend(pieces):
        query_rows, key_block, value_block, rel_rows, hor_rows, ver_rows, valid_row = pieces
        query_heads = query_rows.reshape(TOK_DEV, HEADS, HEAD_DIM)
        key_heads = key_block.reshape(KEYS, HEADS, HEAD_DIM)
        value_heads = value_block.reshape(KEYS, HEADS, HEAD_DIM)
        scores = jnp.einsum('qhd,khd->hqk', query_heads, key_heads, precision=lax.Precision.HIGHEST)
        layout = tables[0][rel_rows] + tables[1][hor_rows] + tables[2][ver_rows]
        scores = low_back(scores + jnp.transpose(layout, (2, 0, 1)))
        scores = jnp.where(valid_row[None, None, :] > 0, scores, masked_score)
        row_max = lax.optimization_barrier(jnp.max(scores, -1, keepdims=True))
        exp_scores = jnp.exp(scores - row_max)
        attn_probs = low(exp_scores / lax.optimization_barrier(jnp.sum(exp_scores, -1, keepdims=True)))
        head_mix = jnp.einsum('hqk,khd->qhd', attn_probs, value_heads, precision=lax.Precision.HIGHEST)
        return head_mix.reshape(TOK_DEV, D)
    attended = lax.map(jax.checkpoint(attend), (queries.reshape(REGIONS, TOK_DEV, D), region_k, region_v, relative_bucket.reshape(REGIONS, TOK_DEV, KEYS), horiz_bucket.reshape(REGIONS, TOK_DEV, KEYS), vert_bucket.reshape(REGIONS, TOK_DEV, KEYS), key_valid))
    attended = low_back(low(attended.reshape(TOKENS, D)))
    attn_branch = low_back(matmul_hi(attended, w_output))
    x_middle = x_input + attn_branch
    normed_two = low(norm_rows(x_middle, gain_ffn))
    gate_pre = low_back(matmul_hi(normed_two, w_gate))
    up_pre = low_back(matmul_hi(normed_two, w_up))
    activated = low(jax.nn.gelu(gate_pre, approximate=True) * up_pre)
    ffn_branch = low_back(matmul_hi(activated, w_down))
    return (x_middle + ffn_branch, x_middle)

def reference(hidden_in, out_cotangent, query_weight, key_weight, value_weight, output_weight, attn_gain, relative_table, horiz_table, vert_table, ffn_gain, gate_weight, up_weight, down_weight, key_keep, halo_rows, relative_bucket, horiz_bucket, vert_bucket):
    key_rows, key_valid = region_keys(halo_rows, key_keep)
    weights = tuple((weight_arr.astype(jnp.float32) for weight_arr in (query_weight, key_weight, value_weight, output_weight, attn_gain, relative_table, horiz_table, vert_table, ffn_gain, gate_weight, up_weight, down_weight)))
    x_input = hidden_in.astype(jnp.float32)

    def run(x_value, *params):
        return forward(x_value, params, key_rows, key_valid, relative_bucket, horiz_bucket, vert_bucket)
    x_final, pull, x_middle = jax.vjp(run, x_input, *weights, has_aux=True)
    grads = pull(out_cotangent.astype(jnp.float32))
    keep_float = key_keep.astype(jnp.float32)
    valid_count = jnp.sum(keep_float)

    def rms_of(values):
        return jnp.sqrt(jnp.sum(keep_float * lax.optimization_barrier(jnp.sum(values * values, -1))) / (valid_count * D))
    residual_rms = jnp.stack([rms_of(x_input), rms_of(x_middle), rms_of(x_final)])
    return (x_final.astype(jnp.bfloat16), grads[0].astype(jnp.bfloat16), grads[1], grads[2], grads[3], grads[4], grads[5], grads[6], grads[7], grads[8], grads[9], grads[10], grads[11], grads[12], residual_rms)
```

```python
import functools

import jax
import jax.numpy as jnp
from jax import lax
from jax.experimental import pallas as pl
from jax.experimental.pallas import tpu as pltpu
from jax.sharding import PartitionSpec as P

D = 1024
HEADS = 16
HEAD_DIM = 64
BUCKETS = 32
TABLES = 3

EPS = 1e-06
masked_score = -1e30
FEW = 384
COLS = 128
ROWS = 64
GROUP = 4
WIDE = GROUP * HEAD_DIM
HIST_ROWS = 16
FF_TILE = 256
VMEM_LIMIT = 56 * 1024 * 1024
BF = jnp.bfloat16
F32 = jnp.float32


def shifted(block, axis):
    count = lax.axis_size(axis)
    forward = [(i, i + 1) for i in range(count - 1)]
    backward = [(target, source) for source, target in forward]
    return (
        lax.ppermute(block[1], axis, forward),
        lax.ppermute(block[0], axis, backward),
    )


def norm_rows(values, gain_row):
    return values * lax.rsqrt(jnp.mean(values * values, -1, keepdims=True) + EPS) * gain_row


def stages_of(kind):
    row_bits = [("row", bit) for bit in range(lax.axis_size("row").bit_length() - 1)]
    col_bits = [("col", bit) for bit in range(lax.axis_size("col").bit_length() - 1)]
    if kind == 0:
        return row_bits[:1] + col_bits + row_bits[1:]
    if kind == 1:
        return row_bits[:1] + col_bits[::-1] + row_bits[1:]
    return row_bits[:2] + col_bits + row_bits[2:]


def mask_of(stage):
    axis, bit = stage
    return (lax.axis_size("col") if axis == "row" else 1) << bit


def scatter_masks(kind):
    masks = [0]
    for stage in stages_of(kind)[::-1]:
        masks = masks + [mask ^ mask_of(stage) for mask in masks]
    return tuple(masks)


def gather_masks(kind):
    masks = [0]
    for stage in stages_of(kind)[:0:-1]:
        masks = masks + [mask ^ mask_of(stage) for mask in masks]
    return tuple(masks), mask_of(("row", 0))


def exchange(values, stage):
    axis, bit = stage
    pairs = [(i, i ^ (1 << bit)) for i in range(lax.axis_size(axis))]
    return lax.ppermute(values, axis, pairs)


def after(values, *earlier):
    return lax.optimization_barrier((values, earlier))[0]


class Gather:
    def __init__(self, shard, kind, both=False):
        self.held = shard[None]
        self.stages = stages_of(kind)[::-1] if both else stages_of(kind)[:0:-1]
        self.flight = None

    def send(self):
        if self.stages:
            self.flight = exchange(self.held, self.stages.pop(0))
        return self.held

    def land(self, *done):
        if self.flight is not None:
            if done:
                self.flight = after(self.flight, *done)
            self.held = jnp.concatenate([self.held, self.flight], 0)
            self.flight = None


class Scatter:
    def __init__(self, sent, kept, kind):
        self.stages = stages_of(kind)
        self.parts = [kept]
        self.sent = sent

    def land(self, flight):
        self.parts.append(flight)
        half = flight.shape[0] // 2
        self.sent = None
        if self.stages:
            self.sent = sum(part[half : 2 * half].astype(F32) for part in self.parts).astype(BF)

    def total(self):
        return sum(part[0].astype(F32) for part in self.parts)


class Summing:
    def __init__(self, values):
        self.stages = stages_of(0)
        self.sent = values

    def land(self, flight):
        self.value = self.sent + flight
        self.sent = self.value if self.stages else None


class Rounds:
    def __init__(self):
        self.chains = []
        self.flights = []

    def land(self, *done):
        for chains, flight in self.flights:
            if done:
                flight = after(flight, *done)
            at = 0
            for chain in chains:
                width = chain.sent.shape[-1]
                chain.land(flight[..., at : at + width])
                at += width
        self.flights = []
        self.chains = [chain for chain in self.chains if chain.sent is not None]

    def send(self):
        groups = {}
        for chain in self.chains:
            alone = id(chain) if chain.sent.shape[0] > 4 else 0
            alike = (chain.stages.pop(0), chain.sent.shape[:-1], alone)
            groups.setdefault(alike, []).append(chain)
        sent = []
        for (stage, *_), chains in groups.items():
            values = [chain.sent for chain in chains]
            values = jnp.concatenate(values, -1) if len(values) > 1 else values[0]
            self.flights.append((chains, exchange(values, stage)))
            sent.append(values)
        return sent

    def turn(self, *done):
        self.land(*done)
        return self.send()


def dot_nn(left, right):
    return lax.dot_general(left, right, (((1,), (0,)), ((), ())), preferred_element_type=F32)


def dot_nt(left, right):
    return lax.dot_general(left, right, (((1,), (1,)), ((), ())), preferred_element_type=F32)


def dot_tn(left, right):
    return lax.dot_general(left, right, (((0,), (0,)), ((), ())), preferred_element_type=F32)


LANE_GATHER = lax.GatherDimensionNumbers(
    offset_dims=(),
    collapsed_slice_dims=(1,),
    start_index_map=(1,),
    operand_batching_dims=(0,),
    start_indices_batching_dims=(0,),
)


def lane_gather(rows, index):
    return lax.gather(
        rows,
        index[:, :, None],
        LANE_GATHER,
        (1, 1),
        mode=lax.GatherScatterMode.PROMISE_IN_BOUNDS,
    )


def lanes_of(group):
    if isinstance(group, int):
        return pl.ds(group * WIDE, WIDE)
    return pl.ds(pl.multiple_of(group * WIDE, WIDE), WIDE)


def held_type(height):
    return BF if height % 16 == 0 else F32


def reordered(low, high, masks, device):
    place = [0] * len(masks)
    for at, mask in enumerate(masks):
        place[mask] = at
    index = jnp.array(place, jnp.int32)[jnp.array(masks, jnp.int32) ^ device]
    both = jnp.concatenate([low, high], 0)[index]
    return both[: len(masks) // 2], both[len(masks) // 2 :]


def placed(owner, height):
    start = owner * height
    if isinstance(start, int):
        return pl.ds(start, height)
    if height % 8 == 0:
        start = pl.multiple_of(start, height & -height)
    return pl.ds(start, height)


def join_pieces(own_ref, other_ref, joined_ref, device, masks, core_mask):
    height = own_ref.shape[1]
    for p, mask in enumerate(masks):
        joined_ref[placed(device ^ mask, height), :] = own_ref[p].astype(joined_ref.dtype)
        joined_ref[placed(device ^ mask ^ core_mask, height), :] = other_ref[p].astype(
            joined_ref.dtype
        )


def part_pieces(joined_ref, sent_ref, kept_ref, device, masks, at=0):
    half, height = kept_ref.shape[:2]
    lanes = slice(at, at + joined_ref.shape[1])
    for p, mask in enumerate(masks):
        target_ref = kept_ref if p < half else sent_ref
        target_ref[p % half, :, lanes] = joined_ref[placed(device ^ mask, height), :].astype(BF)


def head_masks():
    lane = lax.broadcasted_iota(jnp.int32, (1, WIDE), 1) >> 6
    return [(lane == h).astype(F32).astype(BF) for h in range(GROUP)]


def stack_heads(block, masks):
    return jnp.concatenate([block * mask for mask in masks], 0)


def unpack_codes(codes_ref, split_ref, keys):
    code = codes_ref[:keys, :]
    split_ref[0, :keys, :] = code & 31
    split_ref[1, :keys, :] = (code >> 5) & 31
    split_ref[2, :keys, :] = code >> 10


def bias_of(split_ref, table_ref, head, keys):
    spread = [
        jnp.broadcast_to(table_ref[pl.ds(t * HEADS + head, 1), :], (keys, COLS))
        for t in range(TABLES)
    ]
    found = [lane_gather(spread[t], split_ref[t, :keys, :]) for t in range(TABLES)]
    return found[0] + found[1] + found[2]


def bias_kernel(codes_ref, table_ref, bias_ref, split_ref, *, first_head):
    unpack_codes(codes_ref, split_ref, FEW)

    @pl.loop(0, bias_ref.shape[0])
    def _(head):
        bias_ref[head] = bias_of(split_ref, table_ref, first_head + head, FEW)


def layout_bias(codes, table_lanes, first_head):
    tokens = codes.shape[1]
    return pl.pallas_call(
        functools.partial(bias_kernel, first_head=first_head),
        grid=(tokens // COLS,),
        in_specs=[
            pl.BlockSpec((FEW, COLS), lambda i: (0, i)),
            pl.BlockSpec(table_lanes.shape, lambda i: (0, 0)),
        ],
        out_specs=pl.BlockSpec((HEADS // 2, FEW, COLS), lambda i: (0, 0, i)),
        out_shape=jax.ShapeDtypeStruct((HEADS // 2, FEW, tokens), F32),
        scratch_shapes=[pltpu.VMEM((TABLES, FEW, COLS), jnp.int32)],
        compiler_params=pltpu.CompilerParams(vmem_limit_bytes=VMEM_LIMIT),
        cost_estimate=pl.CostEstimate(
            flops=16_000_000_000, bytes_accessed=7_000_000, transcendentals=0
        ),
        name="layout_bias",
    )(codes, table_lanes)


def each_group(run, groups, short):
    if short:
        for group in range(groups):
            run(group)
    else:
        lax.fori_loop(0, groups, lambda group, carry: (run(group), carry)[1], 0)


def own_blocks(turned):
    return jnp.concatenate(
        [
            turned[h * HEAD_DIM : (h + 1) * HEAD_DIM, h * COLS : (h + 1) * COLS]
            for h in range(GROUP)
        ],
        0,
    )


def attend_kernel(
    count_ref,
    normed_ref,
    picked_ref,
    wq_ref,
    wk_ref,
    wv_ref,
    wo_ref,
    codes_ref,
    table_ref,
    low_bias_ref,
    high_bias_ref,
    x_ref,
    gain_ref,
    q_ref,
    k_ref,
    v_ref,
    mixed_ref,
    lse_ref,
    prob_ref,
    mid_ref,
    normed_two_ref,
    split_ref,
    turned_ref,
    attended_ref,
):
    step = pl.program_id(0)
    few = count_ref[0] <= FEW
    total_keys = picked_ref.shape[0]

    def project(rows):
        picked = picked_ref[rows, :]
        k_ref[rows, :] = dot_nn(picked, wk_ref[...]).astype(BF)
        values = dot_nn(picked, wv_ref[...]).astype(BF)
        v_ref[rows, :] = values
        turned_ref[:, rows] = values.T

    @pl.when(step == 0)
    def _():
        q_ref[...] = dot_nn(normed_ref[...], wq_ref[...]).astype(BF)

    @pl.when(jnp.logical_and(step == 0, few))
    def _():
        project(pl.ds(0, FEW))

    @pl.when(jnp.logical_and(step == 0, jnp.logical_not(few)))
    def _():
        @pl.loop(0, total_keys // 256)
        def _(block):
            project(pl.ds(pl.multiple_of(block * 256, 256), 256))

    here = pl.ds(pl.multiple_of(step * COLS, COLS), COLS)
    masks = head_masks()

    def attend(keys, short):
        def run(group):
            lanes = lanes_of(group)
            queries = stack_heads(q_ref[here, lanes], masks)
            scores = dot_nt(k_ref[0:keys, lanes], queries)
            pieces = []
            for h in range(GROUP):
                head = group * GROUP + h
                if short:
                    half = HEADS // 2
                    bias = low_bias_ref[head] if head < half else high_bias_ref[head - half]
                else:
                    bias = bias_of(split_ref, table_ref, head, keys)
                score = scores[:, h * COLS : (h + 1) * COLS] + bias
                top = jnp.max(score, 0, keepdims=True)
                grown = jnp.exp(score - top)
                total = jnp.sum(grown, 0, keepdims=True)
                prob = grown * (1.0 / total)
                if short:
                    prob_ref[head] = prob
                lse_ref[pl.ds(head, 1), :] = top + jnp.log(total)
                pieces.append(prob.astype(BF))
            mixed = dot_nn(turned_ref[lanes, 0:keys], jnp.concatenate(pieces, 1))
            mixed_ref[lanes, here] = own_blocks(mixed).astype(BF)

        if not short:
            unpack_codes(codes_ref, split_ref, keys)
        each_group(run, HEADS // GROUP, short)

    pl.when(few)(lambda: attend(FEW, True))
    pl.when(jnp.logical_not(few))(lambda: attend(total_keys, False))

    @pl.when(step == pl.num_programs(0) - 1)
    def _():
        gain = gain_ref[0:1, :]
        attended_ref[...] = mixed_ref[...].T

        @pl.loop(0, x_ref.shape[0] // 256)
        def _(block):
            rows = pl.ds(pl.multiple_of(block * 256, 256), 256)
            middle = x_ref[rows, :].astype(F32) + dot_nn(attended_ref[rows, :], wo_ref[...])
            mid_ref[rows, :] = middle
            normed_two_ref[rows, :] = norm_rows(middle, gain).astype(BF)


def attention_forward(count, normed, picked, weights, codes, table_lanes, bias, x_block, gain_two):
    tokens = normed.shape[0]
    keys = picked.shape[0]
    full = lambda shape: pl.BlockSpec(shape, lambda i, c: (0, 0))
    weight = lambda at: pl.BlockSpec((D, D), lambda i, c: (0, at), pipeline_mode=pl.Buffered(1))
    across = lambda height: pl.BlockSpec((height, COLS), lambda i, c: (0, i))
    headed = pl.BlockSpec((HEADS, FEW, COLS), lambda i, c: (0, 0, i))
    shape = jax.ShapeDtypeStruct
    return pl.pallas_call(
        attend_kernel,
        grid_spec=pltpu.PrefetchScalarGridSpec(
            num_scalar_prefetch=1,
            grid=(tokens // COLS,),
            in_specs=[
                full((tokens, D)),
                full((keys, D)),
                weight(0),
                weight(1),
                weight(2),
                weight(3),
                across(keys),
                full(table_lanes.shape),
                pl.BlockSpec((HEADS // 2, FEW, COLS), lambda i, c: (0, 0, i)),
                pl.BlockSpec((HEADS // 2, FEW, COLS), lambda i, c: (0, 0, i)),
                full((tokens, D)),
                full((8, D)),
            ],
            out_specs=[
                full((tokens, D)),
                full((keys, D)),
                full((keys, D)),
                full((D, tokens)),
                across(HEADS),
                headed,
                full((tokens, D)),
                full((tokens, D)),
            ],
            scratch_shapes=[
                pltpu.VMEM((TABLES, keys, COLS), jnp.int32),
                pltpu.VMEM((D, keys), BF),
                pltpu.VMEM((tokens, D), BF),
            ],
        ),
        out_shape=[
            shape((tokens, D), BF),
            shape((keys, D), BF),
            shape((keys, D), BF),
            shape((D, tokens), BF),
            shape((HEADS, tokens), F32),
            shape((HEADS, FEW, tokens), F32),
            shape((tokens, D), F32),
            shape((tokens, D), BF),
        ],
        compiler_params=pltpu.CompilerParams(vmem_limit_bytes=VMEM_LIMIT),
        cost_estimate=pl.CostEstimate(
            flops=20_000_000_000, bytes_accessed=50_000_000, transcendentals=3_000_000
        ),
        name="attention_forward",
    )(count, normed, picked, weights, weights, weights, weights, codes, table_lanes, *bias, x_block, gain_two)


def ffn_kernel(
    scalar_ref,
    normed_ref,
    out_cot_ref,
    mid_ref,
    gain_ref,
    gate_own_ref,
    gate_other_ref,
    up_own_ref,
    up_other_ref,
    down_own_ref,
    down_other_ref,
    gate_sent_ref,
    gate_kept_ref,
    up_sent_ref,
    up_kept_ref,
    down_sent_ref,
    down_kept_ref,
    layer_ref,
    middle_grad_ref,
    attn_grad_ref,
    gain_grad_ref,
    stat_ref,
    turned_ref,
    branch_ref,
    back_ref,
    down_all_ref,
    gate_ref,
    up_ref,
    gate_grad_ref,
    up_grad_ref,
    down_ref,
    *,
    gather_order,
    scatter_order,
):
    step = pl.program_id(0)
    device = scalar_ref[1]
    down_device = device if down_kept_ref.shape[1] % 8 == 0 else 0

    @pl.when(step == 0)
    def _():
        turned_ref[...] = normed_ref[...].T
        join_pieces(down_own_ref, down_other_ref, down_all_ref, down_device, *gather_order[2])

    join_pieces(gate_own_ref, gate_other_ref, gate_ref, device, *gather_order[0])
    join_pieces(up_own_ref, up_other_ref, up_ref, device, *gather_order[1])
    here = pl.ds(pl.multiple_of(step * FF_TILE, FF_TILE), FF_TILE)
    down_ref[...] = down_all_ref[here, :].astype(BF)

    normed = normed_ref[...]
    gate_weight = gate_ref[...].astype(BF)
    up_weight = up_ref[...].astype(BF)
    gate = dot_nn(normed, gate_weight)
    up = dot_nn(normed, up_weight)
    grad_act = dot_nt(out_cot_ref[...], down_ref[...])
    scale = 0.7978845608028654
    square = gate * gate
    bent = jnp.tanh(scale * (gate + 0.044715 * (square * gate)))
    half = 0.5 * (1.0 + bent)
    curved = gate * half
    slope = half + 0.5 * gate * (1.0 - bent * bent) * (scale * (1.0 + 0.134145 * square))
    activated = (curved * up).astype(BF)
    grad_gate = (grad_act * up * slope).astype(BF)
    grad_up = (grad_act * curved).astype(BF)
    branch = dot_nn(activated, down_ref[...])
    back = dot_nt(grad_gate, gate_weight) + dot_nt(grad_up, up_weight)

    @pl.when(step == 0)
    def _():
        branch_ref[...] = branch
        back_ref[...] = back

    @pl.when(step > 0)
    def _():
        branch_ref[...] += branch
        back_ref[...] += back

    gate_grad_ref[...] = dot_nn(turned_ref[...], grad_gate).astype(gate_grad_ref.dtype)
    part_pieces(gate_grad_ref, gate_sent_ref, gate_kept_ref, device, scatter_order[0])
    up_grad_ref[...] = dot_nn(turned_ref[...], grad_up).astype(up_grad_ref.dtype)
    part_pieces(up_grad_ref, up_sent_ref, up_kept_ref, device, scatter_order[1])
    down_all_ref[here, :] = dot_tn(activated, out_cot_ref[...])

    @pl.when(step == pl.num_programs(0) - 1)
    def _():
        part_pieces(
            down_all_ref, down_sent_ref, down_kept_ref, down_device, scatter_order[2]
        )
        gain = gain_ref[0:1, :]
        gain_grad_ref[...] = jnp.zeros_like(gain_grad_ref)
        lane = lax.broadcasted_iota(jnp.int32, (ROWS, 128), 1)

        @pl.loop(0, mid_ref.shape[0] // ROWS)
        def _(block):
            rows = pl.ds(pl.multiple_of(block * ROWS, ROWS), ROWS)
            middle = mid_ref[rows, :]
            final = middle + branch_ref[rows, :]
            layer_ref[rows, :] = final.astype(BF)
            mid_sum = jnp.sum(middle * middle, -1, keepdims=True)
            final_sum = jnp.sum(final * final, -1, keepdims=True)
            stat_ref[rows, :] = jnp.where(lane == 0, mid_sum, final_sum)
            inverse = lax.rsqrt(mid_sum * (1.0 / D) + EPS)
            unit = middle * inverse
            grad_normed = back_ref[rows, :]
            weighted = grad_normed * gain
            inner = jnp.mean(weighted * unit, -1, keepdims=True)
            grad_middle = out_cot_ref[rows, :].astype(F32) + inverse * (weighted - unit * inner)
            middle_grad_ref[rows, :] = grad_middle
            attn_grad_ref[rows, :] = grad_middle.astype(BF)
            gain_grad_ref[0:1, :] += jnp.sum(grad_normed * unit, 0, keepdims=True)


def feed_forward(scalars, normed_two, out_cot, middle, gain_two, gate, up, down):
    tokens = normed_two.shape[0]
    ff = gate[0].shape[2]
    half, rows = gate[0].shape[:2]
    down_rows = down[0].shape[1]
    once = pl.Buffered(1)
    full = lambda shape: pl.BlockSpec(shape, lambda i, c: (0,) * len(shape), pipeline_mode=once)
    tile = pl.BlockSpec((half, rows, FF_TILE), lambda i, c: (0, 0, i))
    shape = jax.ShapeDtypeStruct
    kernel = functools.partial(
        ffn_kernel,
        gather_order=[gather_masks(kind) for kind in range(3)],
        scatter_order=[scatter_masks(kind) for kind in range(3)],
    )
    return pl.pallas_call(
        kernel,
        grid_spec=pltpu.PrefetchScalarGridSpec(
            num_scalar_prefetch=1,
            grid=(ff // FF_TILE,),
            in_specs=[
                full((tokens, D)),
                full((tokens, D)),
                full((tokens, D)),
                full((8, D)),
                tile,
                tile,
                tile,
                tile,
                full((half, down_rows, D)),
                full((half, down_rows, D)),
            ],
            out_specs=[
                tile,
                tile,
                tile,
                tile,
                full((half, down_rows, D)),
                full((half, down_rows, D)),
                full((tokens, D)),
                full((tokens, D)),
                full((tokens, D)),
                full((8, D)),
                full((tokens, 128)),
            ],
            scratch_shapes=[
                pltpu.VMEM((D, tokens), BF),
                pltpu.VMEM((tokens, D), F32),
                pltpu.VMEM((tokens, D), F32),
                pltpu.VMEM((ff, D), F32),
                pltpu.VMEM((D, FF_TILE), held_type(rows)),
                pltpu.VMEM((D, FF_TILE), held_type(rows)),
                pltpu.VMEM((D, FF_TILE), held_type(rows)),
                pltpu.VMEM((D, FF_TILE), held_type(rows)),
                pltpu.VMEM((FF_TILE, D), BF),
            ],
        ),
        out_shape=[shape((half, rows, ff), BF)] * 4
        + [shape((half, down_rows, D), BF)] * 2
        + [
            shape((tokens, D), BF),
            shape((tokens, D), F32),
            shape((tokens, D), BF),
            shape((8, D), F32),
            shape((tokens, 128), F32),
        ],
        compiler_params=pltpu.CompilerParams(vmem_limit_bytes=VMEM_LIMIT),
        cost_estimate=pl.CostEstimate(
            flops=27_000_000_000, bytes_accessed=44_000_000, transcendentals=1_500_000
        ),
        name="feed_forward",
    )(scalars, normed_two, out_cot, middle, gain_two, *gate, *up, *down)


def add_histogram(split_ref, grad_ref, hist_ref, chosen_ref, keys):
    heads = grad_ref.shape[0]
    cols = split_ref.shape[2]
    bucket = lax.broadcasted_iota(jnp.int32, (BUCKETS, cols), 0)

    @pl.loop(0, keys // HIST_ROWS)
    def _(block):
        base = pl.multiple_of(block * HIST_ROWS, HIST_ROWS)
        grads = grad_ref[:, pl.ds(base, HIST_ROWS), :]
        grads = grads.reshape(heads * HIST_ROWS, cols)
        for row in range(HIST_ROWS):
            for t in range(TABLES):
                at = (row * TABLES + t) * BUCKETS
                match = split_ref[t, pl.ds(base + row, 1), :] == bucket
                chosen_ref[at : at + BUCKETS, :] = match.astype(F32).astype(BF)
        hist_ref[...] += dot_nt(chosen_ref[...], grads)


def take_histogram(hist_ref, out_ref):
    height, width = out_ref.shape
    own = lax.broadcasted_iota(jnp.int32, (height, width), 1) & (HIST_ROWS - 1)
    total = jnp.zeros((height, width), F32)
    for row in range(HIST_ROWS):
        piece = hist_ref[row * height : (row + 1) * height, :]
        total = total + jnp.where(own == row, piece, 0.0)
    out_ref[...] = total


def backward_kernel(
    count_ref,
    attn_grad_ref,
    wo_ref,
    q_ref,
    k_ref,
    v_ref,
    lse_ref,
    prob_ref,
    codes_ref,
    table_ref,
    normed_turned_ref,
    picked_turned_ref,
    mixed_ref,
    dq_ref,
    dk_ref,
    dv_ref,
    grad_ref,
    hist_out_ref,
    sent_ref,
    kept_ref,
    back_ref,
    split_ref,
    long_grad_ref,
    turned_ref,
    dq_turned_ref,
    dk_sum_ref,
    dv_sum_ref,
    hist_ref,
    chosen_ref,
    joined_ref,
    *,
    first_head,
    scatter_order,
):
    step = pl.program_id(0)
    few = count_ref[0] <= FEW
    total_keys = k_ref.shape[0]
    heads = q_ref.shape[1] // HEAD_DIM

    @pl.when(step == 0)
    def _():
        back_ref[...] = dot_nt(attn_grad_ref[...], wo_ref[...]).astype(BF)
        dk_sum_ref[...] = jnp.zeros_like(dk_sum_ref)
        dv_sum_ref[...] = jnp.zeros_like(dv_sum_ref)
        hist_ref[...] = jnp.zeros_like(hist_ref)

    @pl.when(jnp.logical_and(step == 0, few))
    def _():
        turned_ref[:, 0:FEW] = k_ref[0:FEW, :].T

    @pl.when(jnp.logical_and(step == 0, jnp.logical_not(few)))
    def _():
        turned_ref[...] = k_ref[...].T

    here = pl.ds(pl.multiple_of(step * COLS, COLS), COLS)
    masks = head_masks()

    def turn_back(keys, short):
        def run(group):
            lanes = lanes_of(group)
            queries = stack_heads(q_ref[here, lanes], masks)
            grads = stack_heads(back_ref[here, lanes], masks)
            prob_grads = dot_nt(v_ref[0:keys, lanes], grads)
            if not short:
                scores = dot_nt(k_ref[0:keys, lanes], queries)
            score_grads = []
            probs = []
            for h in range(GROUP):
                cols = slice(h * COLS, (h + 1) * COLS)
                local = group * GROUP + h
                if short:
                    prob = prob_ref[local]
                else:
                    head = first_head + local
                    bias = bias_of(split_ref, table_ref, head, keys)
                    prob = jnp.exp(scores[:, cols] + bias - lse_ref[pl.ds(head, 1), :])
                weighted = prob * prob_grads[:, cols]
                inner = jnp.sum(weighted, 0, keepdims=True)
                score_grad = (weighted - prob * inner).astype(BF)
                if short:
                    grad_ref[local] = score_grad
                else:
                    long_grad_ref[local] = score_grad
                score_grads.append(score_grad)
                probs.append(prob.astype(BF))
            score_grads = jnp.concatenate(score_grads, 1)
            probs = jnp.concatenate(probs, 1)
            dq_turned_ref[lanes, here] = own_blocks(
                dot_nn(turned_ref[lanes, 0:keys], score_grads)
            ).astype(BF)
            dk_sum_ref[0:keys, lanes] += dot_nn(score_grads, queries)
            dv_sum_ref[0:keys, lanes] += dot_nn(probs, grads)

        if not short:
            unpack_codes(codes_ref, split_ref, keys)
        each_group(run, heads // GROUP, short)
        if not short:
            add_histogram(split_ref, long_grad_ref, hist_ref, chosen_ref, keys)

    pl.when(few)(lambda: turn_back(FEW, True))
    pl.when(jnp.logical_not(few))(lambda: turn_back(total_keys, False))

    def leave(number, gradient):
        joined_ref[...] = gradient.astype(joined_ref.dtype)
        at = number * joined_ref.shape[1]
        part_pieces(joined_ref, sent_ref, kept_ref, count_ref[1], scatter_order, at)

    def finish(keys):
        leave(1, dot_nn(picked_turned_ref[:, 0:keys], dk_ref[0:keys, :]))
        leave(2, dot_nn(picked_turned_ref[:, 0:keys], dv_ref[0:keys, :]))

    @pl.when(step == pl.num_programs(0) - 1)
    def _():
        dk_ref[...] = dk_sum_ref[...].astype(BF)
        dv_ref[...] = dv_sum_ref[...].astype(BF)
        dq_ref[...] = dq_turned_ref[...].T
        leave(0, dot_nn(normed_turned_ref[...], dq_ref[...]))
        first = first_head * HEAD_DIM
        leave(3, dot_nn(mixed_ref[...], attn_grad_ref[:, first : first + heads * HEAD_DIM]))
        take_histogram(hist_ref, hist_out_ref)
        pl.when(few)(lambda: finish(FEW))
        pl.when(jnp.logical_not(few))(lambda: finish(total_keys))


def attention_backward(
    half,
    kind,
    count,
    attn_grad,
    weights,
    queries,
    keys,
    values,
    lse,
    probs,
    codes,
    table_lanes,
    normed_turned,
    picked_turned,
    mixed,
):
    tokens = queries.shape[0]
    device_count = lax.axis_size("row") * lax.axis_size("col")
    rows = D // device_count
    key_total = keys.shape[0]
    heads = HEADS // 2
    width = heads * HEAD_DIM
    full = lambda shape: pl.BlockSpec(shape, lambda i, c: (0, 0))
    side = lambda height: pl.BlockSpec((height, width), lambda i, c: (0, half))
    across = lambda height: pl.BlockSpec((height, COLS), lambda i, c: (0, i))
    shape = jax.ShapeDtypeStruct
    hist_shape = (TABLES * BUCKETS, heads * HIST_ROWS)
    return pl.pallas_call(
        functools.partial(
            backward_kernel,
            first_head=half * heads,
            scatter_order=scatter_masks(kind),
        ),
        grid_spec=pltpu.PrefetchScalarGridSpec(
            num_scalar_prefetch=1,
            grid=(tokens // COLS,),
            in_specs=[
                full((tokens, D)),
                pl.BlockSpec((width, D), lambda i, c: (half, 3)),
                side(tokens),
                side(key_total),
                side(key_total),
                across(HEADS),
                pl.BlockSpec((heads, FEW, COLS), lambda i, c: (half, 0, i)),
                across(key_total),
                full(table_lanes.shape),
                full((D, tokens)),
                full((D, key_total)),
                full((D, tokens)),
            ],
            out_specs=[
                full((tokens, width)),
                full((key_total, width)),
                full((key_total, width)),
                pl.BlockSpec((heads, FEW, COLS), lambda i, c: (0, 0, i)),
                full(hist_shape),
            ]
            + [
                pl.BlockSpec((device_count // 2, rows, 4 * width), lambda i, c: (0, 0, 0)),
            ]
            * 2,
            scratch_shapes=[
                pltpu.VMEM((tokens, width), BF),
                pltpu.VMEM((TABLES, key_total, COLS), jnp.int32),
                pltpu.VMEM((heads, key_total, COLS), BF),
                pltpu.VMEM((width, key_total), BF),
                pltpu.VMEM((width, tokens), BF),
                pltpu.VMEM((key_total, width), F32),
                pltpu.VMEM((key_total, width), F32),
                pltpu.VMEM((HIST_ROWS * hist_shape[0], hist_shape[1]), F32),
                pltpu.VMEM((HIST_ROWS * hist_shape[0], COLS), BF),
                pltpu.VMEM((D, width), held_type(rows)),
            ],
        ),
        out_shape=[
            shape((tokens, width), BF),
            shape((key_total, width), BF),
            shape((key_total, width), BF),
            shape((heads, FEW, tokens), BF),
            shape(hist_shape, F32),
        ]
        + [shape((device_count // 2, rows, 4 * width), BF)] * 2,
        compiler_params=pltpu.CompilerParams(vmem_limit_bytes=VMEM_LIMIT),
        cost_estimate=pl.CostEstimate(
            flops=15_000_000_000, bytes_accessed=30_000_000, transcendentals=0
        ),
        name="attention_backward",
    )(
        count,
        attn_grad,
        weights,
        queries,
        keys,
        values,
        lse,
        probs,
        codes,
        table_lanes,
        normed_turned,
        picked_turned,
        mixed,
    )


def histogram_kernel(
    count_ref, codes_ref, low_ref, high_ref, out_ref, split_ref, both_ref, hist_ref, chosen_ref
):
    out_ref[...] = jnp.zeros_like(out_ref)

    @pl.when(count_ref[0] <= FEW)
    def _():
        unpack_codes(codes_ref, split_ref, FEW)
        both_ref[: HEADS // 2] = low_ref[...]
        both_ref[HEADS // 2 :] = high_ref[...]
        hist_ref[...] = jnp.zeros_like(hist_ref)
        add_histogram(split_ref, both_ref, hist_ref, chosen_ref, FEW)
        take_histogram(hist_ref, out_ref)


def table_histogram(count, codes, low, high):
    tokens = codes.shape[1]
    hist_shape = (TABLES * BUCKETS, HEADS * HIST_ROWS)
    whole = lambda shape: pl.BlockSpec(shape, lambda i, c: (0,) * len(shape))
    return pl.pallas_call(
        histogram_kernel,
        grid_spec=pltpu.PrefetchScalarGridSpec(
            num_scalar_prefetch=1,
            grid=(1,),
            in_specs=[whole((FEW, tokens)), whole(low.shape), whole(high.shape)],
            out_specs=whole(hist_shape),
            scratch_shapes=[
                pltpu.VMEM((TABLES, FEW, tokens), jnp.int32),
                pltpu.VMEM((HEADS, FEW, tokens), BF),
                pltpu.VMEM((HIST_ROWS * hist_shape[0], hist_shape[1]), F32),
                pltpu.VMEM((HIST_ROWS * hist_shape[0], tokens), BF),
            ],
        ),
        out_shape=jax.ShapeDtypeStruct(hist_shape, F32),
        compiler_params=pltpu.CompilerParams(vmem_limit_bytes=VMEM_LIMIT),
        cost_estimate=pl.CostEstimate(
            flops=20_000_000_000, bytes_accessed=8_000_000, transcendentals=0
        ),
        name="table_histogram",
    )(count, codes, low, high)


def key_gradients_kernel(
    count_ref,
    dq_low_ref,
    dq_high_ref,
    dk_low_ref,
    dk_high_ref,
    dv_low_ref,
    dv_high_ref,
    wq_ref,
    wk_ref,
    wv_ref,
    pack_ref,
    x_ref,
    picked_ref,
    lent_ref,
    own_ref,
    gain_ref,
    both_ref,
):
    tokens = x_ref.shape[0]
    half = D // 2
    few = count_ref[0] <= FEW

    def unit(rows):
        rows = rows.astype(F32)
        return rows * lax.rsqrt(jnp.mean(rows * rows, -1, keepdims=True) + EPS)

    def product(low, high, weight_ref):
        return dot_nt(low, weight_ref[:, :half]) + dot_nt(high, weight_ref[:, half:])

    gain_ref[...] = jnp.zeros_like(gain_ref)
    own_ref[...] = product(dq_low_ref[...], dq_high_ref[...], wq_ref)

    @pl.loop(0, tokens // COLS)
    def _(block):
        rows = pl.ds(pl.multiple_of(block * COLS, COLS), COLS)
        gain_ref[0:1, :] += jnp.sum(own_ref[rows, :] * unit(x_ref[rows, :]), 0, keepdims=True)

    def spread(keys, step):
        @pl.loop(0, keys // step)
        def _(block):
            rows = pl.ds(pl.multiple_of(block * step, step), step)
            grads = product(dk_low_ref[rows, :], dk_high_ref[rows, :], wk_ref)
            grads = grads + product(dv_low_ref[rows, :], dv_high_ref[rows, :], wv_ref)
            gain_ref[0:1, :] += jnp.sum(grads * unit(picked_ref[rows, :]), 0, keepdims=True)
            high = grads.astype(BF)
            both_ref[0, rows, :] = high
            both_ref[1, rows, :] = (grads - high.astype(F32)).astype(BF)

        high = both_ref[0, 0:keys, :]
        chosen = pack_ref[0:tokens, 0:keys]
        own_ref[...] += dot_nn(chosen, high) + dot_nn(chosen, both_ref[1, 0:keys, :])
        lent_ref[...] = dot_nn(pack_ref[tokens:, 0:keys], high).astype(BF)

    pl.when(few)(lambda: spread(FEW, FEW))
    pl.when(jnp.logical_not(few))(lambda: spread(pack_ref.shape[1], COLS))


def key_gradients(count, low, high, weights, pack, x_block, picked_x):
    tokens = x_block.shape[0]
    keys = pack.shape[0]
    whole = lambda shape: pl.BlockSpec(shape, lambda i, c: (0, 0))
    weight = lambda at: pl.BlockSpec((D, D), lambda i, c: (0, at))
    shape = jax.ShapeDtypeStruct
    return pl.pallas_call(
        key_gradients_kernel,
        grid_spec=pltpu.PrefetchScalarGridSpec(
            num_scalar_prefetch=1,
            grid=(1,),
            in_specs=[
                whole((tokens, D // 2)),
                whole((tokens, D // 2)),
                whole((keys, D // 2)),
                whole((keys, D // 2)),
                whole((keys, D // 2)),
                whole((keys, D // 2)),
                weight(0),
                weight(1),
                weight(2),
                whole(pack.shape),
                whole((tokens, D)),
                whole((keys, D)),
            ],
            out_specs=[whole((keys - tokens, D)), whole((tokens, D)), whole((8, D))],
            scratch_shapes=[pltpu.VMEM((2, keys, D), BF)],
        ),
        out_shape=[
            shape((keys - tokens, D), BF),
            shape((tokens, D), F32),
            shape((8, D), F32),
        ],
        compiler_params=pltpu.CompilerParams(vmem_limit_bytes=VMEM_LIMIT),
        cost_estimate=pl.CostEstimate(
            flops=9_000_000_000, bytes_accessed=18_000_000, transcendentals=0
        ),
        name="key_gradients",
    )(count, low[0], high[0], low[1], high[1], low[2], high[2], weights, weights, weights, pack, x_block, picked_x)


def input_kernel(own_ref, owner_ref, returned_ref, x_ref, gain_ref, middle_ref, out_ref):
    grads = own_ref[...] + dot_nn(owner_ref[...], returned_ref[...])
    rows = x_ref[...].astype(F32)
    inverse = lax.rsqrt(jnp.mean(rows * rows, -1, keepdims=True) + EPS)
    unit = rows * inverse
    weighted = grads * gain_ref[0:1, :]
    inner = jnp.mean(weighted * unit, -1, keepdims=True)
    out_ref[...] = (middle_ref[...] + inverse * (weighted - unit * inner)).astype(BF)


def input_gradient(own, owner, returned, x_block, gain_one, grad_middle):
    tokens = own.shape[0]
    streamed = lambda width: pl.BlockSpec((COLS, width), lambda i: (i, 0))
    whole = lambda shape: pl.BlockSpec(shape, lambda i: (0, 0))
    return pl.pallas_call(
        input_kernel,
        grid=(tokens // COLS,),
        in_specs=[
            streamed(D),
            streamed(owner.shape[1]),
            whole(returned.shape),
            streamed(D),
            whole((8, D)),
            streamed(D),
        ],
        out_specs=streamed(D),
        out_shape=jax.ShapeDtypeStruct((tokens, D), BF),
        compiler_params=pltpu.CompilerParams(vmem_limit_bytes=VMEM_LIMIT),
        cost_estimate=pl.CostEstimate(
            flops=1_000_000_000, bytes_accessed=8_000_000, transcendentals=0
        ),
        name="input_gradient",
    )(own, owner, returned, x_block, gain_one, grad_middle)


def on_device(
    hidden_in,
    out_cotangent,
    query_weight,
    key_weight,
    value_weight,
    output_weight,
    attn_gain,
    relative_table,
    horiz_table,
    vert_table,
    ffn_gain,
    gate_weight,
    up_weight,
    down_weight,
    key_keep,
    halo_rows,
    relative_bucket,
    horiz_bucket,
    vert_bucket,
):
    tokens = hidden_in.shape[0]
    rows = gate_weight.shape[0]
    table_share = relative_table.shape[0]
    row_index = lax.axis_index("row")
    col_index = lax.axis_index("col")
    row_count = lax.axis_size("row")
    col_count = lax.axis_size("col")
    region = row_index * col_count + col_index
    device_count = row_count * col_count

    packed_weights = jnp.concatenate([query_weight, key_weight, value_weight, output_weight], 1)
    weights = lax.all_gather(packed_weights, ("row", "col"), axis=0, tiled=True)
    small = jnp.stack(
        [attn_gain, ffn_gain]
        + [jnp.pad(t, (0, rows - table_share)) for t in (relative_table, horiz_table, vert_table)],
        1,
    )
    small = jnp.pad(small, ((0, 0), (0, 128 - small.shape[1])))
    small, gate_weight, up_weight, down_weight = after(
        (small, gate_weight, up_weight, down_weight), packed_weights
    )
    small_gather = Gather(small, 0, True)
    ffn_gathers = [
        Gather(weight, kind) for kind, weight in enumerate((gate_weight, up_weight, down_weight))
    ]

    def turn(gathers, *done):
        for gather in gathers:
            gather.land(*done)
        return [gather.send() for gather in gathers]

    sent = turn([small_gather] + ffn_gathers)

    halo_rows, key_keep, x_early = after((halo_rows, key_keep, hidden_in), sent)
    own_lists = lax.dynamic_index_in_dim(halo_rows, region, 0, keepdims=False)
    rim = x_early[own_lists]
    sent = turn([small_gather], rim)
    rim = after(rim, sent)
    above, below = shifted(rim[0:2], "row")
    left, right = shifted(rim[2:4], "col")
    neighbours = jnp.stack([region - col_count, region + col_count, region - 1, region + 1])
    present = jnp.stack(
        [row_index > 0, row_index < row_count - 1, col_index > 0, col_index < col_count - 1]
    ).astype(jnp.int32)
    list_ids = jnp.array([1, 0, 3, 2], dtype=jnp.int32)
    clipped = jnp.clip(neighbours, 0, device_count - 1)
    their_lists = after(halo_rows, rim)[clipped, list_ids]
    halo_keep = key_keep[clipped[:, None] * tokens + their_lists] * present[:, None]
    own_keep = lax.dynamic_slice_in_dim(key_keep, region * tokens, tokens)
    key_mask = jnp.concatenate([own_keep, halo_keep.reshape(-1)])
    key_total = key_mask.shape[0]

    place = jnp.cumsum(key_mask) - 1
    count = place[-1:] + 1
    scalars = jnp.concatenate([count, region.reshape(1)])
    slots = jnp.arange(key_total, dtype=jnp.int32)
    pack = ((place[:, None] == slots) & (key_mask[:, None] > 0)).astype(BF)

    sent = turn([small_gather] + ffn_gathers, pack)
    packed_by, relative_bucket = after((pack, relative_bucket), sent)
    found = [
        lax.dot_general(
            packed_by, bucket.astype(BF), (((0,), (1,)), ((), ())), preferred_element_type=F32
        ).astype(jnp.int32)
        for bucket in (relative_bucket, horiz_bucket, vert_bucket)
    ]
    found_vert = jnp.where(slots[:, None] < count, found[2], BUCKETS)
    codes = found[0] + found[1] * BUCKETS + found_vert * (BUCKETS * BUCKETS)

    sent = turn([small_gather], codes)
    packed_by, above = after((pack, above), sent, codes)
    x_keys = jnp.concatenate([hidden_in, above, below, left, right], 0)
    picked_x = dot_nn(packed_by.T, x_keys).astype(BF)
    turn([small_gather], picked_x)
    while small_gather.flight is not None:
        turn([small_gather])
    sent = turn(ffn_gathers, small_gather.held)
    small_masks = [0]
    for stage in stages_of(0)[::-1]:
        small_masks = small_masks + [mask ^ mask_of(stage) for mask in small_masks]
    place_of = [0] * device_count
    for at, mask in enumerate(small_masks):
        place_of[mask] = at
    devices = jnp.arange(device_count, dtype=jnp.int32)
    small_all = small_gather.held[jnp.array(place_of, jnp.int32)[devices ^ region]]
    gain_attn, gain_ffn = [small_all[:, :, i].reshape(-1) for i in range(2)]
    table_rows = [
        small_all[:, :table_share, 2 + t].reshape(BUCKETS, HEADS).T for t in range(TABLES)
    ]
    table_lanes = jnp.pad(
        jnp.stack(table_rows).astype(F32), ((0, 0), (0, 0), (0, 128 - BUCKETS))
    )
    table_lanes = table_lanes.at[2, :, BUCKETS].set(masked_score).reshape(TABLES * HEADS, 128)
    gain_one = gain_attn.astype(F32)
    gain_two = jnp.broadcast_to(gain_ffn.astype(F32), (8, D))

    low_bias = layout_bias(after(codes, sent), table_lanes, 0)
    sent = turn(ffn_gathers, low_bias)
    high_bias = layout_bias(after(codes, sent, low_bias), table_lanes, HEADS // 2)
    x_input = hidden_in.astype(F32)
    normed_one = norm_rows(x_input, gain_one).astype(BF)
    picked = norm_rows(picked_x.astype(F32), gain_one).astype(BF)
    normed_turned = normed_one.T
    picked_turned = picked.T
    turn(ffn_gathers, high_bias, picked_turned, normed_turned)
    while any(gather.flight is not None for gather in ffn_gathers):
        turn(ffn_gathers)
    gathered = [gather.held for gather in ffn_gathers]
    ffn_weights = [(held, exchange(held, ("row", 0))) for held in gathered]
    normed_one = after(normed_one, gathered, normed_turned, picked_turned)
    queries, keys, values, mixed, lse, probs, x_middle, normed_two = attention_forward(
        scalars,
        normed_one,
        picked,
        weights,
        codes,
        table_lanes,
        (low_bias, high_bias),
        hidden_in,
        gain_two,
    )
    ffn_weights = [(own, after(other, normed_two)) for own, other in ffn_weights]
    uneven = down_weight.shape[0] % 8 != 0
    if uneven:
        order, core_mask = gather_masks(2)
        order = order + tuple(mask ^ core_mask for mask in order)
        ffn_weights[2] = reordered(*ffn_weights[2], order, region)
    (
        gate_sent,
        gate_kept,
        up_sent,
        up_kept,
        down_sent,
        down_kept,
        layer_out,
        grad_middle,
        grad_attn,
        ffn_gain_part,
        row_stats,
    ) = feed_forward(scalars, normed_two, out_cotangent, x_middle, gain_two, *ffn_weights)
    if uneven:
        down_kept, down_sent = reordered(down_kept, down_sent, scatter_masks(2), region)
    ffn_chains = [
        Scatter(gate_sent, gate_kept, 0),
        Scatter(up_sent, up_kept, 1),
        Scatter(down_sent, down_kept, 2),
    ]
    rounds = Rounds()
    rounds.chains += ffn_chains

    def backward(half, kind, grad_attn):
        return attention_backward(
            half,
            kind,
            scalars,
            grad_attn,
            weights,
            queries,
            keys,
            values,
            lse,
            probs,
            codes,
            table_lanes,
            normed_turned,
            picked_turned,
            mixed,
        )

    sent = rounds.send()
    low_half = backward(0, 2, after(grad_attn, sent))
    low_chain = Scatter(low_half[5], low_half[6], 2)
    rounds.land(low_half[0])
    rounds.chains.append(low_chain)
    sent = rounds.send()
    high_half = backward(1, 1, after(grad_attn, low_half[0], sent))
    high_chain = Scatter(high_half[5], high_half[6], 1)
    rounds.land(high_half[0])
    rounds.chains.append(high_chain)
    sent = rounds.send()
    short_hist = table_histogram(
        scalars, after(codes, high_half[0], sent), low_half[3], high_half[3]
    )
    sent = rounds.turn(short_hist)
    lent, own_grads, attn_gain_part = key_gradients(
        scalars,
        low_half[:3],
        high_half[:3],
        weights,
        after(pack, short_hist, sent),
        hidden_in,
        picked_x,
    )
    hist = short_hist + jnp.concatenate([low_half[4], high_half[4]], 1)
    grad_table = jnp.sum(hist.reshape(TABLES * BUCKETS, HEADS, HIST_ROWS), -1)
    keep_float = own_keep.astype(F32)
    stat_part = jnp.stack(
        [
            jnp.sum(keep_float * jnp.sum(x_input * x_input, -1)),
            jnp.sum(keep_float * row_stats[:, 0]),
            jnp.sum(keep_float * row_stats[:, 1]),
            jnp.sum(keep_float),
        ]
    )
    small_chain = Summing(
        jnp.concatenate(
            [
                jnp.pad(stat_part, (0, 124)),
                ffn_gain_part[0],
                attn_gain_part[0],
                grad_table.reshape(-1),
            ]
        ).reshape(-1, 128)
    )
    rounds.land(lent)
    lent = lent.reshape(4, -1, D)
    back_above, back_below = shifted(lent[0:2], "row")
    back_left, back_right = shifted(lent[2:4], "col")
    rounds.chains.append(small_chain)
    sent = rounds.send()
    returned = jnp.concatenate([back_above, back_below, back_left, back_right], 0)
    owner_lists = own_lists.reshape(-1)
    owner = (jnp.arange(tokens, dtype=jnp.int32)[:, None] == owner_lists).astype(BF)
    input_grad = input_gradient(
        own_grads,
        owner,
        after(returned, sent),
        hidden_in,
        jnp.broadcast_to(gain_one, (8, D)),
        grad_middle,
    )
    rounds.turn(input_grad)
    while rounds.chains:
        rounds.turn()

    summed = small_chain.value.reshape(-1)
    residual_rms = jnp.sqrt(summed[:3] / (summed[3] * D))
    own_part = lambda at, size: lax.dynamic_slice_in_dim(summed, at + region * size, size)
    ffn_gain_grad = own_part(128, rows)
    attn_gain_grad = own_part(128 + D, rows)
    table_at = 128 + 2 * D
    table_grads = [own_part(table_at + t * BUCKETS * HEADS, table_share) for t in range(TABLES)]
    gate_grad, up_grad, down_grad = [chain.total() for chain in ffn_chains]
    sides = [low_chain.total(), high_chain.total()]
    width = D // 2
    query_grad, key_grad, value_grad, output_grad = [
        jnp.concatenate([side[:, i * width : (i + 1) * width] for side in sides], 1)
        for i in range(4)
    ]
    return (
        layer_out,
        input_grad,
        query_grad,
        key_grad,
        value_grad,
        output_grad,
        attn_gain_grad,
        table_grads[0],
        table_grads[1],
        table_grads[2],
        ffn_gain_grad,
        gate_grad,
        up_grad,
        down_grad,
        residual_rms,
    )


def solution(mesh):
    split = P(("row", "col"), None)
    line = P(("row", "col"))
    return jax.shard_map(
        on_device,
        mesh=mesh,
        in_specs=(split,) * 6 + (line,) * 5 + (split,) * 3 + (P(), P()) + (split,) * 3,
        out_specs=(split,) * 6 + (line,) * 5 + (split,) * 3 + (P(),),
        check_vma=False,
    )
```

```python
import functools

import jax
import jax.numpy as jnp
from jax import lax
from jax.experimental import pallas as pl
from jax.experimental.pallas import tpu as pltpu
from jax.sharding import PartitionSpec as P

D = 1024
HEADS = 16
HEAD_DIM = 64
BUCKETS = 32
TABLES = 3

EPS = 1e-06
masked_score = -1e30
FEW = 384
COLS = 128
ROWS = 64
GROUP = 4
WIDE = GROUP * HEAD_DIM
HIST_ROWS = 16
FF_TILE = 256
VMEM_LIMIT = 56 * 1024 * 1024
BF = jnp.bfloat16
F32 = jnp.float32


def shifted(block, axis):
    count = lax.axis_size(axis)
    forward = [(i, i + 1) for i in range(count - 1)]
    backward = [(target, source) for source, target in forward]
    return (
        lax.ppermute(block[1], axis, forward),
        lax.ppermute(block[0], axis, backward),
    )


def norm_rows(values, gain_row):
    return values * lax.rsqrt(jnp.mean(values * values, -1, keepdims=True) + EPS) * gain_row


def stages_of(kind):
    row_bits = [("row", bit) for bit in range(lax.axis_size("row").bit_length() - 1)]
    col_bits = [("col", bit) for bit in range(lax.axis_size("col").bit_length() - 1)]
    if kind == 0:
        return row_bits[:1] + col_bits + row_bits[1:]
    if kind == 1:
        return row_bits[:1] + col_bits[::-1] + row_bits[1:]
    if kind == 2:
        return row_bits[:2] + col_bits + row_bits[2:]
    return row_bits[:2] + col_bits[::-1] + row_bits[2:]


def mask_of(stage):
    axis, bit = stage
    return (lax.axis_size("col") if axis == "row" else 1) << bit


def scatter_masks(kind):
    masks = [0]
    for stage in stages_of(kind)[::-1]:
        masks = masks + [mask ^ mask_of(stage) for mask in masks]
    return tuple(masks)


def gather_masks(kind):
    masks = [0]
    for stage in stages_of(kind)[:0:-1]:
        masks = masks + [mask ^ mask_of(stage) for mask in masks]
    return tuple(masks), mask_of(("row", 0))


def exchange(values, stage):
    axis, bit = stage
    pairs = [(i, i ^ (1 << bit)) for i in range(lax.axis_size(axis))]
    return lax.ppermute(values, axis, pairs)


def after(values, *earlier):
    return lax.optimization_barrier((values, earlier))[0]


class Gather:
    def __init__(self, shard, kind, both=False):
        self.held = shard[None]
        self.stages = stages_of(kind)[::-1] if both else stages_of(kind)[:0:-1]
        self.flight = None

    def send(self):
        if self.stages:
            self.flight = exchange(self.held, self.stages.pop(0))
        return self.held

    def land(self, *done):
        if self.flight is not None:
            if done:
                self.flight = after(self.flight, *done)
            self.held = jnp.concatenate([self.held, self.flight], 0)
            self.flight = None


class Scatter:
    def __init__(self, sent, kept, kind):
        self.stages = stages_of(kind)
        self.parts = [kept]
        self.sent = sent

    def land(self, flight):
        self.parts.append(flight)
        half = flight.shape[0] // 2
        self.sent = None
        if self.stages:
            self.sent = sum(part[half : 2 * half].astype(F32) for part in self.parts).astype(BF)

    def total(self):
        return sum(part[0].astype(F32) for part in self.parts)


class Rounds:
    def __init__(self):
        self.chains = []
        self.flights = []

    def land(self, *done):
        for chains, flight in self.flights:
            if done:
                flight = after(flight, *done)
            at = 0
            for chain in chains:
                width = chain.sent.shape[-1]
                chain.land(flight[..., at : at + width])
                at += width
        self.flights = []
        self.chains = [chain for chain in self.chains if chain.sent is not None]

    def send(self):
        groups = {}
        for chain in self.chains:
            alone = id(chain) if chain.sent.shape[0] > 4 else 0
            alike = (chain.stages.pop(0), chain.sent.shape[:-1], alone)
            groups.setdefault(alike, []).append(chain)
        sent = []
        for (stage, *_), chains in groups.items():
            values = [chain.sent for chain in chains]
            values = jnp.concatenate(values, -1) if len(values) > 1 else values[0]
            self.flights.append((chains, exchange(values, stage)))
            sent.append(values)
        return sent

    def turn(self, *done):
        self.land(*done)
        return self.send()


def dot_nn(left, right):
    return lax.dot_general(left, right, (((1,), (0,)), ((), ())), preferred_element_type=F32)


def dot_nt(left, right):
    return lax.dot_general(left, right, (((1,), (1,)), ((), ())), preferred_element_type=F32)


def dot_tn(left, right):
    return lax.dot_general(left, right, (((0,), (0,)), ((), ())), preferred_element_type=F32)


LANE_GATHER = lax.GatherDimensionNumbers(
    offset_dims=(),
    collapsed_slice_dims=(1,),
    start_index_map=(1,),
    operand_batching_dims=(0,),
    start_indices_batching_dims=(0,),
)


def lane_gather(rows, index):
    return lax.gather(
        rows,
        index[:, :, None],
        LANE_GATHER,
        (1, 1),
        mode=lax.GatherScatterMode.PROMISE_IN_BOUNDS,
    )


def lanes_of(group):
    if isinstance(group, int):
        return pl.ds(group * WIDE, WIDE)
    return pl.ds(pl.multiple_of(group * WIDE, WIDE), WIDE)


def held_type(height):
    return BF if height % 16 == 0 else F32


def reordered(low, high, masks, device):
    place = [0] * len(masks)
    for at, mask in enumerate(masks):
        place[mask] = at
    index = jnp.array(place, jnp.int32)[jnp.array(masks, jnp.int32) ^ device]
    both = jnp.concatenate([low, high], 0)[index]
    return both[: len(masks) // 2], both[len(masks) // 2 :]


def placed(owner, height):
    start = owner * height
    if isinstance(start, int):
        return pl.ds(start, height)
    if height % 8 == 0:
        start = pl.multiple_of(start, height & -height)
    return pl.ds(start, height)


def join_pieces(own_ref, other_ref, joined_ref, device, masks, core_mask, at=0):
    height = own_ref.shape[1]
    lanes = slice(at, at + own_ref.shape[2])
    for p, mask in enumerate(masks):
        joined_ref[placed(device ^ mask, height), lanes] = own_ref[p].astype(joined_ref.dtype)
        joined_ref[placed(device ^ mask ^ core_mask, height), lanes] = other_ref[p].astype(
            joined_ref.dtype
        )


def part_pieces(joined_ref, sent_ref, kept_ref, device, masks, at=0, source=0):
    half, height, width = kept_ref.shape
    width = min(width, joined_ref.shape[1])
    lanes = slice(at, at + width)
    taken = slice(source, source + width)
    for p, mask in enumerate(masks):
        target_ref = kept_ref if p < half else sent_ref
        target_ref[p % half, :, lanes] = joined_ref[placed(device ^ mask, height), taken].astype(BF)


def head_masks():
    lane = lax.broadcasted_iota(jnp.int32, (1, WIDE), 1) >> 6
    return [(lane == h).astype(F32).astype(BF) for h in range(GROUP)]


def stack_heads(block, masks):
    return jnp.concatenate([block * mask for mask in masks], 0)


def unpack_codes(codes_ref, split_ref, keys):
    code = codes_ref[:keys, :]
    split_ref[0, :keys, :] = code & 31
    split_ref[1, :keys, :] = (code >> 5) & 31
    split_ref[2, :keys, :] = code >> 10


def bias_of(split_ref, table_ref, head, keys):
    spread = [
        jnp.broadcast_to(table_ref[pl.ds(t * HEADS + head, 1), :], (keys, COLS))
        for t in range(TABLES)
    ]
    found = [lane_gather(spread[t], split_ref[t, :keys, :]) for t in range(TABLES)]
    return found[0] + found[1] + found[2]


def bias_kernel(codes_ref, table_ref, bias_ref, split_ref, *, first_head):
    unpack_codes(codes_ref, split_ref, FEW)

    @pl.loop(0, bias_ref.shape[0])
    def _(head):
        bias_ref[head] = bias_of(split_ref, table_ref, first_head + head, FEW)


def layout_bias(codes, table_lanes, first_head):
    tokens = codes.shape[1]
    return pl.pallas_call(
        functools.partial(bias_kernel, first_head=first_head),
        grid=(tokens // COLS,),
        in_specs=[
            pl.BlockSpec((FEW, COLS), lambda i: (0, i)),
            pl.BlockSpec(table_lanes.shape, lambda i: (0, 0)),
        ],
        out_specs=pl.BlockSpec((HEADS // 2, FEW, COLS), lambda i: (0, 0, i)),
        out_shape=jax.ShapeDtypeStruct((HEADS // 2, FEW, tokens), F32),
        scratch_shapes=[pltpu.VMEM((TABLES, FEW, COLS), jnp.int32)],
        compiler_params=pltpu.CompilerParams(vmem_limit_bytes=VMEM_LIMIT),
        cost_estimate=pl.CostEstimate(
            flops=16_000_000_000, bytes_accessed=7_000_000, transcendentals=0
        ),
        name="layout_bias",
    )(codes, table_lanes)


def each_group(run, groups, short):
    if short:
        for group in range(groups):
            run(group)
    else:
        lax.fori_loop(0, groups, lambda group, carry: (run(group), carry)[1], 0)


def own_blocks(turned):
    return jnp.concatenate(
        [
            turned[h * HEAD_DIM : (h + 1) * HEAD_DIM, h * COLS : (h + 1) * COLS]
            for h in range(GROUP)
        ],
        0,
    )


def attend_kernel(
    count_ref,
    normed_ref,
    picked_ref,
    wq_ref,
    wk_ref,
    wv_ref,
    wo_ref,
    codes_ref,
    table_ref,
    low_bias_ref,
    high_bias_ref,
    x_ref,
    gain_ref,
    q_ref,
    k_ref,
    v_ref,
    mixed_ref,
    lse_ref,
    prob_ref,
    mid_ref,
    normed_two_ref,
    split_ref,
    turned_ref,
    attended_ref,
):
    step = pl.program_id(0)
    few = count_ref[0] <= FEW
    total_keys = picked_ref.shape[0]

    def project(rows):
        picked = picked_ref[rows, :]
        k_ref[rows, :] = dot_nn(picked, wk_ref[...]).astype(BF)
        values = dot_nn(picked, wv_ref[...]).astype(BF)
        v_ref[rows, :] = values
        turned_ref[:, rows] = values.T

    @pl.when(step == 0)
    def _():
        q_ref[...] = dot_nn(normed_ref[...], wq_ref[...]).astype(BF)

    @pl.when(jnp.logical_and(step == 0, few))
    def _():
        project(pl.ds(0, FEW))

    @pl.when(jnp.logical_and(step == 0, jnp.logical_not(few)))
    def _():
        @pl.loop(0, total_keys // 256)
        def _(block):
            project(pl.ds(pl.multiple_of(block * 256, 256), 256))

    here = pl.ds(pl.multiple_of(step * COLS, COLS), COLS)
    masks = head_masks()

    def attend(keys, short):
        def run(group):
            lanes = lanes_of(group)
            queries = stack_heads(q_ref[here, lanes], masks)
            scores = dot_nt(k_ref[0:keys, lanes], queries)
            pieces = []
            for h in range(GROUP):
                head = group * GROUP + h
                if short:
                    half = HEADS // 2
                    bias = low_bias_ref[head] if head < half else high_bias_ref[head - half]
                else:
                    bias = bias_of(split_ref, table_ref, head, keys)
                score = scores[:, h * COLS : (h + 1) * COLS] + bias
                top = jnp.max(score, 0, keepdims=True)
                grown = jnp.exp(score - top)
                total = jnp.sum(grown, 0, keepdims=True)
                prob = grown * (1.0 / total)
                if short:
                    prob_ref[head] = prob
                lse_ref[pl.ds(head, 1), :] = top + jnp.log(total)
                pieces.append(prob.astype(BF))
            mixed = dot_nn(turned_ref[lanes, 0:keys], jnp.concatenate(pieces, 1))
            mixed_ref[lanes, here] = own_blocks(mixed).astype(BF)

        if not short:
            unpack_codes(codes_ref, split_ref, keys)
        each_group(run, HEADS // GROUP, short)

    pl.when(few)(lambda: attend(FEW, True))
    pl.when(jnp.logical_not(few))(lambda: attend(total_keys, False))

    @pl.when(step == pl.num_programs(0) - 1)
    def _():
        gain = gain_ref[0:1, :]
        attended_ref[...] = mixed_ref[...].T

        @pl.loop(0, x_ref.shape[0] // 256)
        def _(block):
            rows = pl.ds(pl.multiple_of(block * 256, 256), 256)
            middle = x_ref[rows, :].astype(F32) + dot_nn(attended_ref[rows, :], wo_ref[...])
            mid_ref[rows, :] = middle
            normed_two_ref[rows, :] = norm_rows(middle, gain).astype(BF)


def attention_forward(count, normed, picked, weights, codes, table_lanes, bias, x_block, gain_two):
    tokens = normed.shape[0]
    keys = picked.shape[0]
    full = lambda shape: pl.BlockSpec(shape, lambda i, c: (0, 0))
    weight = lambda at: pl.BlockSpec((D, D), lambda i, c: (0, at), pipeline_mode=pl.Buffered(1))
    across = lambda height: pl.BlockSpec((height, COLS), lambda i, c: (0, i))
    headed = pl.BlockSpec((HEADS, FEW, COLS), lambda i, c: (0, 0, i))
    shape = jax.ShapeDtypeStruct
    return pl.pallas_call(
        attend_kernel,
        grid_spec=pltpu.PrefetchScalarGridSpec(
            num_scalar_prefetch=1,
            grid=(tokens // COLS,),
            in_specs=[
                full((tokens, D)),
                full((keys, D)),
                weight(0),
                weight(1),
                weight(2),
                weight(3),
                across(keys),
                full(table_lanes.shape),
                pl.BlockSpec((HEADS // 2, FEW, COLS), lambda i, c: (0, 0, i)),
                pl.BlockSpec((HEADS // 2, FEW, COLS), lambda i, c: (0, 0, i)),
                full((tokens, D)),
                full((8, D)),
            ],
            out_specs=[
                full((tokens, D)),
                full((keys, D)),
                full((keys, D)),
                full((D, tokens)),
                across(HEADS),
                headed,
                full((tokens, D)),
                full((tokens, D)),
            ],
            scratch_shapes=[
                pltpu.VMEM((TABLES, keys, COLS), jnp.int32),
                pltpu.VMEM((D, keys), BF),
                pltpu.VMEM((tokens, D), BF),
            ],
        ),
        out_shape=[
            shape((tokens, D), BF),
            shape((keys, D), BF),
            shape((keys, D), BF),
            shape((D, tokens), BF),
            shape((HEADS, tokens), F32),
            shape((HEADS, FEW, tokens), F32),
            shape((tokens, D), F32),
            shape((tokens, D), BF),
        ],
        compiler_params=pltpu.CompilerParams(vmem_limit_bytes=VMEM_LIMIT),
        cost_estimate=pl.CostEstimate(
            flops=20_000_000_000, bytes_accessed=50_000_000, transcendentals=3_000_000
        ),
        name="attention_forward",
    )(count, normed, picked, weights, weights, weights, weights, codes, table_lanes, *bias, x_block, gain_two)


def ffn_kernel(
    scalar_ref,
    normed_ref,
    out_cot_ref,
    mid_ref,
    gain_ref,
    gate_ref,
    up_own_ref,
    up_other_ref,
    down_own_ref,
    down_other_ref,
    gate_sent_ref,
    gate_kept_ref,
    up_sent_ref,
    up_kept_ref,
    down_sent_ref,
    down_kept_ref,
    layer_ref,
    middle_grad_ref,
    attn_grad_ref,
    gain_grad_ref,
    stat_ref,
    turned_ref,
    branch_ref,
    back_ref,
    down_all_ref,
    pair_ref,
    pair_grad_ref,
    down_ref,
    *,
    gather_order,
    scatter_order,
):
    step = pl.program_id(0)
    device = scalar_ref[1]
    down_device = device if down_kept_ref.shape[1] % 8 == 0 else 0

    @pl.when(step == 0)
    def _():
        turned_ref[...] = normed_ref[...].T
        join_pieces(down_own_ref, down_other_ref, down_all_ref, down_device, *gather_order[2])

    pair_ref[:, :FF_TILE] = gate_ref[...].astype(pair_ref.dtype)
    join_pieces(up_own_ref, up_other_ref, pair_ref, device, *gather_order[1], FF_TILE)
    here = pl.ds(pl.multiple_of(step * FF_TILE, FF_TILE), FF_TILE)
    down_ref[...] = down_all_ref[here, :].astype(BF)

    normed = normed_ref[...]
    pair_weight = pair_ref[...].astype(BF)
    both = dot_nn(normed, pair_weight)
    gate = both[:, :FF_TILE]
    up = both[:, FF_TILE:]
    grad_act = dot_nt(out_cot_ref[...], down_ref[...])
    scale = 0.7978845608028654
    square = gate * gate
    bent = jnp.tanh(scale * (gate + 0.044715 * (square * gate)))
    half = 0.5 * (1.0 + bent)
    curved = gate * half
    slope = half + 0.5 * gate * (1.0 - bent * bent) * (scale * (1.0 + 0.134145 * square))
    activated = (curved * up).astype(BF)
    grad_gate = (grad_act * up * slope).astype(BF)
    grad_up = (grad_act * curved).astype(BF)
    grad_pair = jnp.concatenate([grad_gate, grad_up], 1)
    branch = dot_nn(activated, down_ref[...])
    back = dot_nt(grad_pair, pair_weight)

    @pl.when(step == 0)
    def _():
        branch_ref[...] = branch
        back_ref[...] = back

    @pl.when(step > 0)
    def _():
        branch_ref[...] += branch
        back_ref[...] += back

    pair_grad_ref[...] = dot_nn(turned_ref[...], grad_pair).astype(pair_grad_ref.dtype)
    part_pieces(pair_grad_ref, gate_sent_ref, gate_kept_ref, device, scatter_order[0])
    part_pieces(pair_grad_ref, up_sent_ref, up_kept_ref, device, scatter_order[1], 0, FF_TILE)
    down_all_ref[here, :] = dot_tn(activated, out_cot_ref[...])

    @pl.when(step == pl.num_programs(0) - 1)
    def _():
        part_pieces(
            down_all_ref, down_sent_ref, down_kept_ref, down_device, scatter_order[2]
        )
        gain = gain_ref[0:1, :]
        gain_grad_ref[...] = jnp.zeros_like(gain_grad_ref)
        lane = lax.broadcasted_iota(jnp.int32, (ROWS, 128), 1)

        @pl.loop(0, mid_ref.shape[0] // ROWS)
        def _(block):
            rows = pl.ds(pl.multiple_of(block * ROWS, ROWS), ROWS)
            middle = mid_ref[rows, :]
            final = middle + branch_ref[rows, :]
            layer_ref[rows, :] = final.astype(BF)
            mid_sum = jnp.sum(middle * middle, -1, keepdims=True)
            final_sum = jnp.sum(final * final, -1, keepdims=True)
            stat_ref[rows, :] = jnp.where(lane == 0, mid_sum, final_sum)
            inverse = lax.rsqrt(mid_sum * (1.0 / D) + EPS)
            unit = middle * inverse
            grad_normed = back_ref[rows, :]
            weighted = grad_normed * gain
            inner = jnp.mean(weighted * unit, -1, keepdims=True)
            grad_middle = out_cot_ref[rows, :].astype(F32) + inverse * (weighted - unit * inner)
            middle_grad_ref[rows, :] = grad_middle
            attn_grad_ref[rows, :] = grad_middle.astype(BF)
            gain_grad_ref[0:1, :] += jnp.sum(grad_normed * unit, 0, keepdims=True)


def feed_forward(scalars, normed_two, out_cot, middle, gain_two, weights, up, down):
    tokens = normed_two.shape[0]
    half, rows, ff = up[0].shape
    gate_at = 4 * D // FF_TILE
    down_rows = down[0].shape[1]
    once = pl.Buffered(1)
    full = lambda shape: pl.BlockSpec(shape, lambda i, c: (0,) * len(shape), pipeline_mode=once)
    tile = pl.BlockSpec((half, rows, FF_TILE), lambda i, c: (0, 0, i))
    shape = jax.ShapeDtypeStruct
    kernel = functools.partial(
        ffn_kernel,
        gather_order=[None, gather_masks(1), gather_masks(3)],
        scatter_order=[scatter_masks(kind) for kind in range(3)],
    )
    return pl.pallas_call(
        kernel,
        grid_spec=pltpu.PrefetchScalarGridSpec(
            num_scalar_prefetch=1,
            grid=(ff // FF_TILE,),
            in_specs=[
                full((tokens, D)),
                full((tokens, D)),
                full((tokens, D)),
                full((8, D)),
                pl.BlockSpec((D, FF_TILE), lambda i, c: (0, gate_at + i)),
                tile,
                tile,
                full((half, down_rows, D)),
                full((half, down_rows, D)),
            ],
            out_specs=[
                tile,
                tile,
                tile,
                tile,
                full((half, down_rows, D)),
                full((half, down_rows, D)),
                full((tokens, D)),
                full((tokens, D)),
                full((tokens, D)),
                full((8, D)),
                full((tokens, 128)),
            ],
            scratch_shapes=[
                pltpu.VMEM((D, tokens), BF),
                pltpu.VMEM((tokens, D), F32),
                pltpu.VMEM((tokens, D), F32),
                pltpu.VMEM((ff, D), F32),
                pltpu.VMEM((D, 2 * FF_TILE), held_type(rows)),
                pltpu.VMEM((D, 2 * FF_TILE), held_type(rows)),
                pltpu.VMEM((FF_TILE, D), BF),
            ],
        ),
        out_shape=[shape((half, rows, ff), BF)] * 4
        + [shape((half, down_rows, D), BF)] * 2
        + [
            shape((tokens, D), BF),
            shape((tokens, D), F32),
            shape((tokens, D), BF),
            shape((8, D), F32),
            shape((tokens, 128), F32),
        ],
        compiler_params=pltpu.CompilerParams(vmem_limit_bytes=VMEM_LIMIT),
        cost_estimate=pl.CostEstimate(
            flops=27_000_000_000, bytes_accessed=44_000_000, transcendentals=1_500_000
        ),
        name="feed_forward",
    )(scalars, normed_two, out_cot, middle, gain_two, weights, *up, *down)


def add_histogram(split_ref, grad_ref, hist_ref, chosen_ref, keys):
    heads = grad_ref.shape[0]
    cols = split_ref.shape[2]
    bucket = lax.broadcasted_iota(jnp.int32, (BUCKETS, cols), 0)

    @pl.loop(0, keys // HIST_ROWS)
    def _(block):
        base = pl.multiple_of(block * HIST_ROWS, HIST_ROWS)
        grads = grad_ref[:, pl.ds(base, HIST_ROWS), :]
        grads = grads.reshape(heads * HIST_ROWS, cols)
        for row in range(HIST_ROWS):
            for t in range(TABLES):
                at = (row * TABLES + t) * BUCKETS
                match = split_ref[t, pl.ds(base + row, 1), :] == bucket
                chosen_ref[at : at + BUCKETS, :] = match.astype(F32).astype(BF)
        hist_ref[...] += dot_nt(chosen_ref[...], grads)


def take_histogram(hist_ref, out_ref):
    height, width = out_ref.shape
    own = lax.broadcasted_iota(jnp.int32, (height, width), 1) & (HIST_ROWS - 1)
    total = jnp.zeros((height, width), F32)
    for row in range(HIST_ROWS):
        piece = hist_ref[row * height : (row + 1) * height, :]
        total = total + jnp.where(own == row, piece, 0.0)
    out_ref[...] = total


def backward_kernel(
    count_ref,
    attn_grad_ref,
    wo_ref,
    q_ref,
    k_ref,
    v_ref,
    lse_ref,
    prob_ref,
    codes_ref,
    table_ref,
    normed_turned_ref,
    picked_turned_ref,
    mixed_ref,
    dq_ref,
    dk_ref,
    dv_ref,
    grad_ref,
    hist_out_ref,
    sent_ref,
    kept_ref,
    back_ref,
    split_ref,
    long_grad_ref,
    turned_ref,
    dq_turned_ref,
    dk_sum_ref,
    dv_sum_ref,
    hist_ref,
    chosen_ref,
    joined_ref,
    *,
    first_head,
    scatter_order,
):
    step = pl.program_id(0)
    few = count_ref[0] <= FEW
    total_keys = k_ref.shape[0]
    heads = q_ref.shape[1] // HEAD_DIM

    @pl.when(step == 0)
    def _():
        back_ref[...] = dot_nt(attn_grad_ref[...], wo_ref[...]).astype(BF)
        dk_sum_ref[...] = jnp.zeros_like(dk_sum_ref)
        dv_sum_ref[...] = jnp.zeros_like(dv_sum_ref)
        hist_ref[...] = jnp.zeros_like(hist_ref)

    @pl.when(jnp.logical_and(step == 0, few))
    def _():
        turned_ref[:, 0:FEW] = k_ref[0:FEW, :].T

    @pl.when(jnp.logical_and(step == 0, jnp.logical_not(few)))
    def _():
        turned_ref[...] = k_ref[...].T

    here = pl.ds(pl.multiple_of(step * COLS, COLS), COLS)
    masks = head_masks()

    def turn_back(keys, short):
        def run(group):
            lanes = lanes_of(group)
            queries = stack_heads(q_ref[here, lanes], masks)
            grads = stack_heads(back_ref[here, lanes], masks)
            prob_grads = dot_nt(v_ref[0:keys, lanes], grads)
            if not short:
                scores = dot_nt(k_ref[0:keys, lanes], queries)
            score_grads = []
            probs = []
            for h in range(GROUP):
                cols = slice(h * COLS, (h + 1) * COLS)
                local = group * GROUP + h
                if short:
                    prob = prob_ref[local]
                else:
                    head = first_head + local
                    bias = bias_of(split_ref, table_ref, head, keys)
                    prob = jnp.exp(scores[:, cols] + bias - lse_ref[pl.ds(head, 1), :])
                weighted = prob * prob_grads[:, cols]
                inner = jnp.sum(weighted, 0, keepdims=True)
                score_grad = (weighted - prob * inner).astype(BF)
                if short:
                    grad_ref[local] = score_grad
                else:
                    long_grad_ref[local] = score_grad
                score_grads.append(score_grad)
                probs.append(prob.astype(BF))
            score_grads = jnp.concatenate(score_grads, 1)
            probs = jnp.concatenate(probs, 1)
            dq_turned_ref[lanes, here] = own_blocks(
                dot_nn(turned_ref[lanes, 0:keys], score_grads)
            ).astype(BF)
            dk_sum_ref[0:keys, lanes] += dot_nn(score_grads, queries)
            dv_sum_ref[0:keys, lanes] += dot_nn(probs, grads)

        if not short:
            unpack_codes(codes_ref, split_ref, keys)
        each_group(run, heads // GROUP, short)
        if not short:
            add_histogram(split_ref, long_grad_ref, hist_ref, chosen_ref, keys)

    pl.when(few)(lambda: turn_back(FEW, True))
    pl.when(jnp.logical_not(few))(lambda: turn_back(total_keys, False))

    def leave(number, gradient):
        joined_ref[...] = gradient.astype(joined_ref.dtype)
        at = number * joined_ref.shape[1]
        part_pieces(joined_ref, sent_ref, kept_ref, count_ref[1], scatter_order, at)

    def finish(keys):
        leave(1, dot_nn(picked_turned_ref[:, 0:keys], dk_ref[0:keys, :]))
        leave(2, dot_nn(picked_turned_ref[:, 0:keys], dv_ref[0:keys, :]))

    @pl.when(step == pl.num_programs(0) - 1)
    def _():
        dk_ref[...] = dk_sum_ref[...].astype(BF)
        dv_ref[...] = dv_sum_ref[...].astype(BF)
        dq_ref[...] = dq_turned_ref[...].T
        leave(0, dot_nn(normed_turned_ref[...], dq_ref[...]))
        first = first_head * HEAD_DIM
        leave(3, dot_nn(mixed_ref[...], attn_grad_ref[:, first : first + heads * HEAD_DIM]))
        take_histogram(hist_ref, hist_out_ref)
        pl.when(few)(lambda: finish(FEW))
        pl.when(jnp.logical_not(few))(lambda: finish(total_keys))


def attention_backward(
    half,
    kind,
    count,
    attn_grad,
    weights,
    queries,
    keys,
    values,
    lse,
    probs,
    codes,
    table_lanes,
    normed_turned,
    picked_turned,
    mixed,
):
    tokens = queries.shape[0]
    device_count = lax.axis_size("row") * lax.axis_size("col")
    rows = D // device_count
    key_total = keys.shape[0]
    heads = HEADS // 2
    width = heads * HEAD_DIM
    full = lambda shape: pl.BlockSpec(shape, lambda i, c: (0, 0))
    side = lambda height: pl.BlockSpec((height, width), lambda i, c: (0, half))
    across = lambda height: pl.BlockSpec((height, COLS), lambda i, c: (0, i))
    shape = jax.ShapeDtypeStruct
    hist_shape = (TABLES * BUCKETS, heads * HIST_ROWS)
    return pl.pallas_call(
        functools.partial(
            backward_kernel,
            first_head=half * heads,
            scatter_order=scatter_masks(kind),
        ),
        grid_spec=pltpu.PrefetchScalarGridSpec(
            num_scalar_prefetch=1,
            grid=(tokens // COLS,),
            in_specs=[
                full((tokens, D)),
                pl.BlockSpec((width, D), lambda i, c: (half, 3)),
                side(tokens),
                side(key_total),
                side(key_total),
                across(HEADS),
                pl.BlockSpec((heads, FEW, COLS), lambda i, c: (half, 0, i)),
                across(key_total),
                full(table_lanes.shape),
                full((D, tokens)),
                full((D, key_total)),
                full((D, tokens)),
            ],
            out_specs=[
                full((tokens, width)),
                full((key_total, width)),
                full((key_total, width)),
                pl.BlockSpec((heads, FEW, COLS), lambda i, c: (0, 0, i)),
                full(hist_shape),
            ]
            + [
                pl.BlockSpec((device_count // 2, rows, 4 * width), lambda i, c: (0, 0, 0)),
            ]
            * 2,
            scratch_shapes=[
                pltpu.VMEM((tokens, width), BF),
                pltpu.VMEM((TABLES, key_total, COLS), jnp.int32),
                pltpu.VMEM((heads, key_total, COLS), BF),
                pltpu.VMEM((width, key_total), BF),
                pltpu.VMEM((width, tokens), BF),
                pltpu.VMEM((key_total, width), F32),
                pltpu.VMEM((key_total, width), F32),
                pltpu.VMEM((HIST_ROWS * hist_shape[0], hist_shape[1]), F32),
                pltpu.VMEM((HIST_ROWS * hist_shape[0], COLS), BF),
                pltpu.VMEM((D, width), held_type(rows)),
            ],
        ),
        out_shape=[
            shape((tokens, width), BF),
            shape((key_total, width), BF),
            shape((key_total, width), BF),
            shape((heads, FEW, tokens), BF),
            shape(hist_shape, F32),
        ]
        + [shape((device_count // 2, rows, 4 * width), BF)] * 2,
        compiler_params=pltpu.CompilerParams(vmem_limit_bytes=VMEM_LIMIT),
        cost_estimate=pl.CostEstimate(
            flops=15_000_000_000, bytes_accessed=30_000_000, transcendentals=0
        ),
        name="attention_backward",
    )(
        count,
        attn_grad,
        weights,
        queries,
        keys,
        values,
        lse,
        probs,
        codes,
        table_lanes,
        normed_turned,
        picked_turned,
        mixed,
    )


def histogram_kernel(
    count_ref, codes_ref, low_ref, high_ref, out_ref, split_ref, both_ref, hist_ref, chosen_ref
):
    out_ref[...] = jnp.zeros_like(out_ref)

    @pl.when(count_ref[0] <= FEW)
    def _():
        unpack_codes(codes_ref, split_ref, FEW)
        both_ref[: HEADS // 2] = low_ref[...]
        both_ref[HEADS // 2 :] = high_ref[...]
        hist_ref[...] = jnp.zeros_like(hist_ref)
        add_histogram(split_ref, both_ref, hist_ref, chosen_ref, FEW)
        take_histogram(hist_ref, out_ref)


def table_histogram(count, codes, low, high):
    tokens = codes.shape[1]
    hist_shape = (TABLES * BUCKETS, HEADS * HIST_ROWS)
    whole = lambda shape: pl.BlockSpec(shape, lambda i, c: (0,) * len(shape))
    return pl.pallas_call(
        histogram_kernel,
        grid_spec=pltpu.PrefetchScalarGridSpec(
            num_scalar_prefetch=1,
            grid=(1,),
            in_specs=[whole((FEW, tokens)), whole(low.shape), whole(high.shape)],
            out_specs=whole(hist_shape),
            scratch_shapes=[
                pltpu.VMEM((TABLES, FEW, tokens), jnp.int32),
                pltpu.VMEM((HEADS, FEW, tokens), BF),
                pltpu.VMEM((HIST_ROWS * hist_shape[0], hist_shape[1]), F32),
                pltpu.VMEM((HIST_ROWS * hist_shape[0], tokens), BF),
            ],
        ),
        out_shape=jax.ShapeDtypeStruct(hist_shape, F32),
        compiler_params=pltpu.CompilerParams(vmem_limit_bytes=VMEM_LIMIT),
        cost_estimate=pl.CostEstimate(
            flops=20_000_000_000, bytes_accessed=8_000_000, transcendentals=0
        ),
        name="table_histogram",
    )(count, codes, low, high)


def key_gradients_kernel(
    count_ref,
    dq_low_ref,
    dq_high_ref,
    dk_low_ref,
    dk_high_ref,
    dv_low_ref,
    dv_high_ref,
    wq_ref,
    wk_ref,
    wv_ref,
    pack_ref,
    x_ref,
    picked_ref,
    lent_ref,
    own_ref,
    gain_ref,
    both_ref,
):
    tokens = x_ref.shape[0]
    half = D // 2
    few = count_ref[0] <= FEW

    def unit(rows):
        rows = rows.astype(F32)
        return rows * lax.rsqrt(jnp.mean(rows * rows, -1, keepdims=True) + EPS)

    def product(low, high, weight_ref):
        return dot_nt(low, weight_ref[:, :half]) + dot_nt(high, weight_ref[:, half:])

    gain_ref[...] = jnp.zeros_like(gain_ref)
    own_ref[...] = product(dq_low_ref[...], dq_high_ref[...], wq_ref)

    @pl.loop(0, tokens // COLS)
    def _(block):
        rows = pl.ds(pl.multiple_of(block * COLS, COLS), COLS)
        gain_ref[0:1, :] += jnp.sum(own_ref[rows, :] * unit(x_ref[rows, :]), 0, keepdims=True)

    def spread(keys, step):
        @pl.loop(0, keys // step)
        def _(block):
            rows = pl.ds(pl.multiple_of(block * step, step), step)
            grads = product(dk_low_ref[rows, :], dk_high_ref[rows, :], wk_ref)
            grads = grads + product(dv_low_ref[rows, :], dv_high_ref[rows, :], wv_ref)
            gain_ref[0:1, :] += jnp.sum(grads * unit(picked_ref[rows, :]), 0, keepdims=True)
            high = grads.astype(BF)
            both_ref[0, rows, :] = high
            both_ref[1, rows, :] = (grads - high.astype(F32)).astype(BF)

        high = both_ref[0, 0:keys, :]
        chosen = pack_ref[0:tokens, 0:keys]
        own_ref[...] += dot_nn(chosen, high) + dot_nn(chosen, both_ref[1, 0:keys, :])
        lent_ref[...] = dot_nn(pack_ref[tokens:, 0:keys], high).astype(BF)

    pl.when(few)(lambda: spread(FEW, FEW))
    pl.when(jnp.logical_not(few))(lambda: spread(pack_ref.shape[1], COLS))


def key_gradients(count, low, high, weights, pack, x_block, picked_x):
    tokens = x_block.shape[0]
    keys = pack.shape[0]
    whole = lambda shape: pl.BlockSpec(shape, lambda i, c: (0, 0))
    weight = lambda at: pl.BlockSpec((D, D), lambda i, c: (0, at))
    shape = jax.ShapeDtypeStruct
    return pl.pallas_call(
        key_gradients_kernel,
        grid_spec=pltpu.PrefetchScalarGridSpec(
            num_scalar_prefetch=1,
            grid=(1,),
            in_specs=[
                whole((tokens, D // 2)),
                whole((tokens, D // 2)),
                whole((keys, D // 2)),
                whole((keys, D // 2)),
                whole((keys, D // 2)),
                whole((keys, D // 2)),
                weight(0),
                weight(1),
                weight(2),
                whole(pack.shape),
                whole((tokens, D)),
                whole((keys, D)),
            ],
            out_specs=[whole((keys - tokens, D)), whole((tokens, D)), whole((8, D))],
            scratch_shapes=[pltpu.VMEM((2, keys, D), BF)],
        ),
        out_shape=[
            shape((keys - tokens, D), BF),
            shape((tokens, D), F32),
            shape((8, D), F32),
        ],
        compiler_params=pltpu.CompilerParams(vmem_limit_bytes=VMEM_LIMIT),
        cost_estimate=pl.CostEstimate(
            flops=9_000_000_000, bytes_accessed=18_000_000, transcendentals=0
        ),
        name="key_gradients",
    )(count, low[0], high[0], low[1], high[1], low[2], high[2], weights, weights, weights, pack, x_block, picked_x)


def input_kernel(own_ref, owner_ref, returned_ref, x_ref, gain_ref, middle_ref, out_ref):
    grads = own_ref[...] + dot_nn(owner_ref[...], returned_ref[...])
    rows = x_ref[...].astype(F32)
    inverse = lax.rsqrt(jnp.mean(rows * rows, -1, keepdims=True) + EPS)
    unit = rows * inverse
    weighted = grads * gain_ref[0:1, :]
    inner = jnp.mean(weighted * unit, -1, keepdims=True)
    out_ref[...] = (middle_ref[...] + inverse * (weighted - unit * inner)).astype(BF)


def input_gradient(own, owner, returned, x_block, gain_one, grad_middle):
    tokens = own.shape[0]
    streamed = lambda width: pl.BlockSpec((COLS, width), lambda i: (i, 0))
    whole = lambda shape: pl.BlockSpec(shape, lambda i: (0, 0))
    return pl.pallas_call(
        input_kernel,
        grid=(tokens // COLS,),
        in_specs=[
            streamed(D),
            streamed(owner.shape[1]),
            whole(returned.shape),
            streamed(D),
            whole((8, D)),
            streamed(D),
        ],
        out_specs=streamed(D),
        out_shape=jax.ShapeDtypeStruct((tokens, D), BF),
        compiler_params=pltpu.CompilerParams(vmem_limit_bytes=VMEM_LIMIT),
        cost_estimate=pl.CostEstimate(
            flops=1_000_000_000, bytes_accessed=8_000_000, transcendentals=0
        ),
        name="input_gradient",
    )(own, owner, returned, x_block, gain_one, grad_middle)


def on_device(
    hidden_in,
    out_cotangent,
    query_weight,
    key_weight,
    value_weight,
    output_weight,
    attn_gain,
    relative_table,
    horiz_table,
    vert_table,
    ffn_gain,
    gate_weight,
    up_weight,
    down_weight,
    key_keep,
    halo_rows,
    relative_bucket,
    horiz_bucket,
    vert_bucket,
):
    tokens = hidden_in.shape[0]
    rows = gate_weight.shape[0]
    table_share = relative_table.shape[0]
    row_index = lax.axis_index("row")
    col_index = lax.axis_index("col")
    row_count = lax.axis_size("row")
    col_count = lax.axis_size("col")
    region = row_index * col_count + col_index
    device_count = row_count * col_count

    packed_weights = jnp.concatenate(
        [query_weight, key_weight, value_weight, output_weight, gate_weight], 1
    )
    weights = lax.all_gather(packed_weights, ("row", "col"), axis=0, tiled=True)
    small = jnp.stack(
        [attn_gain, ffn_gain]
        + [jnp.pad(t, (0, rows - table_share)) for t in (relative_table, horiz_table, vert_table)],
        1,
    )
    small = jnp.pad(small, ((0, 0), (0, 128 - small.shape[1])))
    small, up_weight, down_weight = after((small, up_weight, down_weight), packed_weights)
    small_gather = Gather(small, 0, True)
    ffn_gathers = [Gather(up_weight, 1), Gather(down_weight, 3)]

    def turn(gathers, *done):
        for gather in gathers:
            gather.land(*done)
        return [gather.send() for gather in gathers]

    sent = turn([small_gather] + ffn_gathers)

    halo_rows, key_keep, x_early = after((halo_rows, key_keep, hidden_in), sent)
    own_lists = lax.dynamic_index_in_dim(halo_rows, region, 0, keepdims=False)
    rim = x_early[own_lists]
    sent = turn([small_gather], rim)
    rim = after(rim, sent)
    above, below = shifted(rim[0:2], "row")
    left, right = shifted(rim[2:4], "col")
    neighbours = jnp.stack([region - col_count, region + col_count, region - 1, region + 1])
    present = jnp.stack(
        [row_index > 0, row_index < row_count - 1, col_index > 0, col_index < col_count - 1]
    ).astype(jnp.int32)
    list_ids = jnp.array([1, 0, 3, 2], dtype=jnp.int32)
    clipped = jnp.clip(neighbours, 0, device_count - 1)
    their_lists = after(halo_rows, rim)[clipped, list_ids]
    halo_keep = key_keep[clipped[:, None] * tokens + their_lists] * present[:, None]
    own_keep = lax.dynamic_slice_in_dim(key_keep, region * tokens, tokens)
    key_mask = jnp.concatenate([own_keep, halo_keep.reshape(-1)])
    key_total = key_mask.shape[0]

    place = jnp.cumsum(key_mask) - 1
    count = place[-1:] + 1
    scalars = jnp.concatenate([count, region.reshape(1)])
    slots = jnp.arange(key_total, dtype=jnp.int32)
    pack = ((place[:, None] == slots) & (key_mask[:, None] > 0)).astype(BF)

    sent = turn([small_gather] + ffn_gathers, pack)
    packed_by, relative_bucket = after((pack, relative_bucket), sent)
    found = [
        lax.dot_general(
            packed_by, bucket.astype(BF), (((0,), (1,)), ((), ())), preferred_element_type=F32
        ).astype(jnp.int32)
        for bucket in (relative_bucket, horiz_bucket, vert_bucket)
    ]
    found_vert = jnp.where(slots[:, None] < count, found[2], BUCKETS)
    codes = found[0] + found[1] * BUCKETS + found_vert * (BUCKETS * BUCKETS)

    sent = turn([small_gather], codes)
    packed_by, above = after((pack, above), sent, codes)
    x_keys = jnp.concatenate([hidden_in, above, below, left, right], 0)
    picked_x = dot_nn(packed_by.T, x_keys).astype(BF)
    turn([small_gather], picked_x)
    while small_gather.flight is not None:
        turn([small_gather])
    sent = turn(ffn_gathers, small_gather.held)
    small_masks = [0]
    for stage in stages_of(0)[::-1]:
        small_masks = small_masks + [mask ^ mask_of(stage) for mask in small_masks]
    place_of = [0] * device_count
    for at, mask in enumerate(small_masks):
        place_of[mask] = at
    devices = jnp.arange(device_count, dtype=jnp.int32)
    small_all = small_gather.held[jnp.array(place_of, jnp.int32)[devices ^ region]]
    gain_attn, gain_ffn = [small_all[:, :, i].reshape(-1) for i in range(2)]
    table_rows = [
        small_all[:, :table_share, 2 + t].reshape(BUCKETS, HEADS).T for t in range(TABLES)
    ]
    table_lanes = jnp.pad(
        jnp.stack(table_rows).astype(F32), ((0, 0), (0, 0), (0, 128 - BUCKETS))
    )
    table_lanes = table_lanes.at[2, :, BUCKETS].set(masked_score).reshape(TABLES * HEADS, 128)
    gain_one = gain_attn.astype(F32)
    gain_two = jnp.broadcast_to(gain_ffn.astype(F32), (8, D))

    low_bias = layout_bias(after(codes, sent), table_lanes, 0)
    sent = turn(ffn_gathers, low_bias)
    high_bias = layout_bias(after(codes, sent, low_bias), table_lanes, HEADS // 2)
    x_input = hidden_in.astype(F32)
    normed_one = norm_rows(x_input, gain_one).astype(BF)
    picked = norm_rows(picked_x.astype(F32), gain_one).astype(BF)
    normed_turned = normed_one.T
    picked_turned = picked.T
    turn(ffn_gathers, high_bias, picked_turned, normed_turned)
    while any(gather.flight is not None for gather in ffn_gathers):
        turn(ffn_gathers)
    gathered = [gather.held for gather in ffn_gathers]
    ffn_weights = [(held, exchange(held, ("row", 0))) for held in gathered]
    normed_one = after(normed_one, gathered, normed_turned, picked_turned)
    queries, keys, values, mixed, lse, probs, x_middle, normed_two = attention_forward(
        scalars,
        normed_one,
        picked,
        weights,
        codes,
        table_lanes,
        (low_bias, high_bias),
        hidden_in,
        gain_two,
    )
    ffn_weights = [(own, after(other, normed_two)) for own, other in ffn_weights]
    uneven = down_weight.shape[0] % 8 != 0
    if uneven:
        order, core_mask = gather_masks(3)
        order = order + tuple(mask ^ core_mask for mask in order)
        ffn_weights[1] = reordered(*ffn_weights[1], order, region)
    (
        gate_sent,
        gate_kept,
        up_sent,
        up_kept,
        down_sent,
        down_kept,
        layer_out,
        grad_middle,
        grad_attn,
        ffn_gain_part,
        row_stats,
    ) = feed_forward(
        scalars, normed_two, out_cotangent, x_middle, gain_two, weights, *ffn_weights
    )
    if uneven:
        down_kept, down_sent = reordered(down_kept, down_sent, scatter_masks(2), region)
    ffn_chains = [
        Scatter(gate_sent, gate_kept, 0),
        Scatter(up_sent, up_kept, 1),
        Scatter(down_sent, down_kept, 2),
    ]
    rounds = Rounds()
    rounds.chains += ffn_chains

    def backward(half, kind, grad_attn):
        return attention_backward(
            half,
            kind,
            scalars,
            grad_attn,
            weights,
            queries,
            keys,
            values,
            lse,
            probs,
            codes,
            table_lanes,
            normed_turned,
            picked_turned,
            mixed,
        )

    sent = rounds.send()
    low_half = backward(0, 2, after(grad_attn, sent))
    low_chain = Scatter(low_half[5], low_half[6], 2)
    rounds.land(low_half[0])
    rounds.chains.append(low_chain)
    sent = rounds.send()
    high_half = backward(1, 1, after(grad_attn, low_half[0], sent))
    high_chain = Scatter(high_half[5], high_half[6], 1)
    rounds.land(high_half[0])
    rounds.chains.append(high_chain)
    sent = rounds.send()
    short_hist = table_histogram(
        scalars, after(codes, high_half[0], sent), low_half[3], high_half[3]
    )
    sent = rounds.turn(short_hist)
    lent, own_grads, attn_gain_part = key_gradients(
        scalars,
        low_half[:3],
        high_half[:3],
        weights,
        after(pack, short_hist, sent),
        hidden_in,
        picked_x,
    )
    hist = short_hist + jnp.concatenate([low_half[4], high_half[4]], 1)
    grad_table = jnp.sum(hist.reshape(TABLES * BUCKETS, HEADS, HIST_ROWS), -1)
    keep_float = own_keep.astype(F32)
    stat_part = jnp.stack(
        [
            jnp.sum(keep_float * jnp.sum(x_input * x_input, -1)),
            jnp.sum(keep_float * row_stats[:, 0]),
            jnp.sum(keep_float * row_stats[:, 1]),
            jnp.sum(keep_float),
        ]
    )
    small_part = jnp.concatenate(
        [
            jnp.pad(stat_part, (0, 124)),
            ffn_gain_part[0],
            attn_gain_part[0],
            grad_table.reshape(-1),
        ]
    ).reshape(-1, 128)
    small_rows = small_part.shape[0]
    small_part = jnp.pad(small_part, ((0, 128 - small_rows), (0, 0)))
    small_parts = lax.all_gather(small_part, ("row", "col"), axis=0, tiled=True)
    summed = jnp.sum(small_parts.reshape(device_count, 128, 128)[:, :small_rows], 0).reshape(-1)
    rounds.land(lent)
    lent = lent.reshape(4, -1, D)
    back_above, back_below = shifted(lent[0:2], "row")
    back_left, back_right = shifted(lent[2:4], "col")
    sent = rounds.send()
    returned = jnp.concatenate([back_above, back_below, back_left, back_right], 0)
    owner_lists = own_lists.reshape(-1)
    owner = (jnp.arange(tokens, dtype=jnp.int32)[:, None] == owner_lists).astype(BF)
    input_grad = input_gradient(
        own_grads,
        owner,
        after(returned, sent),
        hidden_in,
        jnp.broadcast_to(gain_one, (8, D)),
        grad_middle,
    )
    rounds.turn(input_grad)
    while rounds.chains:
        rounds.turn()

    residual_rms = jnp.sqrt(summed[:3] / (summed[3] * D))
    own_part = lambda at, size: lax.dynamic_slice_in_dim(summed, at + region * size, size)
    ffn_gain_grad = own_part(128, rows)
    attn_gain_grad = own_part(128 + D, rows)
    table_at = 128 + 2 * D
    table_grads = [own_part(table_at + t * BUCKETS * HEADS, table_share) for t in range(TABLES)]
    gate_grad, up_grad, down_grad = [chain.total() for chain in ffn_chains]
    sides = [low_chain.total(), high_chain.total()]
    width = D // 2
    query_grad, key_grad, value_grad, output_grad = [
        jnp.concatenate([side[:, i * width : (i + 1) * width] for side in sides], 1)
        for i in range(4)
    ]
    return (
        layer_out,
        input_grad,
        query_grad,
        key_grad,
        value_grad,
        output_grad,
        attn_gain_grad,
        table_grads[0],
        table_grads[1],
        table_grads[2],
        ffn_gain_grad,
        gate_grad,
        up_grad,
        down_grad,
        residual_rms,
    )


def solution(mesh):
    split = P(("row", "col"), None)
    line = P(("row", "col"))
    return jax.shard_map(
        on_device,
        mesh=mesh,
        in_specs=(split,) * 6 + (line,) * 5 + (split,) * 3 + (P(), P()) + (split,) * 3,
        out_specs=(split,) * 6 + (line,) * 5 + (split,) * 3 + (P(),),
        check_vma=False,
    )
```

```python
import functools

import jax
import jax.numpy as jnp
from jax import lax
from jax.experimental import pallas as pl
from jax.experimental.pallas import tpu as pltpu
from jax.sharding import PartitionSpec as P

D = 1024
HEADS = 16
HEAD_DIM = 64
BUCKETS = 32
TABLES = 3

EPS = 1e-06
masked_score = -1e30
FEW = 384
COLS = 128
ROWS = 64
GROUP = 4
WIDE = GROUP * HEAD_DIM
HIST_ROWS = 16
FF_TILE = 256
VMEM_LIMIT = 56 * 1024 * 1024
BF = jnp.bfloat16
F32 = jnp.float32


def shifted(block, axis):
    count = lax.axis_size(axis)
    forward = [(i, i + 1) for i in range(count - 1)]
    backward = [(target, source) for source, target in forward]
    return (
        lax.ppermute(block[1], axis, forward),
        lax.ppermute(block[0], axis, backward),
    )


def norm_rows(values, gain_row):
    return values * lax.rsqrt(jnp.mean(values * values, -1, keepdims=True) + EPS) * gain_row


def stages_of(kind):
    row_bits = [("row", bit) for bit in range(lax.axis_size("row").bit_length() - 1)]
    col_bits = [("col", bit) for bit in range(lax.axis_size("col").bit_length() - 1)]
    if kind == 0:
        return row_bits[:1] + col_bits + row_bits[1:]
    if kind == 1:
        return row_bits[:1] + col_bits[::-1] + row_bits[1:]
    if kind == 2:
        return row_bits[:2] + col_bits + row_bits[2:]
    return row_bits[:2] + col_bits[::-1] + row_bits[2:]


def mask_of(stage):
    axis, bit = stage
    return (lax.axis_size("col") if axis == "row" else 1) << bit


def scatter_masks(kind):
    masks = [0]
    for stage in stages_of(kind)[::-1]:
        masks = masks + [mask ^ mask_of(stage) for mask in masks]
    return tuple(masks)


def gather_masks(kind):
    masks = [0]
    for stage in stages_of(kind)[:0:-1]:
        masks = masks + [mask ^ mask_of(stage) for mask in masks]
    return tuple(masks), mask_of(("row", 0))


def exchange(values, stage):
    axis, bit = stage
    pairs = [(i, i ^ (1 << bit)) for i in range(lax.axis_size(axis))]
    return lax.ppermute(values, axis, pairs)


def after(values, *earlier):
    return lax.optimization_barrier((values, earlier))[0]


class Gather:
    def __init__(self, shard, kind, both=False):
        self.held = shard[None]
        self.stages = stages_of(kind)[::-1] if both else stages_of(kind)[:0:-1]
        self.flight = None

    def send(self):
        if self.stages:
            self.flight = exchange(self.held, self.stages.pop(0))
        return self.held

    def land(self, *done):
        if self.flight is not None:
            if done:
                self.flight = after(self.flight, *done)
            self.held = jnp.concatenate([self.held, self.flight], 0)
            self.flight = None


class Scatter:
    def __init__(self, sent, kept, kind):
        self.stages = stages_of(kind)
        self.first = sent
        self.parts = [(kept, 0)]
        self.pieces, self.rows, self.width = sent.shape


class Rounds:
    def __init__(self):
        self.chains = []
        self.flights = []

    def land(self, *done):
        landed = [flight for chains, flight in self.flights]
        for chains, flight in self.flights:
            if done:
                flight = after(flight, *done)
            for number, chain in enumerate(chains):
                chain.parts.append((flight, number * chain.width))
        self.flights = []
        self.chains = [chain for chain in self.chains if chain.stages]
        return landed

    def send(self):
        sums, firsts = {}, []
        for chain in self.chains:
            stage = chain.stages.pop(0)
            if chain.first is not None:
                firsts.append(([chain], stage, chain.first))
                chain.first = None
            else:
                chain.pieces //= 2
                alike = (stage, chain.pieces, chain.rows, chain.width)
                sums.setdefault(alike, []).append(chain)
        sent = firsts
        if sums:
            values = piece_sums(list(sums.values()), True, BF)
            sent = sent + [
                (chains, alike[0], value)
                for (alike, chains), value in zip(sums.items(), values)
            ]
        for chains, stage, value in sent:
            self.flights.append((chains, exchange(value, stage)))
        return [value for chains, stage, value in sent]

    def turn(self, *done):
        self.land(*done)
        return self.send()


def sum_kernel(*refs, shares):
    refs = list(refs)
    outputs = refs[len(refs) - len(shares) :]
    for out_ref, (counts, width) in zip(outputs, shares):
        for number, count in enumerate(counts):
            total = refs.pop(0)[...].astype(F32)
            for _ in range(count - 1):
                total = total + refs.pop(0)[...].astype(F32)
            out_ref[:, :, number * width : (number + 1) * width] = total.astype(out_ref.dtype)


def piece_sums(groups, upper, dtype):
    steps = min([4] + [chains[0].pieces for chains in groups]) if upper else 1
    arrays, in_specs, out_specs, out_shape, shares = [], [], [], [], []
    for chains in groups:
        pieces, rows, width = chains[0].pieces, chains[0].rows, chains[0].width
        block = pieces // steps if upper else 1
        for chain in chains:
            for array, column in chain.parts:
                arrays.append(array)
                place = lambda i, lane=column // width: (steps + i if upper else 0, 0, lane)
                in_specs.append(pl.BlockSpec((block, rows, width), place))
        total = len(chains) * width
        out_specs.append(pl.BlockSpec((block, rows, total), lambda i: (i, 0, 0)))
        out_shape.append(jax.ShapeDtypeStruct((block * steps, rows, total), dtype))
        shares.append(([len(chain.parts) for chain in chains], width))
    moved = sum(2 * spec.block_shape[0] * spec.block_shape[1] * spec.block_shape[2] * steps for spec in in_specs)
    return pl.pallas_call(
        functools.partial(sum_kernel, shares=shares),
        grid=(steps,),
        in_specs=in_specs,
        out_specs=out_specs,
        out_shape=out_shape,
        compiler_params=pltpu.CompilerParams(vmem_limit_bytes=VMEM_LIMIT),
        cost_estimate=pl.CostEstimate(flops=moved, bytes_accessed=2 * moved, transcendentals=0),
        name="piece_sums",
    )(*arrays)


def dot_nn(left, right):
    return lax.dot_general(left, right, (((1,), (0,)), ((), ())), preferred_element_type=F32)


def dot_nt(left, right):
    return lax.dot_general(left, right, (((1,), (1,)), ((), ())), preferred_element_type=F32)


def dot_tn(left, right):
    return lax.dot_general(left, right, (((0,), (0,)), ((), ())), preferred_element_type=F32)


def pack_kernel(*refs):
    *sources, down_ref, out_ref = refs
    at = 0
    for source_ref in sources:
        width = source_ref.shape[1]
        out_ref[:, at : at + width] = source_ref[...]
        at += width
    down = down_ref[...].astype(F32)
    for b in range(down.shape[0] // 8):
        blocks = [down[8 * b : 8 * b + 8, a * 256 : (a + 1) * 256] for a in range(D // 256)]
        out_ref[:, at + b * 256 : at + (b + 1) * 256] = jnp.concatenate(blocks, 0).astype(BF)


def pack_shards(sources, down):
    rows = sources[0].shape[0]
    widths = [source.shape[1] for source in sources]
    total = sum(widths) + down.shape[0] * D // rows
    if down.shape[0] % 8 != 0 or rows * 256 != 8 * D:
        return jnp.concatenate(list(sources) + [down.reshape(rows, -1)], 1)
    return pl.pallas_call(
        pack_kernel,
        out_shape=jax.ShapeDtypeStruct((rows, total), BF),
        compiler_params=pltpu.CompilerParams(vmem_limit_bytes=VMEM_LIMIT),
        name="pack_shards",
    )(*sources, down)


LANE_GATHER = lax.GatherDimensionNumbers(
    offset_dims=(),
    collapsed_slice_dims=(1,),
    start_index_map=(1,),
    operand_batching_dims=(0,),
    start_indices_batching_dims=(0,),
)


def lane_gather(rows, index):
    return lax.gather(
        rows,
        index[:, :, None],
        LANE_GATHER,
        (1, 1),
        mode=lax.GatherScatterMode.PROMISE_IN_BOUNDS,
    )


def lanes_of(group):
    if isinstance(group, int):
        return pl.ds(group * WIDE, WIDE)
    return pl.ds(pl.multiple_of(group * WIDE, WIDE), WIDE)


def held_type(height):
    return BF if height % 16 == 0 else F32


def reordered(low, high, masks, device):
    place = [0] * len(masks)
    for at, mask in enumerate(masks):
        place[mask] = at
    index = jnp.array(place, jnp.int32)[jnp.array(masks, jnp.int32) ^ device]
    both = jnp.concatenate([low, high], 0)[index]
    return both[: len(masks) // 2], both[len(masks) // 2 :]


def placed(owner, height):
    start = owner * height
    if isinstance(start, int):
        return pl.ds(start, height)
    if height % 8 == 0:
        start = pl.multiple_of(start, height & -height)
    return pl.ds(start, height)


def join_pieces(own_ref, other_ref, joined_ref, device, masks, core_mask, at=0):
    height = own_ref.shape[1]
    lanes = slice(at, at + own_ref.shape[2])
    for p, mask in enumerate(masks):
        joined_ref[placed(device ^ mask, height), lanes] = own_ref[p].astype(joined_ref.dtype)
        joined_ref[placed(device ^ mask ^ core_mask, height), lanes] = other_ref[p].astype(
            joined_ref.dtype
        )


def part_pieces(joined_ref, sent_ref, kept_ref, device, masks, at=0, source=0):
    half, height, width = kept_ref.shape
    width = min(width, joined_ref.shape[1])
    lanes = slice(at, at + width)
    taken = slice(source, source + width)
    for p, mask in enumerate(masks):
        target_ref = kept_ref if p < half else sent_ref
        target_ref[p % half, :, lanes] = joined_ref[placed(device ^ mask, height), taken].astype(BF)


def head_masks():
    lane = lax.broadcasted_iota(jnp.int32, (1, WIDE), 1) >> 6
    return [(lane == h).astype(F32).astype(BF) for h in range(GROUP)]


def stack_heads(block, masks):
    return jnp.concatenate([block * mask for mask in masks], 0)


def unpack_codes(codes_ref, split_ref, keys):
    code = codes_ref[:keys, :]
    split_ref[0, :keys, :] = code & 31
    split_ref[1, :keys, :] = (code >> 5) & 31
    split_ref[2, :keys, :] = code >> 10


def bias_of(split_ref, table_ref, head, keys):
    spread = [
        jnp.broadcast_to(table_ref[pl.ds(t * HEADS + head, 1), :], (keys, COLS))
        for t in range(TABLES)
    ]
    found = [lane_gather(spread[t], split_ref[t, :keys, :]) for t in range(TABLES)]
    return found[0] + found[1] + found[2]


def bias_kernel(codes_ref, table_ref, bias_ref, split_ref, *, first_head):
    unpack_codes(codes_ref, split_ref, FEW)

    @pl.loop(0, bias_ref.shape[0])
    def _(head):
        bias_ref[head] = bias_of(split_ref, table_ref, first_head + head, FEW)


def layout_bias(codes, table_lanes, first_head):
    tokens = codes.shape[1]
    return pl.pallas_call(
        functools.partial(bias_kernel, first_head=first_head),
        grid=(tokens // COLS,),
        in_specs=[
            pl.BlockSpec((FEW, COLS), lambda i: (0, i)),
            pl.BlockSpec(table_lanes.shape, lambda i: (0, 0)),
        ],
        out_specs=pl.BlockSpec((HEADS // 2, FEW, COLS), lambda i: (0, 0, i)),
        out_shape=jax.ShapeDtypeStruct((HEADS // 2, FEW, tokens), F32),
        scratch_shapes=[pltpu.VMEM((TABLES, FEW, COLS), jnp.int32)],
        compiler_params=pltpu.CompilerParams(vmem_limit_bytes=VMEM_LIMIT),
        cost_estimate=pl.CostEstimate(
            flops=16_000_000_000, bytes_accessed=7_000_000, transcendentals=0
        ),
        name="layout_bias",
    )(codes, table_lanes)


def each_group(run, groups, short):
    if short:
        for group in range(groups):
            run(group)
    else:
        lax.fori_loop(0, groups, lambda group, carry: (run(group), carry)[1], 0)


def own_blocks(turned):
    return jnp.concatenate(
        [
            turned[h * HEAD_DIM : (h + 1) * HEAD_DIM, h * COLS : (h + 1) * COLS]
            for h in range(GROUP)
        ],
        0,
    )


def attend_kernel(
    count_ref,
    normed_ref,
    picked_ref,
    wq_ref,
    wk_ref,
    wv_ref,
    wo_ref,
    codes_ref,
    table_ref,
    low_bias_ref,
    high_bias_ref,
    x_ref,
    gain_ref,
    q_ref,
    k_ref,
    v_ref,
    mixed_ref,
    lse_ref,
    prob_ref,
    mid_ref,
    normed_two_ref,
    split_ref,
    turned_ref,
    attended_ref,
):
    step = pl.program_id(0)
    few = count_ref[0] <= FEW
    total_keys = picked_ref.shape[0]

    def project(rows):
        picked = picked_ref[rows, :]
        k_ref[rows, :] = dot_nn(picked, wk_ref[...]).astype(BF)
        values = dot_nn(picked, wv_ref[...]).astype(BF)
        v_ref[rows, :] = values
        turned_ref[:, rows] = values.T

    @pl.when(step == 0)
    def _():
        q_ref[...] = dot_nn(normed_ref[...], wq_ref[...]).astype(BF)

    @pl.when(jnp.logical_and(step == 0, few))
    def _():
        project(pl.ds(0, FEW))

    @pl.when(jnp.logical_and(step == 0, jnp.logical_not(few)))
    def _():
        @pl.loop(0, total_keys // 256)
        def _(block):
            project(pl.ds(pl.multiple_of(block * 256, 256), 256))

    here = pl.ds(pl.multiple_of(step * COLS, COLS), COLS)
    masks = head_masks()

    def attend(keys, short):
        def run(group):
            lanes = lanes_of(group)
            queries = stack_heads(q_ref[here, lanes], masks)
            scores = dot_nt(k_ref[0:keys, lanes], queries)
            pieces = []
            for h in range(GROUP):
                head = group * GROUP + h
                if short:
                    half = HEADS // 2
                    bias = low_bias_ref[head] if head < half else high_bias_ref[head - half]
                else:
                    bias = bias_of(split_ref, table_ref, head, keys)
                score = scores[:, h * COLS : (h + 1) * COLS] + bias
                top = jnp.max(score, 0, keepdims=True)
                grown = jnp.exp(score - top)
                total = jnp.sum(grown, 0, keepdims=True)
                prob = grown * (1.0 / total)
                if short:
                    prob_ref[head] = prob
                lse_ref[pl.ds(head, 1), :] = top + jnp.log(total)
                pieces.append(prob.astype(BF))
            mixed = dot_nn(turned_ref[lanes, 0:keys], jnp.concatenate(pieces, 1))
            mixed_ref[lanes, here] = own_blocks(mixed).astype(BF)

        if not short:
            unpack_codes(codes_ref, split_ref, keys)
        each_group(run, HEADS // GROUP, short)

    pl.when(few)(lambda: attend(FEW, True))
    pl.when(jnp.logical_not(few))(lambda: attend(total_keys, False))

    @pl.when(step == pl.num_programs(0) - 1)
    def _():
        gain = gain_ref[0:1, :]
        attended_ref[...] = mixed_ref[...].T

        @pl.loop(0, x_ref.shape[0] // 256)
        def _(block):
            rows = pl.ds(pl.multiple_of(block * 256, 256), 256)
            middle = x_ref[rows, :].astype(F32) + dot_nn(attended_ref[rows, :], wo_ref[...])
            mid_ref[rows, :] = middle
            normed_two_ref[rows, :] = norm_rows(middle, gain).astype(BF)


def attention_forward(count, normed, picked, weights, codes, table_lanes, bias, x_block, gain_two):
    tokens = normed.shape[0]
    keys = picked.shape[0]
    full = lambda shape: pl.BlockSpec(shape, lambda i, c: (0, 0))
    weight = lambda at: pl.BlockSpec((D, D), lambda i, c: (0, at), pipeline_mode=pl.Buffered(1))
    across = lambda height: pl.BlockSpec((height, COLS), lambda i, c: (0, i))
    headed = pl.BlockSpec((HEADS, FEW, COLS), lambda i, c: (0, 0, i))
    shape = jax.ShapeDtypeStruct
    return pl.pallas_call(
        attend_kernel,
        grid_spec=pltpu.PrefetchScalarGridSpec(
            num_scalar_prefetch=1,
            grid=(tokens // COLS,),
            in_specs=[
                full((tokens, D)),
                full((keys, D)),
                weight(0),
                weight(1),
                weight(2),
                weight(3),
                across(keys),
                full(table_lanes.shape),
                pl.BlockSpec((HEADS // 2, FEW, COLS), lambda i, c: (0, 0, i)),
                pl.BlockSpec((HEADS // 2, FEW, COLS), lambda i, c: (0, 0, i)),
                full((tokens, D)),
                full((8, D)),
            ],
            out_specs=[
                full((tokens, D)),
                full((keys, D)),
                full((keys, D)),
                full((D, tokens)),
                across(HEADS),
                headed,
                full((tokens, D)),
                full((tokens, D)),
            ],
            scratch_shapes=[
                pltpu.VMEM((TABLES, keys, COLS), jnp.int32),
                pltpu.VMEM((D, keys), BF),
                pltpu.VMEM((tokens, D), BF),
            ],
        ),
        out_shape=[
            shape((tokens, D), BF),
            shape((keys, D), BF),
            shape((keys, D), BF),
            shape((D, tokens), BF),
            shape((HEADS, tokens), F32),
            shape((HEADS, FEW, tokens), F32),
            shape((tokens, D), F32),
            shape((tokens, D), BF),
        ],
        compiler_params=pltpu.CompilerParams(vmem_limit_bytes=VMEM_LIMIT),
        cost_estimate=pl.CostEstimate(
            flops=20_000_000_000, bytes_accessed=50_000_000, transcendentals=3_000_000
        ),
        name="attention_forward",
    )(count, normed, picked, weights, weights, weights, weights, codes, table_lanes, *bias, x_block, gain_two)


def ffn_kernel(
    scalar_ref,
    normed_ref,
    out_cot_ref,
    mid_ref,
    gain_ref,
    keep_ref,
    gate_ref,
    up_ref,
    packed_ref,
    gate_sent_ref,
    gate_kept_ref,
    up_sent_ref,
    up_kept_ref,
    down_sent_ref,
    down_kept_ref,
    layer_ref,
    middle_grad_ref,
    attn_grad_ref,
    gain_grad_ref,
    turned_ref,
    branch_ref,
    back_ref,
    down_all_ref,
    gate_grad_ref,
    up_grad_ref,
    down_ref,
    landed_ref,
    landed_sem,
    *,
    scatter_order,
):
    step = pl.program_id(0)
    device = scalar_ref[1]
    down_device = device if down_kept_ref.shape[1] % 8 == 0 else 0

    @pl.when(step == 0)
    def _():
        if landed_ref.shape[0] == D:
            at = packed_ref.shape[1] - landed_ref.shape[1]
            source_ref = packed_ref.at[:, at:]
        else:
            source_ref = packed_ref
        copy = pltpu.make_async_copy(source_ref, landed_ref, landed_sem)
        copy.start()
        turned_ref[...] = normed_ref[...].T
        copy.wait()
        if landed_ref.shape[0] != D:
            down_all_ref[...] = landed_ref[...].astype(F32)
        else:
            height = landed_ref.shape[1] // 32
            for d in range(D // 32):
                for b in range(height // 8):
                    block = landed_ref[d * 32 : (d + 1) * 32, b * 256 : (b + 1) * 256].astype(F32)
                    rows = slice(d * height + 8 * b, d * height + 8 * b + 8)
                    for a in range(D // 256):
                        lanes = slice(a * 256, (a + 1) * 256)
                        down_all_ref[rows, lanes] = block[8 * a : 8 * a + 8]
        branch_ref[...] = jnp.zeros_like(branch_ref)
        back_ref[...] = jnp.zeros_like(back_ref)

    here = pl.ds(pl.multiple_of(step * FF_TILE, FF_TILE), FF_TILE)
    down_ref[...] = down_all_ref[here, :].astype(BF)

    normed = normed_ref[...]
    gate = dot_nn(normed, gate_ref[...])
    up = dot_nn(normed, up_ref[...])
    grad_act = dot_nt(out_cot_ref[...], down_ref[...])
    scale = 0.7978845608028654
    square = gate * gate
    bent = jnp.tanh(scale * (gate + 0.044715 * (square * gate)))
    half = 0.5 * (1.0 + bent)
    curved = gate * half
    slope = half + 0.5 * gate * (1.0 - bent * bent) * (scale * (1.0 + 0.134145 * square))
    activated = (curved * up).astype(BF)
    grad_gate = (grad_act * up * slope).astype(BF)
    grad_up = (grad_act * curved).astype(BF)
    branch_ref[...] += dot_nn(activated, down_ref[...])
    back_ref[...] += dot_nt(grad_gate, gate_ref[...]) + dot_nt(grad_up, up_ref[...])
    gate_grad_ref[...] = dot_nn(turned_ref[...], grad_gate).astype(gate_grad_ref.dtype)
    part_pieces(gate_grad_ref, gate_sent_ref, gate_kept_ref, device, scatter_order[0])
    up_grad_ref[...] = dot_nn(turned_ref[...], grad_up).astype(up_grad_ref.dtype)
    part_pieces(up_grad_ref, up_sent_ref, up_kept_ref, device, scatter_order[1])
    down_all_ref[here, :] = dot_tn(activated, out_cot_ref[...])

    @pl.when(step == pl.num_programs(0) - 1)
    def _():
        part_pieces(
            down_all_ref, down_sent_ref, down_kept_ref, down_device, scatter_order[2]
        )
        gain = gain_ref[0:1, :]
        gain_grad_ref[...] = jnp.zeros_like(gain_grad_ref)
        lane = lax.broadcasted_iota(jnp.int32, (ROWS, 128), 1)

        @pl.loop(0, mid_ref.shape[0] // ROWS)
        def _(block):
            rows = pl.ds(pl.multiple_of(block * ROWS, ROWS), ROWS)
            middle = mid_ref[rows, :]
            final = middle + branch_ref[rows, :]
            layer_ref[rows, :] = final.astype(BF)
            mid_sum = jnp.sum(middle * middle, -1, keepdims=True)
            final_sum = jnp.sum(final * final, -1, keepdims=True)
            sums = jnp.where(lane == 1, mid_sum, jnp.where(lane == 2, final_sum, 1.0))
            gain_grad_ref[1:2, :128] += jnp.sum(keep_ref[rows, :] * sums, 0, keepdims=True)
            inverse = lax.rsqrt(mid_sum * (1.0 / D) + EPS)
            unit = middle * inverse
            grad_normed = back_ref[rows, :]
            weighted = grad_normed * gain
            inner = jnp.mean(weighted * unit, -1, keepdims=True)
            grad_middle = out_cot_ref[rows, :].astype(F32) + inverse * (weighted - unit * inner)
            middle_grad_ref[rows, :] = grad_middle
            attn_grad_ref[rows, :] = grad_middle.astype(BF)
            gain_grad_ref[0:1, :] += jnp.sum(grad_normed * unit, 0, keepdims=True)


def feed_forward(scalars, normed_two, out_cot, middle, gain_two, keep, weights, down):
    tokens = normed_two.shape[0]
    ff = (weights.shape[1] - 4 * D) // 3
    half = lax.axis_size("row") * lax.axis_size("col") // 2
    down_rows = ff // (2 * half)
    rows = D // (2 * half)
    gate_at = 4 * D // FF_TILE
    up_at = gate_at + ff // FF_TILE
    once = pl.Buffered(1)
    full = lambda shape: pl.BlockSpec(shape, lambda i, c: (0,) * len(shape), pipeline_mode=once)
    tile = pl.BlockSpec((half, rows, FF_TILE), lambda i, c: (0, 0, i))
    shape = jax.ShapeDtypeStruct
    kernel = functools.partial(
        ffn_kernel,
        scatter_order=[scatter_masks(kind) for kind in range(3)],
    )
    return pl.pallas_call(
        kernel,
        grid_spec=pltpu.PrefetchScalarGridSpec(
            num_scalar_prefetch=1,
            grid=(ff // FF_TILE,),
            in_specs=[
                full((tokens, D)),
                full((tokens, D)),
                full((tokens, D)),
                full((8, D)),
                full((tokens, 128)),
                pl.BlockSpec((D, FF_TILE), lambda i, c: (0, gate_at + i)),
                pl.BlockSpec((D, FF_TILE), lambda i, c: (0, up_at + i)),
                pl.BlockSpec(memory_space=pl.ANY),
            ],
            out_specs=[
                tile,
                tile,
                tile,
                tile,
                full((half, down_rows, D)),
                full((half, down_rows, D)),
                full((tokens, D)),
                full((tokens, D)),
                full((tokens, D)),
                full((8, D)),
            ],
            scratch_shapes=[
                pltpu.VMEM((D, tokens), BF),
                pltpu.VMEM((tokens, D), F32),
                pltpu.VMEM((tokens, D), F32),
                pltpu.VMEM((ff, D), F32),
                pltpu.VMEM((D, FF_TILE), held_type(rows)),
                pltpu.VMEM((D, FF_TILE), held_type(rows)),
                pltpu.VMEM((FF_TILE, D), BF),
                pltpu.VMEM((ff, D) if down is not None else (D, ff), BF),
                pltpu.SemaphoreType.DMA(()),
            ],
        ),
        out_shape=[shape((half, rows, ff), BF)] * 4
        + [shape((half, down_rows, D), BF)] * 2
        + [
            shape((tokens, D), BF),
            shape((tokens, D), F32),
            shape((tokens, D), BF),
            shape((8, D), F32),
        ],
        compiler_params=pltpu.CompilerParams(vmem_limit_bytes=VMEM_LIMIT),
        cost_estimate=pl.CostEstimate(
            flops=27_000_000_000, bytes_accessed=44_000_000, transcendentals=1_500_000
        ),
        name="feed_forward",
    )(scalars, normed_two, out_cot, middle, gain_two, keep, weights, weights, weights if down is None else down)


def add_histogram(split_ref, grad_ref, hist_ref, chosen_ref, keys):
    heads = grad_ref.shape[0]
    cols = split_ref.shape[2]
    bucket = lax.broadcasted_iota(jnp.int32, (BUCKETS, cols), 0)

    @pl.loop(0, keys // HIST_ROWS)
    def _(block):
        base = pl.multiple_of(block * HIST_ROWS, HIST_ROWS)
        grads = grad_ref[:, pl.ds(base, HIST_ROWS), :]
        grads = grads.reshape(heads * HIST_ROWS, cols)
        for row in range(HIST_ROWS):
            for t in range(TABLES):
                at = (row * TABLES + t) * BUCKETS
                match = split_ref[t, pl.ds(base + row, 1), :] == bucket
                chosen_ref[at : at + BUCKETS, :] = match.astype(F32).astype(BF)
        hist_ref[...] += dot_nt(chosen_ref[...], grads)


def take_histogram(hist_ref, out_ref):
    height, width = out_ref.shape
    own = lax.broadcasted_iota(jnp.int32, (height, width), 1) & (HIST_ROWS - 1)
    total = jnp.zeros((height, width), F32)
    for row in range(HIST_ROWS):
        piece = hist_ref[row * height : (row + 1) * height, :]
        total = total + jnp.where(own == row, piece, 0.0)
    out_ref[...] = total


def backward_kernel(
    count_ref,
    attn_grad_ref,
    wo_ref,
    q_ref,
    k_ref,
    v_ref,
    lse_ref,
    prob_ref,
    codes_ref,
    table_ref,
    normed_ref,
    picked_ref,
    mixed_ref,
    dq_ref,
    dk_ref,
    dv_ref,
    grad_ref,
    hist_out_ref,
    sent_ref,
    kept_ref,
    back_ref,
    split_ref,
    long_grad_ref,
    turned_ref,
    dq_turned_ref,
    dk_sum_ref,
    dv_sum_ref,
    hist_ref,
    chosen_ref,
    joined_ref,
    *,
    first_head,
    scatter_order,
):
    step = pl.program_id(0)
    few = count_ref[0] <= FEW
    total_keys = k_ref.shape[0]
    heads = q_ref.shape[1] // HEAD_DIM

    @pl.when(step == 0)
    def _():
        back_ref[...] = dot_nt(attn_grad_ref[...], wo_ref[...]).astype(BF)
        dk_sum_ref[...] = jnp.zeros_like(dk_sum_ref)
        dv_sum_ref[...] = jnp.zeros_like(dv_sum_ref)
        hist_ref[...] = jnp.zeros_like(hist_ref)

    @pl.when(jnp.logical_and(step == 0, few))
    def _():
        turned_ref[:, 0:FEW] = k_ref[0:FEW, :].T

    @pl.when(jnp.logical_and(step == 0, jnp.logical_not(few)))
    def _():
        turned_ref[...] = k_ref[...].T

    here = pl.ds(pl.multiple_of(step * COLS, COLS), COLS)
    masks = head_masks()

    def turn_back(keys, short):
        def run(group):
            lanes = lanes_of(group)
            queries = stack_heads(q_ref[here, lanes], masks)
            grads = stack_heads(back_ref[here, lanes], masks)
            prob_grads = dot_nt(v_ref[0:keys, lanes], grads)
            if not short:
                scores = dot_nt(k_ref[0:keys, lanes], queries)
            score_grads = []
            probs = []
            for h in range(GROUP):
                cols = slice(h * COLS, (h + 1) * COLS)
                local = group * GROUP + h
                if short:
                    prob = prob_ref[local]
                else:
                    head = first_head + local
                    bias = bias_of(split_ref, table_ref, head, keys)
                    prob = jnp.exp(scores[:, cols] + bias - lse_ref[pl.ds(head, 1), :])
                weighted = prob * prob_grads[:, cols]
                inner = jnp.sum(weighted, 0, keepdims=True)
                score_grad = (weighted - prob * inner).astype(BF)
                if short:
                    grad_ref[local] = score_grad
                else:
                    long_grad_ref[local] = score_grad
                score_grads.append(score_grad)
                probs.append(prob.astype(BF))
            score_grads = jnp.concatenate(score_grads, 1)
            probs = jnp.concatenate(probs, 1)
            dq_turned_ref[lanes, here] = own_blocks(
                dot_nn(turned_ref[lanes, 0:keys], score_grads)
            ).astype(BF)
            dk_sum_ref[0:keys, lanes] += dot_nn(score_grads, queries)
            dv_sum_ref[0:keys, lanes] += dot_nn(probs, grads)

        if not short:
            unpack_codes(codes_ref, split_ref, keys)
        each_group(run, heads // GROUP, short)
        if not short:
            add_histogram(split_ref, long_grad_ref, hist_ref, chosen_ref, keys)

    pl.when(few)(lambda: turn_back(FEW, True))
    pl.when(jnp.logical_not(few))(lambda: turn_back(total_keys, False))

    def leave(number, gradient):
        joined_ref[...] = gradient.astype(joined_ref.dtype)
        at = number * joined_ref.shape[1]
        part_pieces(joined_ref, sent_ref, kept_ref, count_ref[1], scatter_order, at)

    def finish(keys):
        leave(1, dot_tn(picked_ref[0:keys, :], dk_ref[0:keys, :]))
        leave(2, dot_tn(picked_ref[0:keys, :], dv_ref[0:keys, :]))

    @pl.when(step == pl.num_programs(0) - 1)
    def _():
        dk_ref[...] = dk_sum_ref[...].astype(BF)
        dv_ref[...] = dv_sum_ref[...].astype(BF)
        dq_ref[...] = dq_turned_ref[...].T
        leave(0, dot_tn(normed_ref[...], dq_ref[...]))
        first = first_head * HEAD_DIM
        leave(3, dot_nn(mixed_ref[...], attn_grad_ref[:, first : first + heads * HEAD_DIM]))
        take_histogram(hist_ref, hist_out_ref)
        pl.when(few)(lambda: finish(FEW))
        pl.when(jnp.logical_not(few))(lambda: finish(total_keys))


def attention_backward(
    half,
    kind,
    count,
    attn_grad,
    weights,
    queries,
    keys,
    values,
    lse,
    probs,
    codes,
    table_lanes,
    normed,
    picked,
    mixed,
):
    tokens = queries.shape[0]
    device_count = lax.axis_size("row") * lax.axis_size("col")
    rows = D // device_count
    key_total = keys.shape[0]
    heads = HEADS // 2
    width = heads * HEAD_DIM
    full = lambda shape: pl.BlockSpec(shape, lambda i, c: (0, 0))
    side = lambda height: pl.BlockSpec((height, width), lambda i, c: (0, half))
    across = lambda height: pl.BlockSpec((height, COLS), lambda i, c: (0, i))
    shape = jax.ShapeDtypeStruct
    hist_shape = (TABLES * BUCKETS, heads * HIST_ROWS)
    return pl.pallas_call(
        functools.partial(
            backward_kernel,
            first_head=half * heads,
            scatter_order=scatter_masks(kind),
        ),
        grid_spec=pltpu.PrefetchScalarGridSpec(
            num_scalar_prefetch=1,
            grid=(tokens // COLS,),
            in_specs=[
                full((tokens, D)),
                pl.BlockSpec((width, D), lambda i, c: (half, 3)),
                side(tokens),
                side(key_total),
                side(key_total),
                across(HEADS),
                pl.BlockSpec((heads, FEW, COLS), lambda i, c: (half, 0, i)),
                across(key_total),
                full(table_lanes.shape),
                full((tokens, D)),
                full((key_total, D)),
                full((D, tokens)),
            ],
            out_specs=[
                full((tokens, width)),
                full((key_total, width)),
                full((key_total, width)),
                pl.BlockSpec((heads, FEW, COLS), lambda i, c: (0, 0, i)),
                full(hist_shape),
            ]
            + [
                pl.BlockSpec((device_count // 2, rows, 4 * width), lambda i, c: (0, 0, 0)),
            ]
            * 2,
            scratch_shapes=[
                pltpu.VMEM((tokens, width), BF),
                pltpu.VMEM((TABLES, key_total, COLS), jnp.int32),
                pltpu.VMEM((heads, key_total, COLS), BF),
                pltpu.VMEM((width, key_total), BF),
                pltpu.VMEM((width, tokens), BF),
                pltpu.VMEM((key_total, width), F32),
                pltpu.VMEM((key_total, width), F32),
                pltpu.VMEM((HIST_ROWS * hist_shape[0], hist_shape[1]), F32),
                pltpu.VMEM((HIST_ROWS * hist_shape[0], COLS), BF),
                pltpu.VMEM((D, width), held_type(rows)),
            ],
        ),
        out_shape=[
            shape((tokens, width), BF),
            shape((key_total, width), BF),
            shape((key_total, width), BF),
            shape((heads, FEW, tokens), BF),
            shape(hist_shape, F32),
        ]
        + [shape((device_count // 2, rows, 4 * width), BF)] * 2,
        compiler_params=pltpu.CompilerParams(vmem_limit_bytes=VMEM_LIMIT),
        cost_estimate=pl.CostEstimate(
            flops=15_000_000_000, bytes_accessed=30_000_000, transcendentals=0
        ),
        name="attention_backward",
    )(
        count,
        attn_grad,
        weights,
        queries,
        keys,
        values,
        lse,
        probs,
        codes,
        table_lanes,
        normed,
        picked,
        mixed,
    )


def histogram_kernel(
    count_ref, codes_ref, low_ref, high_ref, out_ref, split_ref, both_ref, hist_ref, chosen_ref
):
    out_ref[...] = jnp.zeros_like(out_ref)

    @pl.when(count_ref[0] <= FEW)
    def _():
        unpack_codes(codes_ref, split_ref, FEW)
        both_ref[: HEADS // 2] = low_ref[...]
        both_ref[HEADS // 2 :] = high_ref[...]
        hist_ref[...] = jnp.zeros_like(hist_ref)
        add_histogram(split_ref, both_ref, hist_ref, chosen_ref, FEW)
        take_histogram(hist_ref, out_ref)


def table_histogram(count, codes, low, high):
    tokens = codes.shape[1]
    hist_shape = (TABLES * BUCKETS, HEADS * HIST_ROWS)
    whole = lambda shape: pl.BlockSpec(shape, lambda i, c: (0,) * len(shape))
    return pl.pallas_call(
        histogram_kernel,
        grid_spec=pltpu.PrefetchScalarGridSpec(
            num_scalar_prefetch=1,
            grid=(1,),
            in_specs=[whole((FEW, tokens)), whole(low.shape), whole(high.shape)],
            out_specs=whole(hist_shape),
            scratch_shapes=[
                pltpu.VMEM((TABLES, FEW, tokens), jnp.int32),
                pltpu.VMEM((HEADS, FEW, tokens), BF),
                pltpu.VMEM((HIST_ROWS * hist_shape[0], hist_shape[1]), F32),
                pltpu.VMEM((HIST_ROWS * hist_shape[0], tokens), BF),
            ],
        ),
        out_shape=jax.ShapeDtypeStruct(hist_shape, F32),
        compiler_params=pltpu.CompilerParams(vmem_limit_bytes=VMEM_LIMIT),
        cost_estimate=pl.CostEstimate(
            flops=20_000_000_000, bytes_accessed=8_000_000, transcendentals=0
        ),
        name="table_histogram",
    )(count, codes, low, high)


def key_gradients_kernel(
    count_ref,
    dq_low_ref,
    dq_high_ref,
    dk_low_ref,
    dk_high_ref,
    dv_low_ref,
    dv_high_ref,
    wq_ref,
    wk_ref,
    wv_ref,
    pack_ref,
    x_ref,
    picked_ref,
    lent_ref,
    own_ref,
    gain_ref,
    both_ref,
):
    tokens = x_ref.shape[0]
    half = D // 2
    few = count_ref[0] <= FEW

    def unit(rows):
        rows = rows.astype(F32)
        return rows * lax.rsqrt(jnp.mean(rows * rows, -1, keepdims=True) + EPS)

    def product(low, high, weight_ref):
        return dot_nt(low, weight_ref[:, :half]) + dot_nt(high, weight_ref[:, half:])

    gain_ref[...] = jnp.zeros_like(gain_ref)
    own_ref[...] = product(dq_low_ref[...], dq_high_ref[...], wq_ref)

    @pl.loop(0, tokens // COLS)
    def _(block):
        rows = pl.ds(pl.multiple_of(block * COLS, COLS), COLS)
        gain_ref[0:1, :] += jnp.sum(own_ref[rows, :] * unit(x_ref[rows, :]), 0, keepdims=True)

    def spread(keys, step):
        @pl.loop(0, keys // step)
        def _(block):
            rows = pl.ds(pl.multiple_of(block * step, step), step)
            grads = product(dk_low_ref[rows, :], dk_high_ref[rows, :], wk_ref)
            grads = grads + product(dv_low_ref[rows, :], dv_high_ref[rows, :], wv_ref)
            gain_ref[0:1, :] += jnp.sum(grads * unit(picked_ref[rows, :]), 0, keepdims=True)
            high = grads.astype(BF)
            both_ref[0, rows, :] = high
            both_ref[1, rows, :] = (grads - high.astype(F32)).astype(BF)

        high = both_ref[0, 0:keys, :]
        chosen = pack_ref[0:tokens, 0:keys]
        own_ref[...] += dot_nn(chosen, high) + dot_nn(chosen, both_ref[1, 0:keys, :])
        lent_ref[...] = dot_nn(pack_ref[tokens:, 0:keys], high).astype(BF)

    pl.when(few)(lambda: spread(FEW, FEW))
    pl.when(jnp.logical_not(few))(lambda: spread(pack_ref.shape[1], COLS))


def key_gradients(count, low, high, weights, pack, x_block, picked_x):
    tokens = x_block.shape[0]
    keys = pack.shape[0]
    whole = lambda shape: pl.BlockSpec(shape, lambda i, c: (0, 0))
    weight = lambda at: pl.BlockSpec((D, D), lambda i, c: (0, at))
    shape = jax.ShapeDtypeStruct
    return pl.pallas_call(
        key_gradients_kernel,
        grid_spec=pltpu.PrefetchScalarGridSpec(
            num_scalar_prefetch=1,
            grid=(1,),
            in_specs=[
                whole((tokens, D // 2)),
                whole((tokens, D // 2)),
                whole((keys, D // 2)),
                whole((keys, D // 2)),
                whole((keys, D // 2)),
                whole((keys, D // 2)),
                weight(0),
                weight(1),
                weight(2),
                whole(pack.shape),
                whole((tokens, D)),
                whole((keys, D)),
            ],
            out_specs=[whole((keys - tokens, D)), whole((tokens, D)), whole((8, D))],
            scratch_shapes=[pltpu.VMEM((2, keys, D), BF)],
        ),
        out_shape=[
            shape((keys - tokens, D), BF),
            shape((tokens, D), F32),
            shape((8, D), F32),
        ],
        compiler_params=pltpu.CompilerParams(vmem_limit_bytes=VMEM_LIMIT),
        cost_estimate=pl.CostEstimate(
            flops=9_000_000_000, bytes_accessed=18_000_000, transcendentals=0
        ),
        name="key_gradients",
    )(count, low[0], high[0], low[1], high[1], low[2], high[2], weights, weights, weights, pack, x_block, picked_x)


def input_kernel(own_ref, owner_ref, returned_ref, x_ref, gain_ref, middle_ref, out_ref):
    grads = own_ref[...] + dot_nn(owner_ref[...], returned_ref[...])
    rows = x_ref[...].astype(F32)
    inverse = lax.rsqrt(jnp.mean(rows * rows, -1, keepdims=True) + EPS)
    unit = rows * inverse
    weighted = grads * gain_ref[0:1, :]
    inner = jnp.mean(weighted * unit, -1, keepdims=True)
    out_ref[...] = (middle_ref[...] + inverse * (weighted - unit * inner)).astype(BF)


def input_gradient(own, owner, returned, x_block, gain_one, grad_middle):
    tokens = own.shape[0]
    streamed = lambda width: pl.BlockSpec((COLS, width), lambda i: (i, 0))
    whole = lambda shape: pl.BlockSpec(shape, lambda i: (0, 0))
    return pl.pallas_call(
        input_kernel,
        grid=(tokens // COLS,),
        in_specs=[
            streamed(D),
            streamed(owner.shape[1]),
            whole(returned.shape),
            streamed(D),
            whole((8, D)),
            streamed(D),
        ],
        out_specs=streamed(D),
        out_shape=jax.ShapeDtypeStruct((tokens, D), BF),
        compiler_params=pltpu.CompilerParams(vmem_limit_bytes=VMEM_LIMIT),
        cost_estimate=pl.CostEstimate(
            flops=1_000_000_000, bytes_accessed=8_000_000, transcendentals=0
        ),
        name="input_gradient",
    )(own, owner, returned, x_block, gain_one, grad_middle)


def on_device(
    hidden_in,
    out_cotangent,
    query_weight,
    key_weight,
    value_weight,
    output_weight,
    attn_gain,
    relative_table,
    horiz_table,
    vert_table,
    ffn_gain,
    gate_weight,
    up_weight,
    down_weight,
    key_keep,
    halo_rows,
    relative_bucket,
    horiz_bucket,
    vert_bucket,
):
    tokens = hidden_in.shape[0]
    rows = gate_weight.shape[0]
    table_share = relative_table.shape[0]
    row_index = lax.axis_index("row")
    col_index = lax.axis_index("col")
    row_count = lax.axis_size("row")
    col_count = lax.axis_size("col")
    region = row_index * col_count + col_index
    device_count = row_count * col_count

    packed_weights = pack_shards(
        (query_weight, key_weight, value_weight, output_weight, gate_weight, up_weight),
        down_weight,
    )
    weights = lax.all_gather(packed_weights, ("row", "col"), axis=0, tiled=True)
    small = jnp.stack(
        [attn_gain, ffn_gain]
        + [jnp.pad(t, (0, rows - table_share)) for t in (relative_table, horiz_table, vert_table)],
        1,
    )
    small = after(jnp.pad(small, ((0, 0), (0, 128 - small.shape[1]))), packed_weights)
    small_gather = Gather(small, 0, True)

    def turn(gathers, *done):
        for gather in gathers:
            gather.land(*done)
        return [gather.send() for gather in gathers]

    sent = turn([small_gather])

    halo_rows, key_keep, x_early = after((halo_rows, key_keep, hidden_in), sent)
    own_lists = lax.dynamic_index_in_dim(halo_rows, region, 0, keepdims=False)
    rim = x_early[own_lists]
    sent = turn([small_gather], rim)
    rim = after(rim, sent)
    above, below = shifted(rim[0:2], "row")
    left, right = shifted(rim[2:4], "col")
    neighbours = jnp.stack([region - col_count, region + col_count, region - 1, region + 1])
    present = jnp.stack(
        [row_index > 0, row_index < row_count - 1, col_index > 0, col_index < col_count - 1]
    ).astype(jnp.int32)
    list_ids = jnp.array([1, 0, 3, 2], dtype=jnp.int32)
    clipped = jnp.clip(neighbours, 0, device_count - 1)
    their_lists = after(halo_rows, rim)[clipped, list_ids]
    halo_keep = key_keep[clipped[:, None] * tokens + their_lists] * present[:, None]
    own_keep = lax.dynamic_slice_in_dim(key_keep, region * tokens, tokens)
    key_mask = jnp.concatenate([own_keep, halo_keep.reshape(-1)])
    key_total = key_mask.shape[0]

    place = jnp.cumsum(key_mask) - 1
    count = place[-1:] + 1
    scalars = jnp.concatenate([count, region.reshape(1)])
    slots = jnp.arange(key_total, dtype=jnp.int32)
    pack = ((place[:, None] == slots) & (key_mask[:, None] > 0)).astype(BF)

    sent = turn([small_gather], pack)
    packed_by, relative_bucket = after((pack, relative_bucket), sent)
    found = [
        lax.dot_general(
            packed_by, bucket.astype(BF), (((0,), (1,)), ((), ())), preferred_element_type=F32
        ).astype(jnp.int32)
        for bucket in (relative_bucket, horiz_bucket, vert_bucket)
    ]
    found_vert = jnp.where(slots[:, None] < count, found[2], BUCKETS)
    codes = found[0] + found[1] * BUCKETS + found_vert * (BUCKETS * BUCKETS)

    sent = turn([small_gather], codes)
    packed_by, above = after((pack, above), sent, codes)
    x_keys = jnp.concatenate([hidden_in, above, below, left, right], 0)
    picked_x = dot_nn(packed_by.T, x_keys).astype(BF)
    turn([small_gather], picked_x)
    while small_gather.flight is not None:
        turn([small_gather])
    small_masks = [0]
    for stage in stages_of(0)[::-1]:
        small_masks = small_masks + [mask ^ mask_of(stage) for mask in small_masks]
    place_of = [0] * device_count
    for at, mask in enumerate(small_masks):
        place_of[mask] = at
    devices = jnp.arange(device_count, dtype=jnp.int32)
    small_all = small_gather.held[jnp.array(place_of, jnp.int32)[devices ^ region]]
    gain_attn, gain_ffn = [small_all[:, :, i].reshape(-1) for i in range(2)]
    table_rows = [
        small_all[:, :table_share, 2 + t].reshape(BUCKETS, HEADS).T for t in range(TABLES)
    ]
    table_lanes = jnp.pad(
        jnp.stack(table_rows).astype(F32), ((0, 0), (0, 0), (0, 128 - BUCKETS))
    )
    table_lanes = table_lanes.at[2, :, BUCKETS].set(masked_score).reshape(TABLES * HEADS, 128)
    gain_one = gain_attn.astype(F32)
    gain_two = jnp.broadcast_to(gain_ffn.astype(F32), (8, D))

    low_bias = layout_bias(codes, table_lanes, 0)
    high_bias = layout_bias(after(codes, low_bias), table_lanes, HEADS // 2)
    x_input = hidden_in.astype(F32)
    normed_one = norm_rows(x_input, gain_one).astype(BF)
    picked = norm_rows(picked_x.astype(F32), gain_one).astype(BF)
    owner_lists = own_lists.reshape(-1)
    owner = (jnp.arange(tokens, dtype=jnp.int32)[:, None] == owner_lists).astype(BF)
    x_sum = jnp.sum(x_input * x_input, -1, keepdims=True)
    lanes = jnp.arange(128, dtype=jnp.int32)
    keep = own_keep.astype(F32)[:, None] * jnp.where(lanes == 0, x_sum, 1.0)
    weights = after(weights, high_bias, normed_one, picked, owner, keep)
    queries, keys, values, mixed, lse, probs, x_middle, normed_two = attention_forward(
        scalars,
        normed_one,
        picked,
        weights,
        codes,
        table_lanes,
        (low_bias, high_bias),
        hidden_in,
        gain_two,
    )
    uneven = down_weight.shape[0] % 8 != 0 or rows * 256 != 8 * D
    down = weights[:, weights.shape[1] - gate_weight.shape[1] :].reshape(-1, D) if uneven else None
    (
        gate_sent,
        gate_kept,
        up_sent,
        up_kept,
        down_sent,
        down_kept,
        layer_out,
        grad_middle,
        grad_attn,
        ffn_small,
    ) = feed_forward(
        scalars, normed_two, out_cotangent, x_middle, gain_two, keep, weights, down
    )
    if down_weight.shape[0] % 8 != 0:
        down_kept, down_sent = reordered(down_kept, down_sent, scatter_masks(2), region)
    ffn_chains = [
        Scatter(gate_sent, gate_kept, 0),
        Scatter(up_sent, up_kept, 1),
        Scatter(down_sent, down_kept, 2),
    ]
    rounds = Rounds()
    rounds.chains += ffn_chains

    def backward(half, kind, grad_attn):
        return attention_backward(
            half,
            kind,
            scalars,
            grad_attn,
            weights,
            queries,
            keys,
            values,
            lse,
            probs,
            codes,
            table_lanes,
            normed_one,
            picked,
            mixed,
        )

    sent = rounds.send()
    low_half = backward(0, 2, after(grad_attn, sent))
    low_chain = Scatter(low_half[5], low_half[6], 2)
    rounds.land(low_half[0])
    rounds.chains.append(low_chain)
    sent = rounds.send()
    high_half = backward(1, 1, after(grad_attn, low_half[0], sent))
    high_chain = Scatter(high_half[5], high_half[6], 1)
    rounds.land(high_half[0])
    rounds.chains.append(high_chain)
    sent = rounds.send()
    short_hist = table_histogram(
        scalars, after(codes, high_half[0], sent), low_half[3], high_half[3]
    )
    sent = rounds.turn(short_hist)
    lent, own_grads, attn_gain_part = key_gradients(
        scalars,
        low_half[:3],
        high_half[:3],
        weights,
        after(pack, short_hist, sent),
        hidden_in,
        picked_x,
    )
    hist = short_hist + jnp.concatenate([low_half[4], high_half[4]], 1)
    grad_table = jnp.sum(hist.reshape(TABLES * BUCKETS, HEADS, HIST_ROWS), -1)
    small_part = jnp.concatenate(
        [
            ffn_small[1, :128],
            ffn_small[0],
            attn_gain_part[0],
            grad_table.reshape(-1),
        ]
    ).reshape(-1, 128)
    small_rows = small_part.shape[0]
    small_part = jnp.pad(small_part, ((0, 128 - small_rows), (0, 0)))
    landed = rounds.land(lent)
    small_parts = lax.all_gather(after(small_part, landed), ("row", "col"), axis=0, tiled=True)
    sent = rounds.send()
    lent = after(lent, sent).reshape(4, -1, D)
    back_above, back_below = shifted(lent[0:2], "row")
    back_left, back_right = shifted(lent[2:4], "col")
    returned = jnp.concatenate([back_above, back_below, back_left, back_right], 0)
    landed = rounds.land()
    sent = rounds.send()
    input_grad = input_gradient(
        own_grads,
        owner,
        after(returned, landed, sent),
        hidden_in,
        jnp.broadcast_to(gain_one, (8, D)),
        grad_middle,
    )
    rounds.turn(input_grad)
    while rounds.chains:
        rounds.turn()
    summed = jnp.sum(small_parts.reshape(device_count, 128, 128)[:, :small_rows], 0).reshape(-1)

    residual_rms = jnp.sqrt(summed[:3] / (summed[3] * D))
    own_part = lambda at, size: lax.dynamic_slice_in_dim(summed, at + region * size, size)
    ffn_gain_grad = own_part(128, rows)
    attn_gain_grad = own_part(128 + D, rows)
    table_at = 128 + 2 * D
    table_grads = [own_part(table_at + t * BUCKETS * HEADS, table_share) for t in range(TABLES)]
    gate_grad, up_grad, down_grad = [
        total[0] for total in piece_sums([[chain] for chain in ffn_chains], False, F32)
    ]
    sides = [
        total[0] for total in piece_sums([[low_chain], [high_chain]], False, F32)
    ]
    width = D // 2
    query_grad, key_grad, value_grad, output_grad = [
        jnp.concatenate([side[:, i * width : (i + 1) * width] for side in sides], 1)
        for i in range(4)
    ]
    return (
        layer_out,
        input_grad,
        query_grad,
        key_grad,
        value_grad,
        output_grad,
        attn_gain_grad,
        table_grads[0],
        table_grads[1],
        table_grads[2],
        ffn_gain_grad,
        gate_grad,
        up_grad,
        down_grad,
        residual_rms,
    )


def solution(mesh):
    split = P(("row", "col"), None)
    line = P(("row", "col"))
    return jax.shard_map(
        on_device,
        mesh=mesh,
        in_specs=(split,) * 6 + (line,) * 5 + (split,) * 3 + (P(), P()) + (split,) * 3,
        out_specs=(split,) * 6 + (line,) * 5 + (split,) * 3 + (P(),),
        check_vma=False,
    )
```

```python
import functools

import jax
import jax.numpy as jnp
from jax import lax
from jax.experimental import pallas as pl
from jax.experimental.pallas import tpu as pltpu
from jax.sharding import PartitionSpec as P

D = 1024
HEADS = 16
HEAD_DIM = 64
BUCKETS = 32
TABLES = 3

EPS = 1e-06
masked_score = -1e30
FEW = 384
COLS = 128
ROWS = 64
GROUP = 4
WIDE = GROUP * HEAD_DIM
HIST_ROWS = 16
FF_TILE = 256
VMEM_LIMIT = 56 * 1024 * 1024
BF = jnp.bfloat16
F32 = jnp.float32


def shifted(block, axis):
    count = lax.axis_size(axis)
    forward = [(i, i + 1) for i in range(count - 1)]
    backward = [(target, source) for source, target in forward]
    return (
        lax.ppermute(block[1], axis, forward),
        lax.ppermute(block[0], axis, backward),
    )


def norm_rows(values, gain_row):
    return values * lax.rsqrt(jnp.mean(values * values, -1, keepdims=True) + EPS) * gain_row


def stages_of(kind):
    row_bits = [("row", bit) for bit in range(lax.axis_size("row").bit_length() - 1)]
    col_bits = [("col", bit) for bit in range(lax.axis_size("col").bit_length() - 1)]
    if kind == 0:
        return row_bits[:1] + col_bits + row_bits[1:]
    if kind == 1:
        return row_bits[:1] + col_bits[::-1] + row_bits[1:]
    if kind == 2:
        return row_bits[:2] + col_bits[:1] + row_bits[2:] + col_bits[1:]
    return row_bits[:2] + col_bits[::-1] + row_bits[2:]


def mask_of(stage):
    axis, bit = stage
    return (lax.axis_size("col") if axis == "row" else 1) << bit


def scatter_masks(kind):
    masks = [0]
    for stage in stages_of(kind)[::-1]:
        masks = masks + [mask ^ mask_of(stage) for mask in masks]
    return tuple(masks)


def gather_masks(kind):
    masks = [0]
    for stage in stages_of(kind)[:0:-1]:
        masks = masks + [mask ^ mask_of(stage) for mask in masks]
    return tuple(masks), mask_of(("row", 0))


def exchange(values, stage):
    axis, bit = stage
    pairs = [(i, i ^ (1 << bit)) for i in range(lax.axis_size(axis))]
    return lax.ppermute(values, axis, pairs)


def after(values, *earlier):
    return lax.optimization_barrier((values, earlier))[0]


class Gather:
    def __init__(self, shard, kind, both=False):
        self.held = shard[None]
        self.stages = stages_of(kind)[::-1] if both else stages_of(kind)[:0:-1]
        self.flight = None

    def send(self):
        if self.stages:
            self.flight = exchange(self.held, self.stages.pop(0))
        return self.held

    def land(self, *done):
        if self.flight is not None:
            if done:
                self.flight = after(self.flight, *done)
            self.held = jnp.concatenate([self.held, self.flight], 0)
            self.flight = None


class Scatter:
    def __init__(self, sent, kept, kind):
        self.stages = stages_of(kind)
        self.first = sent
        self.parts = [(kept, 0)]
        self.pieces, self.rows, self.width = sent.shape


class Rounds:
    def __init__(self):
        self.chains = []
        self.flights = []

    def land(self, *done):
        landed = [flight for chains, flight in self.flights]
        for chains, flight in self.flights:
            if done:
                flight = after(flight, *done)
            for number, chain in enumerate(chains):
                chain.parts.append((flight, number * chain.width))
        self.flights = []
        self.chains = [chain for chain in self.chains if chain.stages]
        return landed

    def send(self):
        sums, firsts = {}, []
        for chain in self.chains:
            stage = chain.stages.pop(0)
            if chain.first is not None:
                firsts.append(([chain], stage, chain.first))
                chain.first = None
            else:
                chain.pieces //= 2
                alike = (stage, chain.pieces, chain.rows, chain.width)
                sums.setdefault(alike, []).append(chain)
        sent = firsts
        if sums:
            values = piece_sums(list(sums.values()), True, BF)
            sent = sent + [
                (chains, alike[0], value)
                for (alike, chains), value in zip(sums.items(), values)
            ]
        for chains, stage, value in sent:
            self.flights.append((chains, exchange(value, stage)))
        return [value for chains, stage, value in sent]

    def turn(self, *done):
        self.land(*done)
        return self.send()


def sum_kernel(*refs, shares):
    refs = list(refs)
    outputs = refs[len(refs) - len(shares) :]
    for out_ref, (counts, width) in zip(outputs, shares):
        for number, count in enumerate(counts):
            total = refs.pop(0)[...].astype(F32)
            for _ in range(count - 1):
                total = total + refs.pop(0)[...].astype(F32)
            out_ref[:, :, number * width : (number + 1) * width] = total.astype(out_ref.dtype)


def piece_sums(groups, upper, dtype):
    steps = min([4] + [chains[0].pieces for chains in groups]) if upper else 1
    arrays, in_specs, out_specs, out_shape, shares = [], [], [], [], []
    for chains in groups:
        pieces, rows, width = chains[0].pieces, chains[0].rows, chains[0].width
        block = pieces // steps if upper else 1
        for chain in chains:
            for array, column in chain.parts:
                arrays.append(array)
                place = lambda i, lane=column // width: (steps + i if upper else 0, 0, lane)
                in_specs.append(pl.BlockSpec((block, rows, width), place))
        total = len(chains) * width
        out_specs.append(pl.BlockSpec((block, rows, total), lambda i: (i, 0, 0)))
        out_shape.append(jax.ShapeDtypeStruct((block * steps, rows, total), dtype))
        shares.append(([len(chain.parts) for chain in chains], width))
    moved = sum(2 * spec.block_shape[0] * spec.block_shape[1] * spec.block_shape[2] * steps for spec in in_specs)
    return pl.pallas_call(
        functools.partial(sum_kernel, shares=shares),
        grid=(steps,),
        in_specs=in_specs,
        out_specs=out_specs,
        out_shape=out_shape,
        compiler_params=pltpu.CompilerParams(vmem_limit_bytes=VMEM_LIMIT),
        cost_estimate=pl.CostEstimate(flops=moved, bytes_accessed=2 * moved, transcendentals=0),
        name="piece_sums",
    )(*arrays)


def dot_nn(left, right):
    return lax.dot_general(left, right, (((1,), (0,)), ((), ())), preferred_element_type=F32)


def dot_nt(left, right):
    return lax.dot_general(left, right, (((1,), (1,)), ((), ())), preferred_element_type=F32)


def dot_tn(left, right):
    return lax.dot_general(left, right, (((0,), (0,)), ((), ())), preferred_element_type=F32)


def pack_kernel(*refs):
    *sources, down_ref, out_ref = refs
    at = 0
    for source_ref in sources:
        width = source_ref.shape[1]
        out_ref[:, at : at + width] = source_ref[...]
        at += width
    down = down_ref[...].astype(F32)
    for b in range(down.shape[0] // 8):
        blocks = [down[8 * b : 8 * b + 8, a * 256 : (a + 1) * 256] for a in range(D // 256)]
        out_ref[:, at + b * 256 : at + (b + 1) * 256] = jnp.concatenate(blocks, 0).astype(BF)


def pack_shards(sources, down):
    rows = sources[0].shape[0]
    widths = [source.shape[1] for source in sources]
    total = sum(widths) + down.shape[0] * D // rows
    if down.shape[0] % 8 != 0 or rows * 256 != 8 * D:
        return jnp.concatenate(list(sources) + [down.reshape(rows, -1)], 1)
    return pl.pallas_call(
        pack_kernel,
        out_shape=jax.ShapeDtypeStruct((rows, total), BF),
        compiler_params=pltpu.CompilerParams(vmem_limit_bytes=VMEM_LIMIT),
        name="pack_shards",
    )(*sources, down)


LANE_GATHER = lax.GatherDimensionNumbers(
    offset_dims=(),
    collapsed_slice_dims=(1,),
    start_index_map=(1,),
    operand_batching_dims=(0,),
    start_indices_batching_dims=(0,),
)


def lane_gather(rows, index):
    return lax.gather(
        rows,
        index[:, :, None],
        LANE_GATHER,
        (1, 1),
        mode=lax.GatherScatterMode.PROMISE_IN_BOUNDS,
    )


def lanes_of(group):
    if isinstance(group, int):
        return pl.ds(group * WIDE, WIDE)
    return pl.ds(pl.multiple_of(group * WIDE, WIDE), WIDE)


def held_type(height):
    return BF if height % 16 == 0 else F32


def reordered(low, high, masks, device):
    place = [0] * len(masks)
    for at, mask in enumerate(masks):
        place[mask] = at
    index = jnp.array(place, jnp.int32)[jnp.array(masks, jnp.int32) ^ device]
    both = jnp.concatenate([low, high], 0)[index]
    return both[: len(masks) // 2], both[len(masks) // 2 :]


def placed(owner, height):
    start = owner * height
    if isinstance(start, int):
        return pl.ds(start, height)
    if height % 8 == 0:
        start = pl.multiple_of(start, height & -height)
    return pl.ds(start, height)


def join_pieces(own_ref, other_ref, joined_ref, device, masks, core_mask, at=0):
    height = own_ref.shape[1]
    lanes = slice(at, at + own_ref.shape[2])
    for p, mask in enumerate(masks):
        joined_ref[placed(device ^ mask, height), lanes] = own_ref[p].astype(joined_ref.dtype)
        joined_ref[placed(device ^ mask ^ core_mask, height), lanes] = other_ref[p].astype(
            joined_ref.dtype
        )


def part_pieces(joined_ref, sent_ref, kept_ref, device, masks, at=0, source=0):
    half, height, width = kept_ref.shape
    width = min(width, joined_ref.shape[1])
    lanes = slice(at, at + width)
    taken = slice(source, source + width)
    for p, mask in enumerate(masks):
        target_ref = kept_ref if p < half else sent_ref
        target_ref[p % half, :, lanes] = joined_ref[placed(device ^ mask, height), taken].astype(BF)


def head_masks():
    lane = lax.broadcasted_iota(jnp.int32, (1, WIDE), 1) >> 6
    return [(lane == h).astype(F32).astype(BF) for h in range(GROUP)]


def stack_heads(block, masks):
    return jnp.concatenate([block * mask for mask in masks], 0)


def unpack_codes(codes_ref, split_ref, keys):
    code = codes_ref[:keys, :]
    split_ref[0, :keys, :] = code & 31
    split_ref[1, :keys, :] = (code >> 5) & 31
    split_ref[2, :keys, :] = code >> 10


def bias_of(split_ref, table_ref, head, keys):
    spread = [
        jnp.broadcast_to(table_ref[pl.ds(t * HEADS + head, 1), :], (keys, COLS))
        for t in range(TABLES)
    ]
    found = [lane_gather(spread[t], split_ref[t, :keys, :]) for t in range(TABLES)]
    return found[0] + found[1] + found[2]


def bias_kernel(codes_ref, table_ref, bias_ref, split_ref, *, first_head):
    unpack_codes(codes_ref, split_ref, FEW)

    @pl.loop(0, bias_ref.shape[0])
    def _(head):
        bias_ref[head] = bias_of(split_ref, table_ref, first_head + head, FEW)


def layout_bias(codes, table_lanes, first_head):
    tokens = codes.shape[1]
    return pl.pallas_call(
        functools.partial(bias_kernel, first_head=first_head),
        grid=(tokens // COLS,),
        in_specs=[
            pl.BlockSpec((FEW, COLS), lambda i: (0, i)),
            pl.BlockSpec(table_lanes.shape, lambda i: (0, 0)),
        ],
        out_specs=pl.BlockSpec((HEADS // 2, FEW, COLS), lambda i: (0, 0, i)),
        out_shape=jax.ShapeDtypeStruct((HEADS // 2, FEW, tokens), F32),
        scratch_shapes=[pltpu.VMEM((TABLES, FEW, COLS), jnp.int32)],
        compiler_params=pltpu.CompilerParams(vmem_limit_bytes=VMEM_LIMIT),
        cost_estimate=pl.CostEstimate(
            flops=16_000_000_000, bytes_accessed=7_000_000, transcendentals=0
        ),
        name="layout_bias",
    )(codes, table_lanes)


def each_group(run, groups, short):
    if short:
        for group in range(groups):
            run(group)
    else:
        lax.fori_loop(0, groups, lambda group, carry: (run(group), carry)[1], 0)


def own_blocks(turned):
    return jnp.concatenate(
        [
            turned[h * HEAD_DIM : (h + 1) * HEAD_DIM, h * COLS : (h + 1) * COLS]
            for h in range(GROUP)
        ],
        0,
    )


def attend_kernel(
    count_ref,
    normed_ref,
    picked_ref,
    wq_ref,
    wk_ref,
    wv_ref,
    wo_ref,
    codes_ref,
    table_ref,
    low_bias_ref,
    high_bias_ref,
    x_ref,
    gain_ref,
    q_ref,
    k_ref,
    v_ref,
    mixed_ref,
    lse_ref,
    prob_ref,
    mid_ref,
    normed_two_ref,
    split_ref,
    turned_ref,
    attended_ref,
):
    step = pl.program_id(0)
    few = count_ref[0] <= FEW
    total_keys = picked_ref.shape[0]

    def project(rows):
        picked = picked_ref[rows, :]
        k_ref[rows, :] = dot_nn(picked, wk_ref[...]).astype(BF)
        values = dot_nn(picked, wv_ref[...]).astype(BF)
        v_ref[rows, :] = values
        turned_ref[:, rows] = values.T

    @pl.when(step == 0)
    def _():
        q_ref[...] = dot_nn(normed_ref[...], wq_ref[...]).astype(BF)

    @pl.when(jnp.logical_and(step == 0, few))
    def _():
        project(pl.ds(0, FEW))

    @pl.when(jnp.logical_and(step == 0, jnp.logical_not(few)))
    def _():
        @pl.loop(0, total_keys // 256)
        def _(block):
            project(pl.ds(pl.multiple_of(block * 256, 256), 256))

    here = pl.ds(pl.multiple_of(step * COLS, COLS), COLS)
    masks = head_masks()

    def attend(keys, short):
        def run(group):
            lanes = lanes_of(group)
            queries = stack_heads(q_ref[here, lanes], masks)
            scores = dot_nt(k_ref[0:keys, lanes], queries)
            pieces = []
            for h in range(GROUP):
                head = group * GROUP + h
                if short:
                    half = HEADS // 2
                    bias = low_bias_ref[head] if head < half else high_bias_ref[head - half]
                else:
                    bias = bias_of(split_ref, table_ref, head, keys)
                score = scores[:, h * COLS : (h + 1) * COLS] + bias
                top = jnp.max(score, 0, keepdims=True)
                grown = jnp.exp(score - top)
                total = jnp.sum(grown, 0, keepdims=True)
                prob = grown * (1.0 / total)
                if short:
                    prob_ref[head] = prob
                lse_ref[pl.ds(head, 1), :] = top + jnp.log(total)
                pieces.append(prob.astype(BF))
            mixed = dot_nn(turned_ref[lanes, 0:keys], jnp.concatenate(pieces, 1))
            mixed_ref[lanes, here] = own_blocks(mixed).astype(BF)

        if not short:
            unpack_codes(codes_ref, split_ref, keys)
        each_group(run, HEADS // GROUP, short)

    pl.when(few)(lambda: attend(FEW, True))
    pl.when(jnp.logical_not(few))(lambda: attend(total_keys, False))

    @pl.when(step == pl.num_programs(0) - 1)
    def _():
        gain = gain_ref[0:1, :]
        attended_ref[...] = mixed_ref[...].T

        @pl.loop(0, x_ref.shape[0] // 256)
        def _(block):
            rows = pl.ds(pl.multiple_of(block * 256, 256), 256)
            middle = x_ref[rows, :].astype(F32) + dot_nn(attended_ref[rows, :], wo_ref[...])
            mid_ref[rows, :] = middle
            normed_two_ref[rows, :] = norm_rows(middle, gain).astype(BF)


def attention_forward(count, normed, picked, weights, codes, table_lanes, bias, x_block, gain_two):
    tokens = normed.shape[0]
    keys = picked.shape[0]
    full = lambda shape: pl.BlockSpec(shape, lambda i, c: (0, 0))
    weight = lambda at: pl.BlockSpec((D, D), lambda i, c: (0, at), pipeline_mode=pl.Buffered(1))
    across = lambda height: pl.BlockSpec((height, COLS), lambda i, c: (0, i))
    headed = pl.BlockSpec((HEADS, FEW, COLS), lambda i, c: (0, 0, i))
    shape = jax.ShapeDtypeStruct
    return pl.pallas_call(
        attend_kernel,
        grid_spec=pltpu.PrefetchScalarGridSpec(
            num_scalar_prefetch=1,
            grid=(tokens // COLS,),
            in_specs=[
                full((tokens, D)),
                full((keys, D)),
                weight(0),
                weight(1),
                weight(2),
                weight(3),
                across(keys),
                full(table_lanes.shape),
                pl.BlockSpec((HEADS // 2, FEW, COLS), lambda i, c: (0, 0, i)),
                pl.BlockSpec((HEADS // 2, FEW, COLS), lambda i, c: (0, 0, i)),
                full((tokens, D)),
                full((8, D)),
            ],
            out_specs=[
                full((tokens, D)),
                full((keys, D)),
                full((keys, D)),
                full((D, tokens)),
                across(HEADS),
                headed,
                full((tokens, D)),
                full((tokens, D)),
            ],
            scratch_shapes=[
                pltpu.VMEM((TABLES, keys, COLS), jnp.int32),
                pltpu.VMEM((D, keys), BF),
                pltpu.VMEM((tokens, D), BF),
            ],
        ),
        out_shape=[
            shape((tokens, D), BF),
            shape((keys, D), BF),
            shape((keys, D), BF),
            shape((D, tokens), BF),
            shape((HEADS, tokens), F32),
            shape((HEADS, FEW, tokens), F32),
            shape((tokens, D), F32),
            shape((tokens, D), BF),
        ],
        compiler_params=pltpu.CompilerParams(vmem_limit_bytes=VMEM_LIMIT),
        cost_estimate=pl.CostEstimate(
            flops=20_000_000_000, bytes_accessed=50_000_000, transcendentals=3_000_000
        ),
        name="attention_forward",
    )(count, normed, picked, weights, weights, weights, weights, codes, table_lanes, *bias, x_block, gain_two)


def ffn_kernel(
    scalar_ref,
    normed_ref,
    out_cot_ref,
    mid_ref,
    gain_ref,
    keep_ref,
    gate_ref,
    up_ref,
    packed_ref,
    gate_sent_ref,
    gate_kept_ref,
    up_sent_ref,
    up_kept_ref,
    down_sent_ref,
    down_kept_ref,
    layer_ref,
    middle_grad_ref,
    attn_grad_ref,
    gain_grad_ref,
    turned_ref,
    branch_ref,
    back_ref,
    down_all_ref,
    gate_grad_ref,
    up_grad_ref,
    down_ref,
    landed_ref,
    landed_sem,
    *,
    scatter_order,
):
    step = pl.program_id(0)
    device = scalar_ref[1]
    down_device = device if down_kept_ref.shape[1] % 8 == 0 else 0

    @pl.when(step == 0)
    def _():
        if landed_ref.shape[0] == D:
            at = packed_ref.shape[1] - landed_ref.shape[1]
            source_ref = packed_ref.at[:, at:]
        else:
            source_ref = packed_ref
        copy = pltpu.make_async_copy(source_ref, landed_ref, landed_sem)
        copy.start()
        turned_ref[...] = normed_ref[...].T
        copy.wait()
        if landed_ref.shape[0] != D:
            down_all_ref[...] = landed_ref[...].astype(F32)
        else:
            height = landed_ref.shape[1] // 32
            for d in range(D // 32):
                for b in range(height // 8):
                    block = landed_ref[d * 32 : (d + 1) * 32, b * 256 : (b + 1) * 256].astype(F32)
                    rows = slice(d * height + 8 * b, d * height + 8 * b + 8)
                    for a in range(D // 256):
                        lanes = slice(a * 256, (a + 1) * 256)
                        down_all_ref[rows, lanes] = block[8 * a : 8 * a + 8]
        branch_ref[...] = jnp.zeros_like(branch_ref)
        back_ref[...] = jnp.zeros_like(back_ref)

    here = pl.ds(pl.multiple_of(step * FF_TILE, FF_TILE), FF_TILE)
    down_ref[...] = down_all_ref[here, :].astype(BF)

    normed = normed_ref[...]
    gate = dot_nn(normed, gate_ref[...])
    up = dot_nn(normed, up_ref[...])
    grad_act = dot_nt(out_cot_ref[...], down_ref[...])
    scale = 0.7978845608028654
    square = gate * gate
    bent = jnp.tanh(scale * (gate + 0.044715 * (square * gate)))
    half = 0.5 * (1.0 + bent)
    curved = gate * half
    slope = half + 0.5 * gate * (1.0 - bent * bent) * (scale * (1.0 + 0.134145 * square))
    activated = (curved * up).astype(BF)
    grad_gate = (grad_act * up * slope).astype(BF)
    grad_up = (grad_act * curved).astype(BF)
    branch_ref[...] += dot_nn(activated, down_ref[...])
    back_ref[...] += dot_nt(grad_gate, gate_ref[...]) + dot_nt(grad_up, up_ref[...])
    gate_grad_ref[...] = dot_nn(turned_ref[...], grad_gate).astype(gate_grad_ref.dtype)
    part_pieces(gate_grad_ref, gate_sent_ref, gate_kept_ref, device, scatter_order[0])
    up_grad_ref[...] = dot_nn(turned_ref[...], grad_up).astype(up_grad_ref.dtype)
    part_pieces(up_grad_ref, up_sent_ref, up_kept_ref, device, scatter_order[1])
    down_all_ref[here, :] = dot_tn(activated, out_cot_ref[...])

    @pl.when(step == pl.num_programs(0) - 1)
    def _():
        part_pieces(
            down_all_ref, down_sent_ref, down_kept_ref, down_device, scatter_order[2]
        )
        gain = gain_ref[0:1, :]
        gain_grad_ref[...] = jnp.zeros_like(gain_grad_ref)
        lane = lax.broadcasted_iota(jnp.int32, (ROWS, 128), 1)

        @pl.loop(0, mid_ref.shape[0] // ROWS)
        def _(block):
            rows = pl.ds(pl.multiple_of(block * ROWS, ROWS), ROWS)
            middle = mid_ref[rows, :]
            final = middle + branch_ref[rows, :]
            layer_ref[rows, :] = final.astype(BF)
            mid_sum = jnp.sum(middle * middle, -1, keepdims=True)
            final_sum = jnp.sum(final * final, -1, keepdims=True)
            sums = jnp.where(lane == 1, mid_sum, jnp.where(lane == 2, final_sum, 1.0))
            gain_grad_ref[1:2, :128] += jnp.sum(keep_ref[rows, :] * sums, 0, keepdims=True)
            inverse = lax.rsqrt(mid_sum * (1.0 / D) + EPS)
            unit = middle * inverse
            grad_normed = back_ref[rows, :]
            weighted = grad_normed * gain
            inner = jnp.mean(weighted * unit, -1, keepdims=True)
            grad_middle = out_cot_ref[rows, :].astype(F32) + inverse * (weighted - unit * inner)
            middle_grad_ref[rows, :] = grad_middle
            attn_grad_ref[rows, :] = grad_middle.astype(BF)
            gain_grad_ref[0:1, :] += jnp.sum(grad_normed * unit, 0, keepdims=True)


def feed_forward(scalars, normed_two, out_cot, middle, gain_two, keep, weights, down):
    tokens = normed_two.shape[0]
    ff = (weights.shape[1] - 4 * D) // 3
    half = lax.axis_size("row") * lax.axis_size("col") // 2
    down_rows = ff // (2 * half)
    rows = D // (2 * half)
    gate_at = 4 * D // FF_TILE
    up_at = gate_at + ff // FF_TILE
    once = pl.Buffered(1)
    full = lambda shape: pl.BlockSpec(shape, lambda i, c: (0,) * len(shape), pipeline_mode=once)
    tile = pl.BlockSpec((half, rows, FF_TILE), lambda i, c: (0, 0, i))
    shape = jax.ShapeDtypeStruct
    kernel = functools.partial(
        ffn_kernel,
        scatter_order=[scatter_masks(kind) for kind in range(3)],
    )
    return pl.pallas_call(
        kernel,
        grid_spec=pltpu.PrefetchScalarGridSpec(
            num_scalar_prefetch=1,
            grid=(ff // FF_TILE,),
            in_specs=[
                full((tokens, D)),
                full((tokens, D)),
                full((tokens, D)),
                full((8, D)),
                full((tokens, 128)),
                pl.BlockSpec((D, FF_TILE), lambda i, c: (0, gate_at + i)),
                pl.BlockSpec((D, FF_TILE), lambda i, c: (0, up_at + i)),
                pl.BlockSpec(memory_space=pl.ANY),
            ],
            out_specs=[
                tile,
                tile,
                tile,
                tile,
                full((half, down_rows, D)),
                full((half, down_rows, D)),
                full((tokens, D)),
                full((tokens, D)),
                full((tokens, D)),
                full((8, D)),
            ],
            scratch_shapes=[
                pltpu.VMEM((D, tokens), BF),
                pltpu.VMEM((tokens, D), F32),
                pltpu.VMEM((tokens, D), F32),
                pltpu.VMEM((ff, D), F32),
                pltpu.VMEM((D, FF_TILE), held_type(rows)),
                pltpu.VMEM((D, FF_TILE), held_type(rows)),
                pltpu.VMEM((FF_TILE, D), BF),
                pltpu.VMEM((ff, D) if down is not None else (D, ff), BF),
                pltpu.SemaphoreType.DMA(()),
            ],
        ),
        out_shape=[shape((half, rows, ff), BF)] * 4
        + [shape((half, down_rows, D), BF)] * 2
        + [
            shape((tokens, D), BF),
            shape((tokens, D), F32),
            shape((tokens, D), BF),
            shape((8, D), F32),
        ],
        compiler_params=pltpu.CompilerParams(vmem_limit_bytes=VMEM_LIMIT),
        cost_estimate=pl.CostEstimate(
            flops=27_000_000_000, bytes_accessed=44_000_000, transcendentals=1_500_000
        ),
        name="feed_forward",
    )(scalars, normed_two, out_cot, middle, gain_two, keep, weights, weights, weights if down is None else down)


def add_histogram(split_ref, grad_ref, hist_ref, chosen_ref, keys):
    heads = grad_ref.shape[0]
    cols = split_ref.shape[2]
    bucket = lax.broadcasted_iota(jnp.int32, (BUCKETS, cols), 0)

    @pl.loop(0, keys // HIST_ROWS)
    def _(block):
        base = pl.multiple_of(block * HIST_ROWS, HIST_ROWS)
        grads = grad_ref[:, pl.ds(base, HIST_ROWS), :]
        grads = grads.reshape(heads * HIST_ROWS, cols)
        for row in range(HIST_ROWS):
            for t in range(TABLES):
                at = (row * TABLES + t) * BUCKETS
                match = split_ref[t, pl.ds(base + row, 1), :] == bucket
                chosen_ref[at : at + BUCKETS, :] = match.astype(F32).astype(BF)
        hist_ref[...] += dot_nt(chosen_ref[...], grads)


def take_histogram(hist_ref, out_ref):
    height, width = out_ref.shape
    own = lax.broadcasted_iota(jnp.int32, (height, width), 1) & (HIST_ROWS - 1)
    total = jnp.zeros((height, width), F32)
    for row in range(HIST_ROWS):
        piece = hist_ref[row * height : (row + 1) * height, :]
        total = total + jnp.where(own == row, piece, 0.0)
    out_ref[...] = total


def backward_kernel(
    count_ref,
    attn_grad_ref,
    wo_ref,
    q_ref,
    k_ref,
    v_ref,
    lse_ref,
    prob_ref,
    codes_ref,
    table_ref,
    normed_ref,
    picked_ref,
    mixed_ref,
    dq_ref,
    dk_ref,
    dv_ref,
    grad_ref,
    hist_out_ref,
    sent_ref,
    kept_ref,
    back_ref,
    split_ref,
    long_grad_ref,
    turned_ref,
    dq_turned_ref,
    dk_sum_ref,
    dv_sum_ref,
    hist_ref,
    chosen_ref,
    joined_ref,
    *,
    first_head,
    scatter_order,
):
    step = pl.program_id(0)
    few = count_ref[0] <= FEW
    total_keys = k_ref.shape[0]
    heads = q_ref.shape[1] // HEAD_DIM

    @pl.when(step == 0)
    def _():
        back_ref[...] = dot_nt(attn_grad_ref[...], wo_ref[...]).astype(BF)
        dk_sum_ref[...] = jnp.zeros_like(dk_sum_ref)
        dv_sum_ref[...] = jnp.zeros_like(dv_sum_ref)
        hist_ref[...] = jnp.zeros_like(hist_ref)

    @pl.when(jnp.logical_and(step == 0, few))
    def _():
        turned_ref[:, 0:FEW] = k_ref[0:FEW, :].T

    @pl.when(jnp.logical_and(step == 0, jnp.logical_not(few)))
    def _():
        turned_ref[...] = k_ref[...].T

    here = pl.ds(pl.multiple_of(step * COLS, COLS), COLS)
    masks = head_masks()

    def turn_back(keys, short):
        def run(group):
            lanes = lanes_of(group)
            queries = stack_heads(q_ref[here, lanes], masks)
            grads = stack_heads(back_ref[here, lanes], masks)
            prob_grads = dot_nt(v_ref[0:keys, lanes], grads)
            if not short:
                scores = dot_nt(k_ref[0:keys, lanes], queries)
            score_grads = []
            probs = []
            for h in range(GROUP):
                cols = slice(h * COLS, (h + 1) * COLS)
                local = group * GROUP + h
                if short:
                    prob = prob_ref[local]
                else:
                    head = first_head + local
                    bias = bias_of(split_ref, table_ref, head, keys)
                    prob = jnp.exp(scores[:, cols] + bias - lse_ref[pl.ds(head, 1), :])
                weighted = prob * prob_grads[:, cols]
                inner = jnp.sum(weighted, 0, keepdims=True)
                score_grad = (weighted - prob * inner).astype(BF)
                if short:
                    grad_ref[local] = score_grad
                else:
                    long_grad_ref[local] = score_grad
                score_grads.append(score_grad)
                probs.append(prob.astype(BF))
            score_grads = jnp.concatenate(score_grads, 1)
            probs = jnp.concatenate(probs, 1)
            dq_turned_ref[lanes, here] = own_blocks(
                dot_nn(turned_ref[lanes, 0:keys], score_grads)
            ).astype(BF)
            dk_sum_ref[0:keys, lanes] += dot_nn(score_grads, queries)
            dv_sum_ref[0:keys, lanes] += dot_nn(probs, grads)

        if not short:
            unpack_codes(codes_ref, split_ref, keys)
        each_group(run, heads // GROUP, short)
        if not short:
            add_histogram(split_ref, long_grad_ref, hist_ref, chosen_ref, keys)

    pl.when(few)(lambda: turn_back(FEW, True))
    pl.when(jnp.logical_not(few))(lambda: turn_back(total_keys, False))

    def leave(number, gradient):
        joined_ref[...] = gradient.astype(joined_ref.dtype)
        at = number * joined_ref.shape[1]
        part_pieces(joined_ref, sent_ref, kept_ref, count_ref[1], scatter_order, at)

    def finish(keys):
        leave(1, dot_tn(picked_ref[0:keys, :], dk_ref[0:keys, :]))
        leave(2, dot_tn(picked_ref[0:keys, :], dv_ref[0:keys, :]))

    @pl.when(step == pl.num_programs(0) - 1)
    def _():
        dk_ref[...] = dk_sum_ref[...].astype(BF)
        dv_ref[...] = dv_sum_ref[...].astype(BF)
        dq_ref[...] = dq_turned_ref[...].T
        leave(0, dot_tn(normed_ref[...], dq_ref[...]))
        first = first_head * HEAD_DIM
        leave(3, dot_nn(mixed_ref[...], attn_grad_ref[:, first : first + heads * HEAD_DIM]))
        take_histogram(hist_ref, hist_out_ref)
        pl.when(few)(lambda: finish(FEW))
        pl.when(jnp.logical_not(few))(lambda: finish(total_keys))


def attention_backward(
    half,
    kind,
    count,
    attn_grad,
    weights,
    queries,
    keys,
    values,
    lse,
    probs,
    codes,
    table_lanes,
    normed,
    picked,
    mixed,
):
    tokens = queries.shape[0]
    device_count = lax.axis_size("row") * lax.axis_size("col")
    rows = D // device_count
    key_total = keys.shape[0]
    heads = HEADS // 2
    width = heads * HEAD_DIM
    full = lambda shape: pl.BlockSpec(shape, lambda i, c: (0, 0))
    side = lambda height: pl.BlockSpec((height, width), lambda i, c: (0, half))
    across = lambda height: pl.BlockSpec((height, COLS), lambda i, c: (0, i))
    shape = jax.ShapeDtypeStruct
    hist_shape = (TABLES * BUCKETS, heads * HIST_ROWS)
    return pl.pallas_call(
        functools.partial(
            backward_kernel,
            first_head=half * heads,
            scatter_order=scatter_masks(kind),
        ),
        grid_spec=pltpu.PrefetchScalarGridSpec(
            num_scalar_prefetch=1,
            grid=(tokens // COLS,),
            in_specs=[
                full((tokens, D)),
                pl.BlockSpec((width, D), lambda i, c: (half, 3)),
                side(tokens),
                side(key_total),
                side(key_total),
                across(HEADS),
                pl.BlockSpec((heads, FEW, COLS), lambda i, c: (half, 0, i)),
                across(key_total),
                full(table_lanes.shape),
                full((tokens, D)),
                full((key_total, D)),
                full((D, tokens)),
            ],
            out_specs=[
                full((tokens, width)),
                full((key_total, width)),
                full((key_total, width)),
                pl.BlockSpec((heads, FEW, COLS), lambda i, c: (0, 0, i)),
                full(hist_shape),
            ]
            + [
                pl.BlockSpec((device_count // 2, rows, 4 * width), lambda i, c: (0, 0, 0)),
            ]
            * 2,
            scratch_shapes=[
                pltpu.VMEM((tokens, width), BF),
                pltpu.VMEM((TABLES, key_total, COLS), jnp.int32),
                pltpu.VMEM((heads, key_total, COLS), BF),
                pltpu.VMEM((width, key_total), BF),
                pltpu.VMEM((width, tokens), BF),
                pltpu.VMEM((key_total, width), F32),
                pltpu.VMEM((key_total, width), F32),
                pltpu.VMEM((HIST_ROWS * hist_shape[0], hist_shape[1]), F32),
                pltpu.VMEM((HIST_ROWS * hist_shape[0], COLS), BF),
                pltpu.VMEM((D, width), held_type(rows)),
            ],
        ),
        out_shape=[
            shape((tokens, width), BF),
            shape((key_total, width), BF),
            shape((key_total, width), BF),
            shape((heads, FEW, tokens), BF),
            shape(hist_shape, F32),
        ]
        + [shape((device_count // 2, rows, 4 * width), BF)] * 2,
        compiler_params=pltpu.CompilerParams(vmem_limit_bytes=VMEM_LIMIT),
        cost_estimate=pl.CostEstimate(
            flops=15_000_000_000, bytes_accessed=30_000_000, transcendentals=0
        ),
        name="attention_backward",
    )(
        count,
        attn_grad,
        weights,
        queries,
        keys,
        values,
        lse,
        probs,
        codes,
        table_lanes,
        normed,
        picked,
        mixed,
    )


def onehot_kernel(codes_ref, out_ref, split_ref):
    code = codes_ref[...]
    split_ref[0] = code & 31
    split_ref[1] = (code >> 5) & 31
    split_ref[2] = code >> 10
    bucket = lax.broadcasted_iota(jnp.int32, (BUCKETS, code.shape[1]), 0)
    for row in range(HIST_ROWS):
        for t in range(TABLES):
            at = (row * TABLES + t) * BUCKETS
            match = split_ref[t, row : row + 1, :] == bucket
            out_ref[at : at + BUCKETS, :] = match.astype(F32).astype(BF)


def bucket_onehots(codes):
    tokens = codes.shape[1]
    height = HIST_ROWS * TABLES * BUCKETS
    return pl.pallas_call(
        onehot_kernel,
        grid=(FEW // HIST_ROWS,),
        in_specs=[pl.BlockSpec((HIST_ROWS, tokens), lambda i: (i, 0))],
        out_specs=pl.BlockSpec((height, tokens), lambda i: (i, 0)),
        out_shape=jax.ShapeDtypeStruct((FEW // HIST_ROWS * height, tokens), BF),
        scratch_shapes=[pltpu.VMEM((TABLES, HIST_ROWS, tokens), jnp.int32)],
        compiler_params=pltpu.CompilerParams(vmem_limit_bytes=VMEM_LIMIT),
        cost_estimate=pl.CostEstimate(
            flops=40_000_000, bytes_accessed=39_000_000, transcendentals=0
        ),
        name="bucket_onehots",
    )(codes)


def histogram_kernel(count_ref, chosen_ref, low_ref, high_ref, out_ref, hist_ref):
    step = pl.program_id(0)
    few = count_ref[0] <= FEW

    @pl.when(step == 0)
    def _():
        out_ref[...] = jnp.zeros_like(out_ref)
        hist_ref[...] = jnp.zeros_like(hist_ref)

    @pl.when(few)
    def _():
        rows = pl.ds(pl.multiple_of(step * HIST_ROWS, HIST_ROWS), HIST_ROWS)
        cols = low_ref.shape[2]
        grads = [part[:, rows, :].reshape(-1, cols) for part in (low_ref, high_ref)]
        hist_ref[...] += dot_nt(chosen_ref[...], jnp.concatenate(grads, 0))

    @pl.when(jnp.logical_and(few, step == pl.num_programs(0) - 1))
    def _():
        take_histogram(hist_ref, out_ref)


def table_histogram(count, onehots, low, high):
    tokens = onehots.shape[1]
    hist_shape = (TABLES * BUCKETS, HEADS * HIST_ROWS)
    height = HIST_ROWS * TABLES * BUCKETS
    once = pl.Buffered(1)
    whole = lambda shape: pl.BlockSpec(shape, lambda i, c: (0,) * len(shape), pipeline_mode=once)
    return pl.pallas_call(
        histogram_kernel,
        grid_spec=pltpu.PrefetchScalarGridSpec(
            num_scalar_prefetch=1,
            grid=(FEW // HIST_ROWS,),
            in_specs=[
                pl.BlockSpec((height, tokens), lambda i, c: (i, 0)),
                whole(low.shape),
                whole(high.shape),
            ],
            out_specs=whole(hist_shape),
            scratch_shapes=[pltpu.VMEM((height, hist_shape[1]), F32)],
        ),
        out_shape=jax.ShapeDtypeStruct(hist_shape, F32),
        compiler_params=pltpu.CompilerParams(vmem_limit_bytes=VMEM_LIMIT),
        cost_estimate=pl.CostEstimate(
            flops=10_000_000_000, bytes_accessed=45_000_000, transcendentals=0
        ),
        name="table_histogram",
    )(count, onehots, low, high)


def key_gradients_kernel(
    count_ref,
    dq_low_ref,
    dq_high_ref,
    dk_low_ref,
    dk_high_ref,
    dv_low_ref,
    dv_high_ref,
    wq_ref,
    wk_ref,
    wv_ref,
    pack_ref,
    x_ref,
    picked_ref,
    lent_ref,
    own_ref,
    gain_ref,
    both_ref,
):
    tokens = x_ref.shape[0]
    half = D // 2
    few = count_ref[0] <= FEW

    def unit(rows):
        rows = rows.astype(F32)
        return rows * lax.rsqrt(jnp.mean(rows * rows, -1, keepdims=True) + EPS)

    def product(low, high, weight_ref):
        return dot_nt(low, weight_ref[:, :half]) + dot_nt(high, weight_ref[:, half:])

    gain_ref[...] = jnp.zeros_like(gain_ref)
    own_ref[...] = product(dq_low_ref[...], dq_high_ref[...], wq_ref)

    @pl.loop(0, tokens // COLS)
    def _(block):
        rows = pl.ds(pl.multiple_of(block * COLS, COLS), COLS)
        gain_ref[0:1, :] += jnp.sum(own_ref[rows, :] * unit(x_ref[rows, :]), 0, keepdims=True)

    def spread(keys, step):
        @pl.loop(0, keys // step)
        def _(block):
            rows = pl.ds(pl.multiple_of(block * step, step), step)
            grads = product(dk_low_ref[rows, :], dk_high_ref[rows, :], wk_ref)
            grads = grads + product(dv_low_ref[rows, :], dv_high_ref[rows, :], wv_ref)
            gain_ref[0:1, :] += jnp.sum(grads * unit(picked_ref[rows, :]), 0, keepdims=True)
            high = grads.astype(BF)
            both_ref[0, rows, :] = high
            both_ref[1, rows, :] = (grads - high.astype(F32)).astype(BF)

        high = both_ref[0, 0:keys, :]
        chosen = pack_ref[0:tokens, 0:keys]
        own_ref[...] += dot_nn(chosen, high) + dot_nn(chosen, both_ref[1, 0:keys, :])
        lent_ref[...] = dot_nn(pack_ref[tokens:, 0:keys], high).astype(BF)

    pl.when(few)(lambda: spread(FEW, FEW))
    pl.when(jnp.logical_not(few))(lambda: spread(pack_ref.shape[1], COLS))


def key_gradients(count, low, high, weights, pack, x_block, picked_x):
    tokens = x_block.shape[0]
    keys = pack.shape[0]
    whole = lambda shape: pl.BlockSpec(shape, lambda i, c: (0, 0))
    weight = lambda at: pl.BlockSpec((D, D), lambda i, c: (0, at))
    shape = jax.ShapeDtypeStruct
    return pl.pallas_call(
        key_gradients_kernel,
        grid_spec=pltpu.PrefetchScalarGridSpec(
            num_scalar_prefetch=1,
            grid=(1,),
            in_specs=[
                whole((tokens, D // 2)),
                whole((tokens, D // 2)),
                whole((keys, D // 2)),
                whole((keys, D // 2)),
                whole((keys, D // 2)),
                whole((keys, D // 2)),
                weight(0),
                weight(1),
                weight(2),
                whole(pack.shape),
                whole((tokens, D)),
                whole((keys, D)),
            ],
            out_specs=[whole((keys - tokens, D)), whole((tokens, D)), whole((8, D))],
            scratch_shapes=[pltpu.VMEM((2, keys, D), BF)],
        ),
        out_shape=[
            shape((keys - tokens, D), BF),
            shape((tokens, D), F32),
            shape((8, D), F32),
        ],
        compiler_params=pltpu.CompilerParams(vmem_limit_bytes=VMEM_LIMIT),
        cost_estimate=pl.CostEstimate(
            flops=9_000_000_000, bytes_accessed=18_000_000, transcendentals=0
        ),
        name="key_gradients",
    )(count, low[0], high[0], low[1], high[1], low[2], high[2], weights, weights, weights, pack, x_block, picked_x)


def input_kernel(own_ref, owner_ref, returned_ref, x_ref, gain_ref, middle_ref, out_ref):
    grads = own_ref[...] + dot_nn(owner_ref[...], returned_ref[...])
    rows = x_ref[...].astype(F32)
    inverse = lax.rsqrt(jnp.mean(rows * rows, -1, keepdims=True) + EPS)
    unit = rows * inverse
    weighted = grads * gain_ref[0:1, :]
    inner = jnp.mean(weighted * unit, -1, keepdims=True)
    out_ref[...] = (middle_ref[...] + inverse * (weighted - unit * inner)).astype(BF)


def input_gradient(own, owner, returned, x_block, gain_one, grad_middle):
    tokens = own.shape[0]
    streamed = lambda width: pl.BlockSpec((COLS, width), lambda i: (i, 0))
    whole = lambda shape: pl.BlockSpec(shape, lambda i: (0, 0))
    return pl.pallas_call(
        input_kernel,
        grid=(tokens // COLS,),
        in_specs=[
            streamed(D),
            streamed(owner.shape[1]),
            whole(returned.shape),
            streamed(D),
            whole((8, D)),
            streamed(D),
        ],
        out_specs=streamed(D),
        out_shape=jax.ShapeDtypeStruct((tokens, D), BF),
        compiler_params=pltpu.CompilerParams(vmem_limit_bytes=VMEM_LIMIT),
        cost_estimate=pl.CostEstimate(
            flops=1_000_000_000, bytes_accessed=8_000_000, transcendentals=0
        ),
        name="input_gradient",
    )(own, owner, returned, x_block, gain_one, grad_middle)


def on_device(
    hidden_in,
    out_cotangent,
    query_weight,
    key_weight,
    value_weight,
    output_weight,
    attn_gain,
    relative_table,
    horiz_table,
    vert_table,
    ffn_gain,
    gate_weight,
    up_weight,
    down_weight,
    key_keep,
    halo_rows,
    relative_bucket,
    horiz_bucket,
    vert_bucket,
):
    tokens = hidden_in.shape[0]
    rows = gate_weight.shape[0]
    table_share = relative_table.shape[0]
    row_index = lax.axis_index("row")
    col_index = lax.axis_index("col")
    row_count = lax.axis_size("row")
    col_count = lax.axis_size("col")
    region = row_index * col_count + col_index
    device_count = row_count * col_count

    packed_weights = pack_shards(
        (query_weight, key_weight, value_weight, output_weight, gate_weight, up_weight),
        down_weight,
    )
    weights = lax.all_gather(packed_weights, ("row", "col"), axis=0, tiled=True)
    small = jnp.stack(
        [attn_gain, ffn_gain]
        + [jnp.pad(t, (0, rows - table_share)) for t in (relative_table, horiz_table, vert_table)],
        1,
    )
    small = after(jnp.pad(small, ((0, 0), (0, 128 - small.shape[1]))), packed_weights)
    small_gather = Gather(small, 0, True)

    def turn(gathers, *done):
        for gather in gathers:
            gather.land(*done)
        return [gather.send() for gather in gathers]

    sent = turn([small_gather])

    halo_rows, key_keep, x_early = after((halo_rows, key_keep, hidden_in), sent)
    own_lists = lax.dynamic_index_in_dim(halo_rows, region, 0, keepdims=False)
    rim = x_early[own_lists]
    sent = turn([small_gather], rim)
    rim = after(rim, sent)
    above, below = shifted(rim[0:2], "row")
    left, right = shifted(rim[2:4], "col")
    neighbours = jnp.stack([region - col_count, region + col_count, region - 1, region + 1])
    present = jnp.stack(
        [row_index > 0, row_index < row_count - 1, col_index > 0, col_index < col_count - 1]
    ).astype(jnp.int32)
    list_ids = jnp.array([1, 0, 3, 2], dtype=jnp.int32)
    clipped = jnp.clip(neighbours, 0, device_count - 1)
    their_lists = after(halo_rows, rim)[clipped, list_ids]
    halo_keep = key_keep[clipped[:, None] * tokens + their_lists] * present[:, None]
    own_keep = lax.dynamic_slice_in_dim(key_keep, region * tokens, tokens)
    key_mask = jnp.concatenate([own_keep, halo_keep.reshape(-1)])
    key_total = key_mask.shape[0]

    place = jnp.cumsum(key_mask) - 1
    count = place[-1:] + 1
    scalars = jnp.concatenate([count, region.reshape(1)])
    slots = jnp.arange(key_total, dtype=jnp.int32)
    pack = ((place[:, None] == slots) & (key_mask[:, None] > 0)).astype(BF)

    sent = turn([small_gather], pack)
    packed_by, relative_bucket = after((pack, relative_bucket), sent)
    found = [
        lax.dot_general(
            packed_by, bucket.astype(BF), (((0,), (1,)), ((), ())), preferred_element_type=F32
        ).astype(jnp.int32)
        for bucket in (relative_bucket, horiz_bucket, vert_bucket)
    ]
    found_vert = jnp.where(slots[:, None] < count, found[2], BUCKETS)
    codes = found[0] + found[1] * BUCKETS + found_vert * (BUCKETS * BUCKETS)

    sent = turn([small_gather], codes)
    packed_by, above = after((pack, above), sent, codes)
    x_keys = jnp.concatenate([hidden_in, above, below, left, right], 0)
    picked_x = dot_nn(packed_by.T, x_keys).astype(BF)
    turn([small_gather], picked_x)
    while small_gather.flight is not None:
        turn([small_gather])
    small_masks = [0]
    for stage in stages_of(0)[::-1]:
        small_masks = small_masks + [mask ^ mask_of(stage) for mask in small_masks]
    place_of = [0] * device_count
    for at, mask in enumerate(small_masks):
        place_of[mask] = at
    devices = jnp.arange(device_count, dtype=jnp.int32)
    small_all = small_gather.held[jnp.array(place_of, jnp.int32)[devices ^ region]]
    gain_attn, gain_ffn = [small_all[:, :, i].reshape(-1) for i in range(2)]
    table_rows = [
        small_all[:, :table_share, 2 + t].reshape(BUCKETS, HEADS).T for t in range(TABLES)
    ]
    table_lanes = jnp.pad(
        jnp.stack(table_rows).astype(F32), ((0, 0), (0, 0), (0, 128 - BUCKETS))
    )
    table_lanes = table_lanes.at[2, :, BUCKETS].set(masked_score).reshape(TABLES * HEADS, 128)
    gain_one = gain_attn.astype(F32)
    gain_two = jnp.broadcast_to(gain_ffn.astype(F32), (8, D))

    low_bias = layout_bias(codes, table_lanes, 0)
    high_bias = layout_bias(after(codes, low_bias), table_lanes, HEADS // 2)
    x_input = hidden_in.astype(F32)
    normed_one = norm_rows(x_input, gain_one).astype(BF)
    picked = norm_rows(picked_x.astype(F32), gain_one).astype(BF)
    owner_lists = own_lists.reshape(-1)
    owner = (jnp.arange(tokens, dtype=jnp.int32)[:, None] == owner_lists).astype(BF)
    x_sum = jnp.sum(x_input * x_input, -1, keepdims=True)
    lanes = jnp.arange(128, dtype=jnp.int32)
    keep = own_keep.astype(F32)[:, None] * jnp.where(lanes == 0, x_sum, 1.0)
    onehots = bucket_onehots(after(codes, high_bias))
    weights = after(weights, high_bias, normed_one, picked, owner, keep, onehots)
    queries, keys, values, mixed, lse, probs, x_middle, normed_two = attention_forward(
        scalars,
        normed_one,
        picked,
        weights,
        codes,
        table_lanes,
        (low_bias, high_bias),
        hidden_in,
        gain_two,
    )
    uneven = down_weight.shape[0] % 8 != 0 or rows * 256 != 8 * D
    down = weights[:, weights.shape[1] - gate_weight.shape[1] :].reshape(-1, D) if uneven else None
    (
        gate_sent,
        gate_kept,
        up_sent,
        up_kept,
        down_sent,
        down_kept,
        layer_out,
        grad_middle,
        grad_attn,
        ffn_small,
    ) = feed_forward(
        scalars, normed_two, out_cotangent, x_middle, gain_two, keep, weights, down
    )
    if down_weight.shape[0] % 8 != 0:
        down_kept, down_sent = reordered(down_kept, down_sent, scatter_masks(2), region)
    ffn_chains = [
        Scatter(gate_sent, gate_kept, 0),
        Scatter(up_sent, up_kept, 1),
        Scatter(down_sent, down_kept, 2),
    ]
    rounds = Rounds()
    rounds.chains += ffn_chains

    def backward(half, kind, grad_attn):
        return attention_backward(
            half,
            kind,
            scalars,
            grad_attn,
            weights,
            queries,
            keys,
            values,
            lse,
            probs,
            codes,
            table_lanes,
            normed_one,
            picked,
            mixed,
        )

    sent = rounds.send()
    low_half = backward(0, 3, after(grad_attn, sent))
    low_chain = Scatter(low_half[5], low_half[6], 3)
    rounds.land(low_half[0])
    rounds.chains.append(low_chain)
    sent = rounds.send()
    high_half = backward(1, 0, after(grad_attn, low_half[0], sent))
    high_chain = Scatter(high_half[5], high_half[6], 0)
    rounds.land(high_half[0])
    rounds.chains.append(high_chain)
    sent = rounds.send()
    short_hist = table_histogram(
        scalars, after(onehots, high_half[0], sent), low_half[3], high_half[3]
    )
    lent, own_grads, attn_gain_part = key_gradients(
        scalars,
        low_half[:3],
        high_half[:3],
        weights,
        after(pack, short_hist),
        hidden_in,
        picked_x,
    )
    hist = short_hist + jnp.concatenate([low_half[4], high_half[4]], 1)
    grad_table = jnp.sum(hist.reshape(TABLES * BUCKETS, HEADS, HIST_ROWS), -1)
    small_part = jnp.concatenate(
        [
            ffn_small[1, :128],
            ffn_small[0],
            attn_gain_part[0],
            grad_table.reshape(-1),
        ]
    ).reshape(-1, 128)
    small_rows = small_part.shape[0]
    small_part = jnp.pad(small_part, ((0, 128 - small_rows), (0, 0)))
    landed = rounds.land(lent, short_hist)
    small_parts = lax.all_gather(after(small_part, landed), ("row", "col"), axis=0, tiled=True)
    sent = rounds.send()
    lent = after(lent, sent).reshape(4, -1, D)
    back_above, back_below = shifted(lent[0:2], "row")
    back_left, back_right = shifted(lent[2:4], "col")
    returned = jnp.concatenate([back_above, back_below, back_left, back_right], 0)
    landed = rounds.land()
    sent = rounds.send()
    input_grad = input_gradient(
        own_grads,
        owner,
        after(returned, landed, sent),
        hidden_in,
        jnp.broadcast_to(gain_one, (8, D)),
        grad_middle,
    )
    rounds.turn(input_grad)
    while rounds.chains:
        rounds.turn()
    summed = jnp.sum(small_parts.reshape(device_count, 128, 128)[:, :small_rows], 0).reshape(-1)

    residual_rms = jnp.sqrt(summed[:3] / (summed[3] * D))
    own_part = lambda at, size: lax.dynamic_slice_in_dim(summed, at + region * size, size)
    ffn_gain_grad = own_part(128, rows)
    attn_gain_grad = own_part(128 + D, rows)
    table_at = 128 + 2 * D
    table_grads = [own_part(table_at + t * BUCKETS * HEADS, table_share) for t in range(TABLES)]
    gate_grad, up_grad, down_grad = [
        total[0] for total in piece_sums([[chain] for chain in ffn_chains], False, F32)
    ]
    sides = [
        total[0] for total in piece_sums([[low_chain], [high_chain]], False, F32)
    ]
    width = D // 2
    query_grad, key_grad, value_grad, output_grad = [
        jnp.concatenate([side[:, i * width : (i + 1) * width] for side in sides], 1)
        for i in range(4)
    ]
    return (
        layer_out,
        input_grad,
        query_grad,
        key_grad,
        value_grad,
        output_grad,
        attn_gain_grad,
        table_grads[0],
        table_grads[1],
        table_grads[2],
        ffn_gain_grad,
        gate_grad,
        up_grad,
        down_grad,
        residual_rms,
    )


def solution(mesh):
    split = P(("row", "col"), None)
    line = P(("row", "col"))
    return jax.shard_map(
        on_device,
        mesh=mesh,
        in_specs=(split,) * 6 + (line,) * 5 + (split,) * 3 + (P(), P()) + (split,) * 3,
        out_specs=(split,) * 6 + (line,) * 5 + (split,) * 3 + (P(),),
        check_vma=False,
    )
```

```python
import functools

import jax
import jax.numpy as jnp
from jax import lax
from jax.experimental import pallas as pl
from jax.experimental.pallas import tpu as pltpu
from jax.sharding import PartitionSpec as P

D = 1024
HEADS = 16
HEAD_DIM = 64
BUCKETS = 32
TABLES = 3

EPS = 1e-06
masked_score = -1e30
FEW = 384
COLS = 128
ROWS = 64
GROUP = 4
WIDE = GROUP * HEAD_DIM
HIST_ROWS = 16
FF_TILE = 256
VMEM_LIMIT = 56 * 1024 * 1024
BF = jnp.bfloat16
F32 = jnp.float32


def shifted(block, axis):
    count = lax.axis_size(axis)
    forward = [(i, i + 1) for i in range(count - 1)]
    backward = [(target, source) for source, target in forward]
    return (
        lax.ppermute(block[1], axis, forward),
        lax.ppermute(block[0], axis, backward),
    )


def norm_rows(values, gain_row):
    return values * lax.rsqrt(jnp.mean(values * values, -1, keepdims=True) + EPS) * gain_row


def stages_of(kind):
    row_bits = [("row", bit) for bit in range(lax.axis_size("row").bit_length() - 1)]
    col_bits = [("col", bit) for bit in range(lax.axis_size("col").bit_length() - 1)]
    if kind == 0:
        return row_bits[:1] + col_bits + row_bits[1:]
    if kind == 1:
        return row_bits[:1] + col_bits[::-1] + row_bits[1:]
    if kind == 2:
        return row_bits[:2] + col_bits[:1] + row_bits[2:] + col_bits[1:]
    return row_bits[:2] + col_bits[::-1] + row_bits[2:]


def mask_of(stage):
    axis, bit = stage
    return (lax.axis_size("col") if axis == "row" else 1) << bit


def scatter_masks(kind):
    masks = [0]
    for stage in stages_of(kind)[::-1]:
        masks = masks + [mask ^ mask_of(stage) for mask in masks]
    return tuple(masks)


def gather_masks(kind):
    masks = [0]
    for stage in stages_of(kind)[:0:-1]:
        masks = masks + [mask ^ mask_of(stage) for mask in masks]
    return tuple(masks), mask_of(("row", 0))


def exchange(values, stage):
    axis, bit = stage
    pairs = [(i, i ^ (1 << bit)) for i in range(lax.axis_size(axis))]
    return lax.ppermute(values, axis, pairs)


def after(values, *earlier):
    return lax.optimization_barrier((values, earlier))[0]


class Gather:
    def __init__(self, shard, kind, both=False):
        self.held = shard[None]
        self.stages = stages_of(kind)[::-1] if both else stages_of(kind)[:0:-1]
        self.flight = None

    def send(self):
        if self.stages:
            self.flight = exchange(self.held, self.stages.pop(0))
        return self.held

    def land(self, *done):
        if self.flight is not None:
            if done:
                self.flight = after(self.flight, *done)
            self.held = jnp.concatenate([self.held, self.flight], 0)
            self.flight = None


class Scatter:
    def __init__(self, sent, kept, kind):
        self.stages = stages_of(kind)
        self.first = sent
        self.parts = [(kept, 0)]
        self.pieces, self.rows, self.width = sent.shape


class Rounds:
    def __init__(self):
        self.chains = []
        self.flights = []

    def land(self, *done):
        landed = [flight for chains, flight in self.flights]
        for chains, flight in self.flights:
            if done:
                flight = after(flight, *done)
            for number, chain in enumerate(chains):
                chain.parts.append((flight, number * chain.width))
        self.flights = []
        self.chains = [chain for chain in self.chains if chain.stages]
        return landed

    def land_with(self, values):
        flights, values = lax.optimization_barrier(
            ([flight for chains, flight in self.flights], values)
        )
        self.flights = [(chains, flight) for (chains, _), flight in zip(self.flights, flights)]
        self.land()
        return values

    def send(self):
        sums, firsts = {}, []
        for chain in self.chains:
            stage = chain.stages.pop(0)
            if chain.first is not None:
                firsts.append(([chain], stage, chain.first))
                chain.first = None
            else:
                chain.pieces //= 2
                alike = (stage, chain.pieces, chain.rows, chain.width)
                sums.setdefault(alike, []).append(chain)
        sent = firsts
        if sums:
            values = piece_sums(list(sums.values()), True, BF)
            sent = sent + [
                (chains, alike[0], value)
                for (alike, chains), value in zip(sums.items(), values)
            ]
        for chains, stage, value in sent:
            self.flights.append((chains, exchange(value, stage)))
        return [value for chains, stage, value in sent]

    def turn(self, *done):
        self.land(*done)
        return self.send()


def sum_kernel(*refs, shares):
    refs = list(refs)
    outputs = refs[len(refs) - len(shares) :]
    for out_ref, (counts, width) in zip(outputs, shares):
        for number, count in enumerate(counts):
            total = refs.pop(0)[...].astype(F32)
            for _ in range(count - 1):
                total = total + refs.pop(0)[...].astype(F32)
            out_ref[:, :, number * width : (number + 1) * width] = total.astype(out_ref.dtype)


def piece_sums(groups, upper, dtype):
    steps = min([4] + [chains[0].pieces for chains in groups]) if upper else 1
    arrays, in_specs, out_specs, out_shape, shares = [], [], [], [], []
    for chains in groups:
        pieces, rows, width = chains[0].pieces, chains[0].rows, chains[0].width
        block = pieces // steps if upper else 1
        for chain in chains:
            for array, column in chain.parts:
                arrays.append(array)
                place = lambda i, lane=column // width: (steps + i if upper else 0, 0, lane)
                in_specs.append(pl.BlockSpec((block, rows, width), place))
        total = len(chains) * width
        out_specs.append(pl.BlockSpec((block, rows, total), lambda i: (i, 0, 0)))
        out_shape.append(jax.ShapeDtypeStruct((block * steps, rows, total), dtype))
        shares.append(([len(chain.parts) for chain in chains], width))
    moved = sum(2 * spec.block_shape[0] * spec.block_shape[1] * spec.block_shape[2] * steps for spec in in_specs)
    return pl.pallas_call(
        functools.partial(sum_kernel, shares=shares),
        grid=(steps,),
        in_specs=in_specs,
        out_specs=out_specs,
        out_shape=out_shape,
        compiler_params=pltpu.CompilerParams(vmem_limit_bytes=VMEM_LIMIT),
        cost_estimate=pl.CostEstimate(flops=moved, bytes_accessed=2 * moved, transcendentals=0),
        name="piece_sums",
    )(*arrays)


def dot_nn(left, right):
    return lax.dot_general(left, right, (((1,), (0,)), ((), ())), preferred_element_type=F32)


def dot_nt(left, right):
    return lax.dot_general(left, right, (((1,), (1,)), ((), ())), preferred_element_type=F32)


def dot_tn(left, right):
    return lax.dot_general(left, right, (((0,), (0,)), ((), ())), preferred_element_type=F32)


def pack_kernel(*refs):
    *sources, down_ref, out_ref = refs
    at = 0
    for source_ref in sources:
        width = source_ref.shape[1]
        out_ref[:, at : at + width] = source_ref[...]
        at += width
    down = down_ref[...].astype(F32)
    for b in range(down.shape[0] // 8):
        blocks = [down[8 * b : 8 * b + 8, a * 256 : (a + 1) * 256] for a in range(D // 256)]
        out_ref[:, at + b * 256 : at + (b + 1) * 256] = jnp.concatenate(blocks, 0).astype(BF)


def pack_shards(sources, down):
    rows = sources[0].shape[0]
    widths = [source.shape[1] for source in sources]
    total = sum(widths) + down.shape[0] * D // rows
    if down.shape[0] % 8 != 0 or rows * 256 != 8 * D:
        return jnp.concatenate(list(sources) + [down.reshape(rows, -1)], 1)
    return pl.pallas_call(
        pack_kernel,
        out_shape=jax.ShapeDtypeStruct((rows, total), BF),
        compiler_params=pltpu.CompilerParams(vmem_limit_bytes=VMEM_LIMIT),
        name="pack_shards",
    )(*sources, down)


LANE_GATHER = lax.GatherDimensionNumbers(
    offset_dims=(),
    collapsed_slice_dims=(1,),
    start_index_map=(1,),
    operand_batching_dims=(0,),
    start_indices_batching_dims=(0,),
)


def lane_gather(rows, index):
    return lax.gather(
        rows,
        index[:, :, None],
        LANE_GATHER,
        (1, 1),
        mode=lax.GatherScatterMode.PROMISE_IN_BOUNDS,
    )


def lanes_of(group):
    if isinstance(group, int):
        return pl.ds(group * WIDE, WIDE)
    return pl.ds(pl.multiple_of(group * WIDE, WIDE), WIDE)


def held_type(height):
    return BF if height % 16 == 0 else F32


def reordered(low, high, masks, device):
    place = [0] * len(masks)
    for at, mask in enumerate(masks):
        place[mask] = at
    index = jnp.array(place, jnp.int32)[jnp.array(masks, jnp.int32) ^ device]
    both = jnp.concatenate([low, high], 0)[index]
    return both[: len(masks) // 2], both[len(masks) // 2 :]


def placed(owner, height):
    start = owner * height
    if isinstance(start, int):
        return pl.ds(start, height)
    if height % 8 == 0:
        start = pl.multiple_of(start, height & -height)
    return pl.ds(start, height)


def join_pieces(own_ref, other_ref, joined_ref, device, masks, core_mask, at=0):
    height = own_ref.shape[1]
    lanes = slice(at, at + own_ref.shape[2])
    for p, mask in enumerate(masks):
        joined_ref[placed(device ^ mask, height), lanes] = own_ref[p].astype(joined_ref.dtype)
        joined_ref[placed(device ^ mask ^ core_mask, height), lanes] = other_ref[p].astype(
            joined_ref.dtype
        )


def part_pieces(joined_ref, sent_ref, kept_ref, device, masks, at=0, source=0):
    half, height, width = kept_ref.shape
    width = min(width, joined_ref.shape[1])
    lanes = slice(at, at + width)
    taken = slice(source, source + width)
    for p, mask in enumerate(masks):
        target_ref = kept_ref if p < half else sent_ref
        target_ref[p % half, :, lanes] = joined_ref[placed(device ^ mask, height), taken].astype(BF)


def head_masks():
    lane = lax.broadcasted_iota(jnp.int32, (1, WIDE), 1) >> 6
    return [(lane == h).astype(F32).astype(BF) for h in range(GROUP)]


def stack_heads(block, masks):
    return jnp.concatenate([block * mask for mask in masks], 0)


def unpack_codes(codes_ref, split_ref, keys):
    code = codes_ref[:keys, :]
    split_ref[0, :keys, :] = code & 31
    split_ref[1, :keys, :] = (code >> 5) & 31
    split_ref[2, :keys, :] = code >> 10


def bias_of(split_ref, table_ref, head, keys):
    spread = [
        jnp.broadcast_to(table_ref[pl.ds(t * HEADS + head, 1), :], (keys, COLS))
        for t in range(TABLES)
    ]
    found = [lane_gather(spread[t], split_ref[t, :keys, :]) for t in range(TABLES)]
    return found[0] + found[1] + found[2]


def bias_kernel(codes_ref, table_ref, bias_ref, split_ref, *, first_head):
    unpack_codes(codes_ref, split_ref, FEW)

    @pl.loop(0, bias_ref.shape[0])
    def _(head):
        bias_ref[head] = bias_of(split_ref, table_ref, first_head + head, FEW)


def layout_bias(codes, table_lanes, first_head):
    tokens = codes.shape[1]
    return pl.pallas_call(
        functools.partial(bias_kernel, first_head=first_head),
        grid=(tokens // COLS,),
        in_specs=[
            pl.BlockSpec((FEW, COLS), lambda i: (0, i)),
            pl.BlockSpec(table_lanes.shape, lambda i: (0, 0)),
        ],
        out_specs=pl.BlockSpec((HEADS // 2, FEW, COLS), lambda i: (0, 0, i)),
        out_shape=jax.ShapeDtypeStruct((HEADS // 2, FEW, tokens), F32),
        scratch_shapes=[pltpu.VMEM((TABLES, FEW, COLS), jnp.int32)],
        compiler_params=pltpu.CompilerParams(vmem_limit_bytes=VMEM_LIMIT),
        cost_estimate=pl.CostEstimate(
            flops=16_000_000_000, bytes_accessed=7_000_000, transcendentals=0
        ),
        name="layout_bias",
    )(codes, table_lanes)


def each_group(run, groups, short):
    if short:
        for group in range(groups):
            run(group)
    else:
        lax.fori_loop(0, groups, lambda group, carry: (run(group), carry)[1], 0)


def own_blocks(turned):
    return jnp.concatenate(
        [
            turned[h * HEAD_DIM : (h + 1) * HEAD_DIM, h * COLS : (h + 1) * COLS]
            for h in range(GROUP)
        ],
        0,
    )


def attend_kernel(
    count_ref,
    normed_ref,
    picked_ref,
    wq_ref,
    wk_ref,
    wv_ref,
    wo_ref,
    codes_ref,
    table_ref,
    low_bias_ref,
    high_bias_ref,
    x_ref,
    gain_ref,
    q_ref,
    k_ref,
    v_ref,
    mixed_ref,
    lse_ref,
    prob_ref,
    mid_ref,
    normed_two_ref,
    split_ref,
    turned_ref,
    attended_ref,
):
    step = pl.program_id(0)
    few = count_ref[0] <= FEW
    total_keys = picked_ref.shape[0]

    def project(rows):
        picked = picked_ref[rows, :]
        k_ref[rows, :] = dot_nn(picked, wk_ref[...]).astype(BF)
        values = dot_nn(picked, wv_ref[...]).astype(BF)
        v_ref[rows, :] = values
        turned_ref[:, rows] = values.T

    @pl.when(step == 0)
    def _():
        q_ref[...] = dot_nn(normed_ref[...], wq_ref[...]).astype(BF)

    @pl.when(jnp.logical_and(step == 0, few))
    def _():
        project(pl.ds(0, FEW))

    @pl.when(jnp.logical_and(step == 0, jnp.logical_not(few)))
    def _():
        @pl.loop(0, total_keys // 256)
        def _(block):
            project(pl.ds(pl.multiple_of(block * 256, 256), 256))

    here = pl.ds(pl.multiple_of(step * COLS, COLS), COLS)
    masks = head_masks()

    def attend(keys, short):
        def run(group):
            lanes = lanes_of(group)
            queries = stack_heads(q_ref[here, lanes], masks)
            scores = dot_nt(k_ref[0:keys, lanes], queries)
            pieces = []
            for h in range(GROUP):
                head = group * GROUP + h
                if short:
                    half = HEADS // 2
                    bias = low_bias_ref[head] if head < half else high_bias_ref[head - half]
                else:
                    bias = bias_of(split_ref, table_ref, head, keys)
                score = scores[:, h * COLS : (h + 1) * COLS] + bias
                top = jnp.max(score, 0, keepdims=True)
                grown = jnp.exp(score - top)
                total = jnp.sum(grown, 0, keepdims=True)
                prob = grown * (1.0 / total)
                if short:
                    prob_ref[head] = prob
                lse_ref[pl.ds(head, 1), :] = top + jnp.log(total)
                pieces.append(prob.astype(BF))
            mixed = dot_nn(turned_ref[lanes, 0:keys], jnp.concatenate(pieces, 1))
            mixed_ref[lanes, here] = own_blocks(mixed).astype(BF)

        if not short:
            unpack_codes(codes_ref, split_ref, keys)
        each_group(run, HEADS // GROUP, short)

    pl.when(few)(lambda: attend(FEW, True))
    pl.when(jnp.logical_not(few))(lambda: attend(total_keys, False))

    @pl.when(step == pl.num_programs(0) - 1)
    def _():
        gain = gain_ref[0:1, :]
        attended_ref[...] = mixed_ref[...].T

        @pl.loop(0, x_ref.shape[0] // 256)
        def _(block):
            rows = pl.ds(pl.multiple_of(block * 256, 256), 256)
            middle = x_ref[rows, :].astype(F32) + dot_nn(attended_ref[rows, :], wo_ref[...])
            mid_ref[rows, :] = middle
            normed_two_ref[rows, :] = norm_rows(middle, gain).astype(BF)


def attention_forward(count, normed, picked, weights, codes, table_lanes, bias, x_block, gain_two):
    tokens = normed.shape[0]
    keys = picked.shape[0]
    full = lambda shape: pl.BlockSpec(shape, lambda i, c: (0, 0))
    weight = lambda at: pl.BlockSpec((D, D), lambda i, c: (0, at), pipeline_mode=pl.Buffered(1))
    across = lambda height: pl.BlockSpec((height, COLS), lambda i, c: (0, i))
    headed = pl.BlockSpec((HEADS, FEW, COLS), lambda i, c: (0, 0, i))
    shape = jax.ShapeDtypeStruct
    return pl.pallas_call(
        attend_kernel,
        grid_spec=pltpu.PrefetchScalarGridSpec(
            num_scalar_prefetch=1,
            grid=(tokens // COLS,),
            in_specs=[
                full((tokens, D)),
                full((keys, D)),
                weight(0),
                weight(1),
                weight(2),
                weight(3),
                across(keys),
                full(table_lanes.shape),
                pl.BlockSpec((HEADS // 2, FEW, COLS), lambda i, c: (0, 0, i)),
                pl.BlockSpec((HEADS // 2, FEW, COLS), lambda i, c: (0, 0, i)),
                full((tokens, D)),
                full((8, D)),
            ],
            out_specs=[
                full((tokens, D)),
                full((keys, D)),
                full((keys, D)),
                full((D, tokens)),
                across(HEADS),
                headed,
                full((tokens, D)),
                full((tokens, D)),
            ],
            scratch_shapes=[
                pltpu.VMEM((TABLES, keys, COLS), jnp.int32),
                pltpu.VMEM((D, keys), BF),
                pltpu.VMEM((tokens, D), BF),
            ],
        ),
        out_shape=[
            shape((tokens, D), BF),
            shape((keys, D), BF),
            shape((keys, D), BF),
            shape((D, tokens), BF),
            shape((HEADS, tokens), F32),
            shape((HEADS, FEW, tokens), F32),
            shape((tokens, D), F32),
            shape((tokens, D), BF),
        ],
        compiler_params=pltpu.CompilerParams(vmem_limit_bytes=VMEM_LIMIT),
        cost_estimate=pl.CostEstimate(
            flops=20_000_000_000, bytes_accessed=50_000_000, transcendentals=3_000_000
        ),
        name="attention_forward",
    )(count, normed, picked, weights, weights, weights, weights, codes, table_lanes, *bias, x_block, gain_two)


def ffn_kernel(
    scalar_ref,
    normed_ref,
    out_cot_ref,
    mid_ref,
    gain_ref,
    keep_ref,
    gate_ref,
    up_ref,
    packed_ref,
    gate_sent_ref,
    gate_kept_ref,
    up_sent_ref,
    up_kept_ref,
    down_sent_ref,
    down_kept_ref,
    layer_ref,
    middle_grad_ref,
    attn_grad_ref,
    gain_grad_ref,
    turned_ref,
    branch_ref,
    back_ref,
    down_all_ref,
    gate_grad_ref,
    up_grad_ref,
    down_ref,
    landed_ref,
    landed_sem,
    *,
    scatter_order,
):
    step = pl.program_id(0)
    device = scalar_ref[1]
    down_device = device if down_kept_ref.shape[1] % 8 == 0 else 0

    @pl.when(step == 0)
    def _():
        if landed_ref.shape[0] == D:
            at = packed_ref.shape[1] - landed_ref.shape[1]
            source_ref = packed_ref.at[:, at:]
        else:
            source_ref = packed_ref
        copy = pltpu.make_async_copy(source_ref, landed_ref, landed_sem)
        copy.start()
        turned_ref[...] = normed_ref[...].T
        copy.wait()
        if landed_ref.shape[0] != D:
            down_all_ref[...] = landed_ref[...].astype(F32)
        else:
            height = landed_ref.shape[1] // 32
            for d in range(D // 32):
                for b in range(height // 8):
                    block = landed_ref[d * 32 : (d + 1) * 32, b * 256 : (b + 1) * 256].astype(F32)
                    rows = slice(d * height + 8 * b, d * height + 8 * b + 8)
                    for a in range(D // 256):
                        lanes = slice(a * 256, (a + 1) * 256)
                        down_all_ref[rows, lanes] = block[8 * a : 8 * a + 8]
        branch_ref[...] = jnp.zeros_like(branch_ref)
        back_ref[...] = jnp.zeros_like(back_ref)

    here = pl.ds(pl.multiple_of(step * FF_TILE, FF_TILE), FF_TILE)
    down_ref[...] = down_all_ref[here, :].astype(BF)

    normed = normed_ref[...]
    gate = dot_nn(normed, gate_ref[...])
    up = dot_nn(normed, up_ref[...])
    grad_act = dot_nt(out_cot_ref[...], down_ref[...])
    scale = 0.7978845608028654
    square = gate * gate
    bent = jnp.tanh(scale * (gate + 0.044715 * (square * gate)))
    half = 0.5 * (1.0 + bent)
    curved = gate * half
    slope = half + 0.5 * gate * (1.0 - bent * bent) * (scale * (1.0 + 0.134145 * square))
    activated = (curved * up).astype(BF)
    grad_gate = (grad_act * up * slope).astype(BF)
    grad_up = (grad_act * curved).astype(BF)
    branch_ref[...] += dot_nn(activated, down_ref[...])
    back_ref[...] += dot_nt(grad_gate, gate_ref[...]) + dot_nt(grad_up, up_ref[...])
    gate_grad_ref[...] = dot_nn(turned_ref[...], grad_gate).astype(gate_grad_ref.dtype)
    part_pieces(gate_grad_ref, gate_sent_ref, gate_kept_ref, device, scatter_order[0])
    up_grad_ref[...] = dot_nn(turned_ref[...], grad_up).astype(up_grad_ref.dtype)
    part_pieces(up_grad_ref, up_sent_ref, up_kept_ref, device, scatter_order[1])
    down_all_ref[here, :] = dot_tn(activated, out_cot_ref[...])

    @pl.when(step == pl.num_programs(0) - 1)
    def _():
        part_pieces(
            down_all_ref, down_sent_ref, down_kept_ref, down_device, scatter_order[2]
        )
        gain = gain_ref[0:1, :]
        gain_grad_ref[...] = jnp.zeros_like(gain_grad_ref)
        lane = lax.broadcasted_iota(jnp.int32, (ROWS, 128), 1)

        @pl.loop(0, mid_ref.shape[0] // ROWS)
        def _(block):
            rows = pl.ds(pl.multiple_of(block * ROWS, ROWS), ROWS)
            middle = mid_ref[rows, :]
            final = middle + branch_ref[rows, :]
            layer_ref[rows, :] = final.astype(BF)
            mid_sum = jnp.sum(middle * middle, -1, keepdims=True)
            final_sum = jnp.sum(final * final, -1, keepdims=True)
            sums = jnp.where(lane == 1, mid_sum, jnp.where(lane == 2, final_sum, 1.0))
            gain_grad_ref[1:2, :128] += jnp.sum(keep_ref[rows, :] * sums, 0, keepdims=True)
            inverse = lax.rsqrt(mid_sum * (1.0 / D) + EPS)
            unit = middle * inverse
            grad_normed = back_ref[rows, :]
            weighted = grad_normed * gain
            inner = jnp.mean(weighted * unit, -1, keepdims=True)
            grad_middle = out_cot_ref[rows, :].astype(F32) + inverse * (weighted - unit * inner)
            middle_grad_ref[rows, :] = grad_middle
            attn_grad_ref[rows, :] = grad_middle.astype(BF)
            gain_grad_ref[0:1, :] += jnp.sum(grad_normed * unit, 0, keepdims=True)


def feed_forward(scalars, normed_two, out_cot, middle, gain_two, keep, weights, down):
    tokens = normed_two.shape[0]
    ff = (weights.shape[1] - 4 * D) // 3
    half = lax.axis_size("row") * lax.axis_size("col") // 2
    down_rows = ff // (2 * half)
    rows = D // (2 * half)
    gate_at = 4 * D // FF_TILE
    up_at = gate_at + ff // FF_TILE
    once = pl.Buffered(1)
    full = lambda shape: pl.BlockSpec(shape, lambda i, c: (0,) * len(shape), pipeline_mode=once)
    tile = pl.BlockSpec((half, rows, FF_TILE), lambda i, c: (0, 0, i))
    shape = jax.ShapeDtypeStruct
    kernel = functools.partial(
        ffn_kernel,
        scatter_order=[scatter_masks(kind) for kind in range(3)],
    )
    return pl.pallas_call(
        kernel,
        grid_spec=pltpu.PrefetchScalarGridSpec(
            num_scalar_prefetch=1,
            grid=(ff // FF_TILE,),
            in_specs=[
                full((tokens, D)),
                full((tokens, D)),
                full((tokens, D)),
                full((8, D)),
                full((tokens, 128)),
                pl.BlockSpec((D, FF_TILE), lambda i, c: (0, gate_at + i)),
                pl.BlockSpec((D, FF_TILE), lambda i, c: (0, up_at + i)),
                pl.BlockSpec(memory_space=pl.ANY),
            ],
            out_specs=[
                tile,
                tile,
                tile,
                tile,
                full((half, down_rows, D)),
                full((half, down_rows, D)),
                full((tokens, D)),
                full((tokens, D)),
                full((tokens, D)),
                full((8, D)),
            ],
            scratch_shapes=[
                pltpu.VMEM((D, tokens), BF),
                pltpu.VMEM((tokens, D), F32),
                pltpu.VMEM((tokens, D), F32),
                pltpu.VMEM((ff, D), F32),
                pltpu.VMEM((D, FF_TILE), held_type(rows)),
                pltpu.VMEM((D, FF_TILE), held_type(rows)),
                pltpu.VMEM((FF_TILE, D), BF),
                pltpu.VMEM((ff, D) if down is not None else (D, ff), BF),
                pltpu.SemaphoreType.DMA(()),
            ],
        ),
        out_shape=[shape((half, rows, ff), BF)] * 4
        + [shape((half, down_rows, D), BF)] * 2
        + [
            shape((tokens, D), BF),
            shape((tokens, D), F32),
            shape((tokens, D), BF),
            shape((8, D), F32),
        ],
        compiler_params=pltpu.CompilerParams(vmem_limit_bytes=VMEM_LIMIT),
        cost_estimate=pl.CostEstimate(
            flops=27_000_000_000, bytes_accessed=44_000_000, transcendentals=1_500_000
        ),
        name="feed_forward",
    )(scalars, normed_two, out_cot, middle, gain_two, keep, weights, weights, weights if down is None else down)


def add_histogram(split_ref, grad_ref, hist_ref, chosen_ref, keys):
    heads = grad_ref.shape[0]
    cols = split_ref.shape[2]
    bucket = lax.broadcasted_iota(jnp.int32, (BUCKETS, cols), 0)

    @pl.loop(0, keys // HIST_ROWS)
    def _(block):
        base = pl.multiple_of(block * HIST_ROWS, HIST_ROWS)
        grads = grad_ref[:, pl.ds(base, HIST_ROWS), :]
        grads = grads.reshape(heads * HIST_ROWS, cols)
        for row in range(HIST_ROWS):
            for t in range(TABLES):
                at = (row * TABLES + t) * BUCKETS
                match = split_ref[t, pl.ds(base + row, 1), :] == bucket
                chosen_ref[at : at + BUCKETS, :] = match.astype(F32).astype(BF)
        hist_ref[...] += dot_nt(chosen_ref[...], grads)


def take_histogram(hist_ref, out_ref):
    height, width = out_ref.shape
    own = lax.broadcasted_iota(jnp.int32, (height, width), 1) & (HIST_ROWS - 1)
    total = jnp.zeros((height, width), F32)
    for row in range(HIST_ROWS):
        piece = hist_ref[row * height : (row + 1) * height, :]
        total = total + jnp.where(own == row, piece, 0.0)
    out_ref[...] = total


def backward_kernel(
    count_ref,
    attn_grad_ref,
    wo_ref,
    q_ref,
    k_ref,
    v_ref,
    lse_ref,
    prob_ref,
    codes_ref,
    table_ref,
    normed_ref,
    picked_ref,
    mixed_ref,
    dq_ref,
    dk_ref,
    dv_ref,
    grad_ref,
    hist_out_ref,
    sent_ref,
    kept_ref,
    back_ref,
    split_ref,
    long_grad_ref,
    turned_ref,
    dq_turned_ref,
    dk_sum_ref,
    dv_sum_ref,
    hist_ref,
    chosen_ref,
    joined_ref,
    *,
    first_head,
    scatter_order,
):
    step = pl.program_id(0)
    few = count_ref[0] <= FEW
    total_keys = k_ref.shape[0]
    heads = q_ref.shape[1] // HEAD_DIM

    @pl.when(step == 0)
    def _():
        back_ref[...] = dot_nt(attn_grad_ref[...], wo_ref[...]).astype(BF)
        dk_sum_ref[...] = jnp.zeros_like(dk_sum_ref)
        dv_sum_ref[...] = jnp.zeros_like(dv_sum_ref)
        hist_ref[...] = jnp.zeros_like(hist_ref)

    @pl.when(jnp.logical_and(step == 0, few))
    def _():
        turned_ref[:, 0:FEW] = k_ref[0:FEW, :].T

    @pl.when(jnp.logical_and(step == 0, jnp.logical_not(few)))
    def _():
        turned_ref[...] = k_ref[...].T

    here = pl.ds(pl.multiple_of(step * COLS, COLS), COLS)
    masks = head_masks()

    def turn_back(keys, short):
        def run(group):
            lanes = lanes_of(group)
            queries = stack_heads(q_ref[here, lanes], masks)
            grads = stack_heads(back_ref[here, lanes], masks)
            prob_grads = dot_nt(v_ref[0:keys, lanes], grads)
            if not short:
                scores = dot_nt(k_ref[0:keys, lanes], queries)
            score_grads = []
            probs = []
            for h in range(GROUP):
                cols = slice(h * COLS, (h + 1) * COLS)
                local = group * GROUP + h
                if short:
                    prob = prob_ref[local]
                else:
                    head = first_head + local
                    bias = bias_of(split_ref, table_ref, head, keys)
                    prob = jnp.exp(scores[:, cols] + bias - lse_ref[pl.ds(head, 1), :])
                weighted = prob * prob_grads[:, cols]
                inner = jnp.sum(weighted, 0, keepdims=True)
                score_grad = (weighted - prob * inner).astype(BF)
                if short:
                    grad_ref[local] = score_grad
                else:
                    long_grad_ref[local] = score_grad
                score_grads.append(score_grad)
                probs.append(prob.astype(BF))
            score_grads = jnp.concatenate(score_grads, 1)
            probs = jnp.concatenate(probs, 1)
            dq_turned_ref[lanes, here] = own_blocks(
                dot_nn(turned_ref[lanes, 0:keys], score_grads)
            ).astype(BF)
            dk_sum_ref[0:keys, lanes] += dot_nn(score_grads, queries)
            dv_sum_ref[0:keys, lanes] += dot_nn(probs, grads)

        if not short:
            unpack_codes(codes_ref, split_ref, keys)
        each_group(run, heads // GROUP, short)
        if not short:
            add_histogram(split_ref, long_grad_ref, hist_ref, chosen_ref, keys)

    pl.when(few)(lambda: turn_back(FEW, True))
    pl.when(jnp.logical_not(few))(lambda: turn_back(total_keys, False))

    def leave(number, gradient):
        joined_ref[...] = gradient.astype(joined_ref.dtype)
        at = number * joined_ref.shape[1]
        part_pieces(joined_ref, sent_ref, kept_ref, count_ref[1], scatter_order, at)

    def finish(keys):
        leave(1, dot_tn(picked_ref[0:keys, :], dk_ref[0:keys, :]))
        leave(2, dot_tn(picked_ref[0:keys, :], dv_ref[0:keys, :]))

    @pl.when(step == pl.num_programs(0) - 1)
    def _():
        dk_ref[...] = dk_sum_ref[...].astype(BF)
        dv_ref[...] = dv_sum_ref[...].astype(BF)
        dq_ref[...] = dq_turned_ref[...].T
        leave(0, dot_tn(normed_ref[...], dq_ref[...]))
        first = first_head * HEAD_DIM
        leave(3, dot_nn(mixed_ref[...], attn_grad_ref[:, first : first + heads * HEAD_DIM]))
        take_histogram(hist_ref, hist_out_ref)
        pl.when(few)(lambda: finish(FEW))
        pl.when(jnp.logical_not(few))(lambda: finish(total_keys))


def attention_backward(
    half,
    kind,
    count,
    attn_grad,
    weights,
    queries,
    keys,
    values,
    lse,
    probs,
    codes,
    table_lanes,
    normed,
    picked,
    mixed,
):
    tokens = queries.shape[0]
    device_count = lax.axis_size("row") * lax.axis_size("col")
    rows = D // device_count
    key_total = keys.shape[0]
    heads = HEADS // 2
    width = heads * HEAD_DIM
    full = lambda shape: pl.BlockSpec(shape, lambda i, c: (0, 0))
    side = lambda height: pl.BlockSpec((height, width), lambda i, c: (0, half))
    across = lambda height: pl.BlockSpec((height, COLS), lambda i, c: (0, i))
    shape = jax.ShapeDtypeStruct
    hist_shape = (TABLES * BUCKETS, heads * HIST_ROWS)
    return pl.pallas_call(
        functools.partial(
            backward_kernel,
            first_head=half * heads,
            scatter_order=scatter_masks(kind),
        ),
        grid_spec=pltpu.PrefetchScalarGridSpec(
            num_scalar_prefetch=1,
            grid=(tokens // COLS,),
            in_specs=[
                full((tokens, D)),
                pl.BlockSpec((width, D), lambda i, c: (half, 3)),
                side(tokens),
                side(key_total),
                side(key_total),
                across(HEADS),
                pl.BlockSpec((heads, FEW, COLS), lambda i, c: (half, 0, i)),
                across(key_total),
                full(table_lanes.shape),
                full((tokens, D)),
                full((key_total, D)),
                full((D, tokens)),
            ],
            out_specs=[
                full((tokens, width)),
                full((key_total, width)),
                full((key_total, width)),
                pl.BlockSpec((heads, FEW, COLS), lambda i, c: (0, 0, i)),
                full(hist_shape),
            ]
            + [
                pl.BlockSpec((device_count // 2, rows, 4 * width), lambda i, c: (0, 0, 0)),
            ]
            * 2,
            scratch_shapes=[
                pltpu.VMEM((tokens, width), BF),
                pltpu.VMEM((TABLES, key_total, COLS), jnp.int32),
                pltpu.VMEM((heads, key_total, COLS), BF),
                pltpu.VMEM((width, key_total), BF),
                pltpu.VMEM((width, tokens), BF),
                pltpu.VMEM((key_total, width), F32),
                pltpu.VMEM((key_total, width), F32),
                pltpu.VMEM((HIST_ROWS * hist_shape[0], hist_shape[1]), F32),
                pltpu.VMEM((HIST_ROWS * hist_shape[0], COLS), BF),
                pltpu.VMEM((D, width), held_type(rows)),
            ],
        ),
        out_shape=[
            shape((tokens, width), BF),
            shape((key_total, width), BF),
            shape((key_total, width), BF),
            shape((heads, FEW, tokens), BF),
            shape(hist_shape, F32),
        ]
        + [shape((device_count // 2, rows, 4 * width), BF)] * 2,
        compiler_params=pltpu.CompilerParams(vmem_limit_bytes=VMEM_LIMIT),
        cost_estimate=pl.CostEstimate(
            flops=15_000_000_000, bytes_accessed=30_000_000, transcendentals=0
        ),
        name="attention_backward",
    )(
        count,
        attn_grad,
        weights,
        queries,
        keys,
        values,
        lse,
        probs,
        codes,
        table_lanes,
        normed,
        picked,
        mixed,
    )


def histogram_kernel(
    count_ref, codes_ref, low_ref, high_ref, out_ref, split_ref, both_ref, hist_ref, chosen_ref
):
    out_ref[...] = jnp.zeros_like(out_ref)

    @pl.when(count_ref[0] <= FEW)
    def _():
        unpack_codes(codes_ref, split_ref, FEW)
        both_ref[: HEADS // 2] = low_ref[...]
        both_ref[HEADS // 2 :] = high_ref[...]
        hist_ref[...] = jnp.zeros_like(hist_ref)
        add_histogram(split_ref, both_ref, hist_ref, chosen_ref, FEW)
        take_histogram(hist_ref, out_ref)


def table_histogram(count, codes, low, high):
    tokens = codes.shape[1]
    hist_shape = (TABLES * BUCKETS, HEADS * HIST_ROWS)
    whole = lambda shape: pl.BlockSpec(shape, lambda i, c: (0,) * len(shape))
    return pl.pallas_call(
        histogram_kernel,
        grid_spec=pltpu.PrefetchScalarGridSpec(
            num_scalar_prefetch=1,
            grid=(1,),
            in_specs=[whole((FEW, tokens)), whole(low.shape), whole(high.shape)],
            out_specs=whole(hist_shape),
            scratch_shapes=[
                pltpu.VMEM((TABLES, FEW, tokens), jnp.int32),
                pltpu.VMEM((HEADS, FEW, tokens), BF),
                pltpu.VMEM((HIST_ROWS * hist_shape[0], hist_shape[1]), F32),
                pltpu.VMEM((HIST_ROWS * hist_shape[0], tokens), BF),
            ],
        ),
        out_shape=jax.ShapeDtypeStruct(hist_shape, F32),
        compiler_params=pltpu.CompilerParams(vmem_limit_bytes=VMEM_LIMIT),
        cost_estimate=pl.CostEstimate(
            flops=20_000_000_000, bytes_accessed=8_000_000, transcendentals=0
        ),
        name="table_histogram",
    )(count, codes, low, high)


def key_gradients_kernel(
    count_ref,
    dq_low_ref,
    dq_high_ref,
    dk_low_ref,
    dk_high_ref,
    dv_low_ref,
    dv_high_ref,
    wq_ref,
    wk_ref,
    wv_ref,
    pack_ref,
    x_ref,
    picked_ref,
    lent_ref,
    own_ref,
    gain_ref,
    both_ref,
):
    tokens = x_ref.shape[0]
    half = D // 2
    few = count_ref[0] <= FEW

    def unit(rows):
        rows = rows.astype(F32)
        return rows * lax.rsqrt(jnp.mean(rows * rows, -1, keepdims=True) + EPS)

    def product(low, high, weight_ref):
        return dot_nt(low, weight_ref[:, :half]) + dot_nt(high, weight_ref[:, half:])

    gain_ref[...] = jnp.zeros_like(gain_ref)
    own_ref[...] = product(dq_low_ref[...], dq_high_ref[...], wq_ref)

    @pl.loop(0, tokens // COLS)
    def _(block):
        rows = pl.ds(pl.multiple_of(block * COLS, COLS), COLS)
        gain_ref[0:1, :] += jnp.sum(own_ref[rows, :] * unit(x_ref[rows, :]), 0, keepdims=True)

    def spread(keys, step):
        @pl.loop(0, keys // step)
        def _(block):
            rows = pl.ds(pl.multiple_of(block * step, step), step)
            grads = product(dk_low_ref[rows, :], dk_high_ref[rows, :], wk_ref)
            grads = grads + product(dv_low_ref[rows, :], dv_high_ref[rows, :], wv_ref)
            gain_ref[0:1, :] += jnp.sum(grads * unit(picked_ref[rows, :]), 0, keepdims=True)
            high = grads.astype(BF)
            both_ref[0, rows, :] = high
            both_ref[1, rows, :] = (grads - high.astype(F32)).astype(BF)

        high = both_ref[0, 0:keys, :]
        chosen = pack_ref[0:tokens, 0:keys]
        own_ref[...] += dot_nn(chosen, high) + dot_nn(chosen, both_ref[1, 0:keys, :])
        lent_ref[...] = dot_nn(pack_ref[tokens:, 0:keys], high).astype(BF)

    pl.when(few)(lambda: spread(FEW, FEW))
    pl.when(jnp.logical_not(few))(lambda: spread(pack_ref.shape[1], COLS))


def key_gradients(count, low, high, weights, pack, x_block, picked_x):
    tokens = x_block.shape[0]
    keys = pack.shape[0]
    whole = lambda shape: pl.BlockSpec(shape, lambda i, c: (0, 0))
    weight = lambda at: pl.BlockSpec((D, D), lambda i, c: (0, at))
    shape = jax.ShapeDtypeStruct
    return pl.pallas_call(
        key_gradients_kernel,
        grid_spec=pltpu.PrefetchScalarGridSpec(
            num_scalar_prefetch=1,
            grid=(1,),
            in_specs=[
                whole((tokens, D // 2)),
                whole((tokens, D // 2)),
                whole((keys, D // 2)),
                whole((keys, D // 2)),
                whole((keys, D // 2)),
                whole((keys, D // 2)),
                weight(0),
                weight(1),
                weight(2),
                whole(pack.shape),
                whole((tokens, D)),
                whole((keys, D)),
            ],
            out_specs=[whole((keys - tokens, D)), whole((tokens, D)), whole((8, D))],
            scratch_shapes=[pltpu.VMEM((2, keys, D), BF)],
        ),
        out_shape=[
            shape((keys - tokens, D), BF),
            shape((tokens, D), F32),
            shape((8, D), F32),
        ],
        compiler_params=pltpu.CompilerParams(vmem_limit_bytes=VMEM_LIMIT),
        cost_estimate=pl.CostEstimate(
            flops=9_000_000_000, bytes_accessed=18_000_000, transcendentals=0
        ),
        name="key_gradients",
    )(count, low[0], high[0], low[1], high[1], low[2], high[2], weights, weights, weights, pack, x_block, picked_x)


def input_kernel(own_ref, owner_ref, returned_ref, x_ref, gain_ref, middle_ref, out_ref):
    grads = own_ref[...] + dot_nn(owner_ref[...], returned_ref[...])
    rows = x_ref[...].astype(F32)
    inverse = lax.rsqrt(jnp.mean(rows * rows, -1, keepdims=True) + EPS)
    unit = rows * inverse
    weighted = grads * gain_ref[0:1, :]
    inner = jnp.mean(weighted * unit, -1, keepdims=True)
    out_ref[...] = (middle_ref[...] + inverse * (weighted - unit * inner)).astype(BF)


def input_gradient(own, owner, returned, x_block, gain_one, grad_middle):
    tokens = own.shape[0]
    streamed = lambda width: pl.BlockSpec((COLS, width), lambda i: (i, 0))
    whole = lambda shape: pl.BlockSpec(shape, lambda i: (0, 0))
    return pl.pallas_call(
        input_kernel,
        grid=(tokens // COLS,),
        in_specs=[
            streamed(D),
            streamed(owner.shape[1]),
            whole(returned.shape),
            streamed(D),
            whole((8, D)),
            streamed(D),
        ],
        out_specs=streamed(D),
        out_shape=jax.ShapeDtypeStruct((tokens, D), BF),
        compiler_params=pltpu.CompilerParams(vmem_limit_bytes=VMEM_LIMIT),
        cost_estimate=pl.CostEstimate(
            flops=1_000_000_000, bytes_accessed=8_000_000, transcendentals=0
        ),
        name="input_gradient",
    )(own, owner, returned, x_block, gain_one, grad_middle)


def on_device(
    hidden_in,
    out_cotangent,
    query_weight,
    key_weight,
    value_weight,
    output_weight,
    attn_gain,
    relative_table,
    horiz_table,
    vert_table,
    ffn_gain,
    gate_weight,
    up_weight,
    down_weight,
    key_keep,
    halo_rows,
    relative_bucket,
    horiz_bucket,
    vert_bucket,
):
    tokens = hidden_in.shape[0]
    rows = gate_weight.shape[0]
    table_share = relative_table.shape[0]
    row_index = lax.axis_index("row")
    col_index = lax.axis_index("col")
    row_count = lax.axis_size("row")
    col_count = lax.axis_size("col")
    region = row_index * col_count + col_index
    device_count = row_count * col_count

    packed_weights = pack_shards(
        (query_weight, key_weight, value_weight, output_weight, gate_weight, up_weight),
        down_weight,
    )
    weights = lax.all_gather(packed_weights, ("row", "col"), axis=0, tiled=True)
    small = jnp.stack(
        [attn_gain, ffn_gain]
        + [jnp.pad(t, (0, rows - table_share)) for t in (relative_table, horiz_table, vert_table)],
        1,
    )
    small = after(jnp.pad(small, ((0, 0), (0, 128 - small.shape[1]))), packed_weights)
    small_gather = Gather(small, 0, True)

    def turn(gathers, *done):
        for gather in gathers:
            gather.land(*done)
        return [gather.send() for gather in gathers]

    sent = turn([small_gather])

    halo_rows, key_keep, x_early = after((halo_rows, key_keep, hidden_in), sent)
    own_lists = lax.dynamic_index_in_dim(halo_rows, region, 0, keepdims=False)
    rim = x_early[own_lists]
    sent = turn([small_gather], rim)
    rim = after(rim, sent)
    above, below = shifted(rim[0:2], "row")
    left, right = shifted(rim[2:4], "col")
    neighbours = jnp.stack([region - col_count, region + col_count, region - 1, region + 1])
    present = jnp.stack(
        [row_index > 0, row_index < row_count - 1, col_index > 0, col_index < col_count - 1]
    ).astype(jnp.int32)
    list_ids = jnp.array([1, 0, 3, 2], dtype=jnp.int32)
    clipped = jnp.clip(neighbours, 0, device_count - 1)
    their_lists = after(halo_rows, rim)[clipped, list_ids]
    halo_keep = key_keep[clipped[:, None] * tokens + their_lists] * present[:, None]
    own_keep = lax.dynamic_slice_in_dim(key_keep, region * tokens, tokens)
    key_mask = jnp.concatenate([own_keep, halo_keep.reshape(-1)])
    key_total = key_mask.shape[0]

    place = jnp.cumsum(key_mask) - 1
    count = place[-1:] + 1
    scalars = jnp.concatenate([count, region.reshape(1)])
    slots = jnp.arange(key_total, dtype=jnp.int32)
    pack = ((place[:, None] == slots) & (key_mask[:, None] > 0)).astype(BF)

    sent = turn([small_gather], pack)
    packed_by, relative_bucket = after((pack, relative_bucket), sent)
    found = [
        lax.dot_general(
            packed_by, bucket.astype(BF), (((0,), (1,)), ((), ())), preferred_element_type=F32
        ).astype(jnp.int32)
        for bucket in (relative_bucket, horiz_bucket, vert_bucket)
    ]
    found_vert = jnp.where(slots[:, None] < count, found[2], BUCKETS)
    codes = found[0] + found[1] * BUCKETS + found_vert * (BUCKETS * BUCKETS)

    sent = turn([small_gather], codes)
    packed_by, above = after((pack, above), sent, codes)
    x_keys = jnp.concatenate([hidden_in, above, below, left, right], 0)
    picked_x = dot_nn(packed_by.T, x_keys).astype(BF)
    turn([small_gather], picked_x)
    while small_gather.flight is not None:
        turn([small_gather])
    small_masks = [0]
    for stage in stages_of(0)[::-1]:
        small_masks = small_masks + [mask ^ mask_of(stage) for mask in small_masks]
    place_of = [0] * device_count
    for at, mask in enumerate(small_masks):
        place_of[mask] = at
    devices = jnp.arange(device_count, dtype=jnp.int32)
    small_all = small_gather.held[jnp.array(place_of, jnp.int32)[devices ^ region]]
    gain_attn, gain_ffn = [small_all[:, :, i].reshape(-1) for i in range(2)]
    table_rows = [
        small_all[:, :table_share, 2 + t].reshape(BUCKETS, HEADS).T for t in range(TABLES)
    ]
    table_lanes = jnp.pad(
        jnp.stack(table_rows).astype(F32), ((0, 0), (0, 0), (0, 128 - BUCKETS))
    )
    table_lanes = table_lanes.at[2, :, BUCKETS].set(masked_score).reshape(TABLES * HEADS, 128)
    gain_one = gain_attn.astype(F32)
    gain_two = jnp.broadcast_to(gain_ffn.astype(F32), (8, D))

    low_bias = layout_bias(codes, table_lanes, 0)
    high_bias = layout_bias(after(codes, low_bias), table_lanes, HEADS // 2)
    x_input = hidden_in.astype(F32)
    normed_one = norm_rows(x_input, gain_one).astype(BF)
    picked = norm_rows(picked_x.astype(F32), gain_one).astype(BF)
    owner_lists = own_lists.reshape(-1)
    owner = (jnp.arange(tokens, dtype=jnp.int32)[:, None] == owner_lists).astype(BF)
    x_sum = jnp.sum(x_input * x_input, -1, keepdims=True)
    lanes = jnp.arange(128, dtype=jnp.int32)
    keep = own_keep.astype(F32)[:, None] * jnp.where(lanes == 0, x_sum, 1.0)
    weights = after(weights, high_bias, normed_one, picked, owner, keep)
    queries, keys, values, mixed, lse, probs, x_middle, normed_two = attention_forward(
        scalars,
        normed_one,
        picked,
        weights,
        codes,
        table_lanes,
        (low_bias, high_bias),
        hidden_in,
        gain_two,
    )
    uneven = down_weight.shape[0] % 8 != 0 or rows * 256 != 8 * D
    down = weights[:, weights.shape[1] - gate_weight.shape[1] :].reshape(-1, D) if uneven else None
    (
        gate_sent,
        gate_kept,
        up_sent,
        up_kept,
        down_sent,
        down_kept,
        layer_out,
        grad_middle,
        grad_attn,
        ffn_small,
    ) = feed_forward(
        scalars, normed_two, out_cotangent, x_middle, gain_two, keep, weights, down
    )
    if down_weight.shape[0] % 8 != 0:
        down_kept, down_sent = reordered(down_kept, down_sent, scatter_masks(2), region)
    ffn_chains = [
        Scatter(gate_sent, gate_kept, 0),
        Scatter(up_sent, up_kept, 1),
        Scatter(down_sent, down_kept, 2),
    ]
    rounds = Rounds()
    rounds.chains += ffn_chains

    def backward(half, kind, grad_attn):
        return attention_backward(
            half,
            kind,
            scalars,
            grad_attn,
            weights,
            queries,
            keys,
            values,
            lse,
            probs,
            codes,
            table_lanes,
            normed_one,
            picked,
            mixed,
        )

    sent = rounds.send()
    low_half = backward(0, 3, after(grad_attn, sent))
    low_chain = Scatter(low_half[5], low_half[6], 3)
    rounds.land(low_half[0])
    rounds.chains.append(low_chain)
    sent = rounds.send()
    high_half = backward(1, 0, after(grad_attn, low_half[0], sent))
    high_chain = Scatter(high_half[5], high_half[6], 0)
    rounds.land(high_half[0])
    rounds.chains.append(high_chain)
    sent = rounds.send()
    short_hist = table_histogram(
        scalars, after(codes, high_half[0], sent), low_half[3], high_half[3]
    )
    sent = rounds.turn(short_hist)
    lent, own_grads, attn_gain_part = key_gradients(
        scalars,
        low_half[:3],
        high_half[:3],
        weights,
        after(pack, short_hist, sent),
        hidden_in,
        picked_x,
    )
    hist = short_hist + jnp.concatenate([low_half[4], high_half[4]], 1)
    grad_table = jnp.sum(hist.reshape(TABLES * BUCKETS, HEADS, HIST_ROWS), -1)
    small_part = jnp.concatenate(
        [
            ffn_small[1, :128],
            ffn_small[0],
            attn_gain_part[0],
            grad_table.reshape(-1),
        ]
    ).reshape(-1, 128)
    small_rows = small_part.shape[0]
    small_part = jnp.pad(small_part, ((0, 128 - small_rows), (0, 0)))
    landed = rounds.land(lent)
    small_parts = lax.all_gather(after(small_part, landed), ("row", "col"), axis=0, tiled=True)
    sent = rounds.send()
    lent = after(lent, sent).reshape(4, -1, D)
    back_above, back_below = shifted(lent[0:2], "row")
    back_left, back_right = shifted(lent[2:4], "col")
    returned = jnp.concatenate([back_above, back_below, back_left, back_right], 0)
    returned = rounds.land_with(returned)
    sent = rounds.send()
    input_grad = input_gradient(
        own_grads,
        owner,
        after(returned, sent),
        hidden_in,
        jnp.broadcast_to(gain_one, (8, D)),
        grad_middle,
    )
    rounds.turn(input_grad)
    while rounds.chains:
        rounds.turn()
    summed = jnp.sum(small_parts.reshape(device_count, 128, 128)[:, :small_rows], 0).reshape(-1)

    residual_rms = jnp.sqrt(summed[:3] / (summed[3] * D))
    own_part = lambda at, size: lax.dynamic_slice_in_dim(summed, at + region * size, size)
    ffn_gain_grad = own_part(128, rows)
    attn_gain_grad = own_part(128 + D, rows)
    table_at = 128 + 2 * D
    table_grads = [own_part(table_at + t * BUCKETS * HEADS, table_share) for t in range(TABLES)]
    gate_grad, up_grad, down_grad = [
        total[0] for total in piece_sums([[chain] for chain in ffn_chains], False, F32)
    ]
    sides = [
        total[0] for total in piece_sums([[low_chain], [high_chain]], False, F32)
    ]
    width = D // 2
    query_grad, key_grad, value_grad, output_grad = [
        jnp.concatenate([side[:, i * width : (i + 1) * width] for side in sides], 1)
        for i in range(4)
    ]
    return (
        layer_out,
        input_grad,
        query_grad,
        key_grad,
        value_grad,
        output_grad,
        attn_gain_grad,
        table_grads[0],
        table_grads[1],
        table_grads[2],
        ffn_gain_grad,
        gate_grad,
        up_grad,
        down_grad,
        residual_rms,
    )


def solution(mesh):
    split = P(("row", "col"), None)
    line = P(("row", "col"))
    return jax.shard_map(
        on_device,
        mesh=mesh,
        in_specs=(split,) * 6 + (line,) * 5 + (split,) * 3 + (P(), P()) + (split,) * 3,
        out_specs=(split,) * 6 + (line,) * 5 + (split,) * 3 + (P(),),
        check_vma=False,
    )
```

```python
import functools

import jax
import jax.numpy as jnp
from jax import lax
from jax.experimental import pallas as pl
from jax.experimental.pallas import tpu as pltpu
from jax.sharding import PartitionSpec as P

D = 1024
HEADS = 16
HEAD_DIM = 64
BUCKETS = 32
TABLES = 3

EPS = 1e-06
masked_score = -1e30
FEW = 384
COLS = 128
ROWS = 64
GROUP = 4
WIDE = GROUP * HEAD_DIM
HIST_ROWS = 16
FF_TILE = 256
VMEM_LIMIT = 56 * 1024 * 1024
BF = jnp.bfloat16
F32 = jnp.float32


def shifted(block, axis):
    count = lax.axis_size(axis)
    forward = [(i, i + 1) for i in range(count - 1)]
    backward = [(target, source) for source, target in forward]
    return (
        lax.ppermute(block[1], axis, forward),
        lax.ppermute(block[0], axis, backward),
    )


def norm_rows(values, gain_row):
    return values * lax.rsqrt(jnp.mean(values * values, -1, keepdims=True) + EPS) * gain_row


def stages_of(kind):
    row_bits = [("row", bit) for bit in range(lax.axis_size("row").bit_length() - 1)]
    col_bits = [("col", bit) for bit in range(lax.axis_size("col").bit_length() - 1)]
    if kind == 0:
        return row_bits[:1] + col_bits + row_bits[1:]
    if kind == 1:
        return row_bits[:1] + col_bits[::-1] + row_bits[1:]
    if kind == 2:
        return row_bits[:2] + col_bits[:1] + row_bits[2:] + col_bits[1:]
    return row_bits[:2] + col_bits[::-1] + row_bits[2:]


def mask_of(stage):
    axis, bit = stage
    return (lax.axis_size("col") if axis == "row" else 1) << bit


def scatter_masks(kind):
    masks = [0]
    for stage in stages_of(kind)[::-1]:
        masks = masks + [mask ^ mask_of(stage) for mask in masks]
    return tuple(masks)


def gather_masks(kind):
    masks = [0]
    for stage in stages_of(kind)[:0:-1]:
        masks = masks + [mask ^ mask_of(stage) for mask in masks]
    return tuple(masks), mask_of(("row", 0))


def exchange(values, stage):
    axis, bit = stage
    pairs = [(i, i ^ (1 << bit)) for i in range(lax.axis_size(axis))]
    return lax.ppermute(values, axis, pairs)


def after(values, *earlier):
    return lax.optimization_barrier((values, earlier))[0]


class Gather:
    def __init__(self, shard, kind, both=False):
        self.held = shard[None]
        self.stages = stages_of(kind)[::-1] if both else stages_of(kind)[:0:-1]
        self.flight = None

    def send(self):
        if self.stages:
            self.flight = exchange(self.held, self.stages.pop(0))
        return self.held

    def land(self, *done):
        if self.flight is not None:
            if done:
                self.flight = after(self.flight, *done)
            self.held = jnp.concatenate([self.held, self.flight], 0)
            self.flight = None


class Scatter:
    def __init__(self, sent, kept, kind):
        self.stages = stages_of(kind)
        self.first = sent
        self.parts = [(kept, 0)]
        self.pieces, self.rows, self.width = sent.shape


class Rounds:
    def __init__(self):
        self.chains = []
        self.flights = []

    def land(self, *done):
        landed = [flight for chains, flight in self.flights]
        for chains, flight in self.flights:
            if done:
                flight = after(flight, *done)
            for number, chain in enumerate(chains):
                chain.parts.append((flight, number * chain.width))
        self.flights = []
        self.chains = [chain for chain in self.chains if chain.stages]
        return landed

    def send(self):
        sums, firsts = {}, []
        for chain in self.chains:
            stage = chain.stages.pop(0)
            if chain.first is not None:
                firsts.append(([chain], stage, chain.first))
                chain.first = None
            else:
                chain.pieces //= 2
                alike = (stage, chain.pieces, chain.rows, chain.width)
                sums.setdefault(alike, []).append(chain)
        sent = firsts
        if sums:
            values = piece_sums(list(sums.values()), True, BF)
            sent = sent + [
                (chains, alike[0], value)
                for (alike, chains), value in zip(sums.items(), values)
            ]
        for chains, stage, value in sent:
            self.flights.append((chains, exchange(value, stage)))
        return [value for chains, stage, value in sent]

    def turn(self, *done):
        self.land(*done)
        return self.send()


def sum_kernel(*refs, shares):
    refs = list(refs)
    outputs = refs[len(refs) - len(shares) :]
    for out_ref, (counts, width) in zip(outputs, shares):
        for number, count in enumerate(counts):
            total = refs.pop(0)[...].astype(F32)
            for _ in range(count - 1):
                total = total + refs.pop(0)[...].astype(F32)
            out_ref[:, :, number * width : (number + 1) * width] = total.astype(out_ref.dtype)


def piece_sums(groups, upper, dtype):
    steps = min([4] + [chains[0].pieces for chains in groups]) if upper else 1
    arrays, in_specs, out_specs, out_shape, shares = [], [], [], [], []
    for chains in groups:
        pieces, rows, width = chains[0].pieces, chains[0].rows, chains[0].width
        block = pieces // steps if upper else 1
        for chain in chains:
            for array, column in chain.parts:
                arrays.append(array)
                place = lambda i, lane=column // width: (steps + i if upper else 0, 0, lane)
                in_specs.append(pl.BlockSpec((block, rows, width), place))
        total = len(chains) * width
        out_specs.append(pl.BlockSpec((block, rows, total), lambda i: (i, 0, 0)))
        out_shape.append(jax.ShapeDtypeStruct((block * steps, rows, total), dtype))
        shares.append(([len(chain.parts) for chain in chains], width))
    moved = sum(2 * spec.block_shape[0] * spec.block_shape[1] * spec.block_shape[2] * steps for spec in in_specs)
    return pl.pallas_call(
        functools.partial(sum_kernel, shares=shares),
        grid=(steps,),
        in_specs=in_specs,
        out_specs=out_specs,
        out_shape=out_shape,
        compiler_params=pltpu.CompilerParams(vmem_limit_bytes=VMEM_LIMIT),
        cost_estimate=pl.CostEstimate(flops=moved, bytes_accessed=2 * moved, transcendentals=0),
        name="piece_sums",
    )(*arrays)


def totals_kernel(*refs, low_count):
    *parts, a_ref, b_ref, c_ref, d_ref = refs
    width = a_ref.shape[1] // 2
    for side, side_parts in enumerate((parts[:low_count], parts[low_count:])):
        total = side_parts[0][0].astype(F32)
        for part in side_parts[1:]:
            total = total + part[0].astype(F32)
        for number, out_ref in enumerate((a_ref, b_ref, c_ref, d_ref)):
            taken = total[:, number * width : (number + 1) * width]
            out_ref[:, side * width : (side + 1) * width] = taken


def side_totals(low, high):
    parts = low.parts + high.parts
    specs = [
        pl.BlockSpec((1, low.rows, low.width), lambda i, lane=column // low.width: (0, 0, lane))
        for array, column in parts
    ]
    return pl.pallas_call(
        functools.partial(totals_kernel, low_count=len(low.parts)),
        grid=(1,),
        in_specs=specs,
        out_specs=[pl.BlockSpec((low.rows, D), lambda i: (0, 0))] * 4,
        out_shape=[jax.ShapeDtypeStruct((low.rows, D), F32)] * 4,
        compiler_params=pltpu.CompilerParams(vmem_limit_bytes=VMEM_LIMIT),
        name="side_totals",
    )(*[array for array, column in parts])


def dot_nn(left, right):
    return lax.dot_general(left, right, (((1,), (0,)), ((), ())), preferred_element_type=F32)


def dot_nt(left, right):
    return lax.dot_general(left, right, (((1,), (1,)), ((), ())), preferred_element_type=F32)


def dot_tn(left, right):
    return lax.dot_general(left, right, (((0,), (0,)), ((), ())), preferred_element_type=F32)


def pack_kernel(*refs):
    *sources, down_ref, out_ref = refs
    at = 0
    for source_ref in sources:
        width = source_ref.shape[1]
        out_ref[:, at : at + width] = source_ref[...]
        at += width
    down = down_ref[...].astype(F32)
    for b in range(down.shape[0] // 8):
        blocks = [down[8 * b : 8 * b + 8, a * 256 : (a + 1) * 256] for a in range(D // 256)]
        out_ref[:, at + b * 256 : at + (b + 1) * 256] = jnp.concatenate(blocks, 0).astype(BF)


def pack_shards(sources, down):
    rows = sources[0].shape[0]
    widths = [source.shape[1] for source in sources]
    total = sum(widths) + down.shape[0] * D // rows
    if down.shape[0] % 8 != 0 or rows * 256 != 8 * D:
        return jnp.concatenate(list(sources) + [down.reshape(rows, -1)], 1)
    return pl.pallas_call(
        pack_kernel,
        out_shape=jax.ShapeDtypeStruct((rows, total), BF),
        compiler_params=pltpu.CompilerParams(vmem_limit_bytes=VMEM_LIMIT),
        name="pack_shards",
    )(*sources, down)


LANE_GATHER = lax.GatherDimensionNumbers(
    offset_dims=(),
    collapsed_slice_dims=(1,),
    start_index_map=(1,),
    operand_batching_dims=(0,),
    start_indices_batching_dims=(0,),
)


def lane_gather(rows, index):
    return lax.gather(
        rows,
        index[:, :, None],
        LANE_GATHER,
        (1, 1),
        mode=lax.GatherScatterMode.PROMISE_IN_BOUNDS,
    )


def lanes_of(group):
    if isinstance(group, int):
        return pl.ds(group * WIDE, WIDE)
    return pl.ds(pl.multiple_of(group * WIDE, WIDE), WIDE)


def held_type(height):
    return BF if height % 16 == 0 else F32


def reordered(low, high, masks, device):
    place = [0] * len(masks)
    for at, mask in enumerate(masks):
        place[mask] = at
    index = jnp.array(place, jnp.int32)[jnp.array(masks, jnp.int32) ^ device]
    both = jnp.concatenate([low, high], 0)[index]
    return both[: len(masks) // 2], both[len(masks) // 2 :]


def placed(owner, height):
    start = owner * height
    if isinstance(start, int):
        return pl.ds(start, height)
    if height % 8 == 0:
        start = pl.multiple_of(start, height & -height)
    return pl.ds(start, height)


def join_pieces(own_ref, other_ref, joined_ref, device, masks, core_mask, at=0):
    height = own_ref.shape[1]
    lanes = slice(at, at + own_ref.shape[2])
    for p, mask in enumerate(masks):
        joined_ref[placed(device ^ mask, height), lanes] = own_ref[p].astype(joined_ref.dtype)
        joined_ref[placed(device ^ mask ^ core_mask, height), lanes] = other_ref[p].astype(
            joined_ref.dtype
        )


def part_pieces(joined_ref, sent_ref, kept_ref, device, masks, at=0, source=0):
    half, height, width = kept_ref.shape
    width = min(width, joined_ref.shape[1])
    lanes = slice(at, at + width)
    taken = slice(source, source + width)
    for p, mask in enumerate(masks):
        target_ref = kept_ref if p < half else sent_ref
        target_ref[p % half, :, lanes] = joined_ref[placed(device ^ mask, height), taken].astype(BF)


def head_masks():
    lane = lax.broadcasted_iota(jnp.int32, (1, WIDE), 1) >> 6
    return [(lane == h).astype(F32).astype(BF) for h in range(GROUP)]


def stack_heads(block, masks):
    return jnp.concatenate([block * mask for mask in masks], 0)


def unpack_codes(codes_ref, split_ref, keys):
    code = codes_ref[:keys, :]
    split_ref[0, :keys, :] = code & 31
    split_ref[1, :keys, :] = (code >> 5) & 31
    split_ref[2, :keys, :] = code >> 10


def bias_of(split_ref, table_ref, head, keys):
    spread = [
        jnp.broadcast_to(table_ref[pl.ds(t * HEADS + head, 1), :], (keys, COLS))
        for t in range(TABLES)
    ]
    found = [lane_gather(spread[t], split_ref[t, :keys, :]) for t in range(TABLES)]
    return found[0] + found[1] + found[2]


def bias_kernel(codes_ref, table_ref, bias_ref, split_ref, *, first_head):
    unpack_codes(codes_ref, split_ref, FEW)

    @pl.loop(0, bias_ref.shape[0])
    def _(head):
        bias_ref[head] = bias_of(split_ref, table_ref, first_head + head, FEW)


def layout_bias(codes, table_lanes, first_head):
    tokens = codes.shape[1]
    return pl.pallas_call(
        functools.partial(bias_kernel, first_head=first_head),
        grid=(tokens // COLS,),
        in_specs=[
            pl.BlockSpec((FEW, COLS), lambda i: (0, i)),
            pl.BlockSpec(table_lanes.shape, lambda i: (0, 0)),
        ],
        out_specs=pl.BlockSpec((HEADS // 2, FEW, COLS), lambda i: (0, 0, i)),
        out_shape=jax.ShapeDtypeStruct((HEADS // 2, FEW, tokens), F32),
        scratch_shapes=[pltpu.VMEM((TABLES, FEW, COLS), jnp.int32)],
        compiler_params=pltpu.CompilerParams(vmem_limit_bytes=VMEM_LIMIT),
        cost_estimate=pl.CostEstimate(
            flops=16_000_000_000, bytes_accessed=7_000_000, transcendentals=0
        ),
        name="layout_bias",
    )(codes, table_lanes)


def each_group(run, groups, short):
    if short:
        for group in range(groups):
            run(group)
    else:
        lax.fori_loop(0, groups, lambda group, carry: (run(group), carry)[1], 0)


def own_blocks(turned):
    return jnp.concatenate(
        [
            turned[h * HEAD_DIM : (h + 1) * HEAD_DIM, h * COLS : (h + 1) * COLS]
            for h in range(GROUP)
        ],
        0,
    )


def attend_kernel(
    count_ref,
    normed_ref,
    picked_ref,
    wq_ref,
    wk_ref,
    wv_ref,
    wo_ref,
    codes_ref,
    table_ref,
    low_bias_ref,
    high_bias_ref,
    x_ref,
    gain_ref,
    q_ref,
    k_ref,
    v_ref,
    mixed_ref,
    lse_ref,
    prob_ref,
    mid_ref,
    normed_two_ref,
    split_ref,
    turned_ref,
    attended_ref,
):
    step = pl.program_id(0)
    few = count_ref[0] <= FEW
    total_keys = picked_ref.shape[0]

    def project(rows):
        picked = picked_ref[rows, :]
        k_ref[rows, :] = dot_nn(picked, wk_ref[...]).astype(BF)
        values = dot_nn(picked, wv_ref[...]).astype(BF)
        v_ref[rows, :] = values
        turned_ref[:, rows] = values.T

    @pl.when(step == 0)
    def _():
        q_ref[...] = dot_nn(normed_ref[...], wq_ref[...]).astype(BF)

    @pl.when(jnp.logical_and(step == 0, few))
    def _():
        project(pl.ds(0, FEW))

    @pl.when(jnp.logical_and(step == 0, jnp.logical_not(few)))
    def _():
        @pl.loop(0, total_keys // 256)
        def _(block):
            project(pl.ds(pl.multiple_of(block * 256, 256), 256))

    here = pl.ds(pl.multiple_of(step * COLS, COLS), COLS)
    masks = head_masks()

    def attend(keys, short):
        def run(group):
            lanes = lanes_of(group)
            queries = stack_heads(q_ref[here, lanes], masks)
            scores = dot_nt(k_ref[0:keys, lanes], queries)
            pieces = []
            for h in range(GROUP):
                head = group * GROUP + h
                if short:
                    half = HEADS // 2
                    bias = low_bias_ref[head] if head < half else high_bias_ref[head - half]
                else:
                    bias = bias_of(split_ref, table_ref, head, keys)
                score = scores[:, h * COLS : (h + 1) * COLS] + bias
                top = jnp.max(score, 0, keepdims=True)
                grown = jnp.exp(score - top)
                total = jnp.sum(grown, 0, keepdims=True)
                prob = grown * (1.0 / total)
                if short:
                    prob_ref[head] = prob
                lse_ref[pl.ds(head, 1), :] = top + jnp.log(total)
                pieces.append(prob.astype(BF))
            mixed = dot_nn(turned_ref[lanes, 0:keys], jnp.concatenate(pieces, 1))
            mixed_ref[lanes, here] = own_blocks(mixed).astype(BF)

        if not short:
            unpack_codes(codes_ref, split_ref, keys)
        each_group(run, HEADS // GROUP, short)

    pl.when(few)(lambda: attend(FEW, True))
    pl.when(jnp.logical_not(few))(lambda: attend(total_keys, False))

    @pl.when(step == pl.num_programs(0) - 1)
    def _():
        gain = gain_ref[0:1, :]
        attended_ref[...] = mixed_ref[...].T

        @pl.loop(0, x_ref.shape[0] // 256)
        def _(block):
            rows = pl.ds(pl.multiple_of(block * 256, 256), 256)
            middle = x_ref[rows, :].astype(F32) + dot_nn(attended_ref[rows, :], wo_ref[...])
            mid_ref[rows, :] = middle
            normed_two_ref[rows, :] = norm_rows(middle, gain).astype(BF)


def attention_forward(count, normed, picked, weights, codes, table_lanes, bias, x_block, gain_two):
    tokens = normed.shape[0]
    keys = picked.shape[0]
    full = lambda shape: pl.BlockSpec(shape, lambda i, c: (0, 0))
    weight = lambda at: pl.BlockSpec((D, D), lambda i, c: (0, at), pipeline_mode=pl.Buffered(1))
    across = lambda height: pl.BlockSpec((height, COLS), lambda i, c: (0, i))
    headed = pl.BlockSpec((HEADS, FEW, COLS), lambda i, c: (0, 0, i))
    shape = jax.ShapeDtypeStruct
    return pl.pallas_call(
        attend_kernel,
        grid_spec=pltpu.PrefetchScalarGridSpec(
            num_scalar_prefetch=1,
            grid=(tokens // COLS,),
            in_specs=[
                full((tokens, D)),
                full((keys, D)),
                weight(0),
                weight(1),
                weight(2),
                weight(3),
                across(keys),
                full(table_lanes.shape),
                pl.BlockSpec((HEADS // 2, FEW, COLS), lambda i, c: (0, 0, i)),
                pl.BlockSpec((HEADS // 2, FEW, COLS), lambda i, c: (0, 0, i)),
                full((tokens, D)),
                full((8, D)),
            ],
            out_specs=[
                full((tokens, D)),
                full((keys, D)),
                full((keys, D)),
                full((D, tokens)),
                across(HEADS),
                headed,
                full((tokens, D)),
                full((tokens, D)),
            ],
            scratch_shapes=[
                pltpu.VMEM((TABLES, keys, COLS), jnp.int32),
                pltpu.VMEM((D, keys), BF),
                pltpu.VMEM((tokens, D), BF),
            ],
        ),
        out_shape=[
            shape((tokens, D), BF),
            shape((keys, D), BF),
            shape((keys, D), BF),
            shape((D, tokens), BF),
            shape((HEADS, tokens), F32),
            shape((HEADS, FEW, tokens), F32),
            shape((tokens, D), F32),
            shape((tokens, D), BF),
        ],
        compiler_params=pltpu.CompilerParams(vmem_limit_bytes=VMEM_LIMIT),
        cost_estimate=pl.CostEstimate(
            flops=20_000_000_000, bytes_accessed=50_000_000, transcendentals=3_000_000
        ),
        name="attention_forward",
    )(count, normed, picked, weights, weights, weights, weights, codes, table_lanes, *bias, x_block, gain_two)


def ffn_kernel(
    scalar_ref,
    normed_ref,
    out_cot_ref,
    mid_ref,
    gain_ref,
    keep_ref,
    gate_ref,
    up_ref,
    packed_ref,
    gate_sent_ref,
    gate_kept_ref,
    up_sent_ref,
    up_kept_ref,
    down_sent_ref,
    down_kept_ref,
    layer_ref,
    middle_grad_ref,
    attn_grad_ref,
    gain_grad_ref,
    turned_ref,
    branch_ref,
    back_ref,
    down_all_ref,
    gate_grad_ref,
    up_grad_ref,
    down_ref,
    landed_ref,
    landed_sem,
    *,
    scatter_order,
):
    step = pl.program_id(0)
    device = scalar_ref[1]
    down_device = device if down_kept_ref.shape[1] % 8 == 0 else 0

    @pl.when(step == 0)
    def _():
        if landed_ref.shape[0] == D:
            at = packed_ref.shape[1] - landed_ref.shape[1]
            source_ref = packed_ref.at[:, at:]
        else:
            source_ref = packed_ref
        copy = pltpu.make_async_copy(source_ref, landed_ref, landed_sem)
        copy.start()
        turned_ref[...] = normed_ref[...].T
        copy.wait()
        if landed_ref.shape[0] != D:
            down_all_ref[...] = landed_ref[...].astype(F32)
        else:
            height = landed_ref.shape[1] // 32
            for d in range(D // 32):
                for b in range(height // 8):
                    block = landed_ref[d * 32 : (d + 1) * 32, b * 256 : (b + 1) * 256].astype(F32)
                    rows = slice(d * height + 8 * b, d * height + 8 * b + 8)
                    for a in range(D // 256):
                        lanes = slice(a * 256, (a + 1) * 256)
                        down_all_ref[rows, lanes] = block[8 * a : 8 * a + 8]
        branch_ref[...] = jnp.zeros_like(branch_ref)
        back_ref[...] = jnp.zeros_like(back_ref)

    here = pl.ds(pl.multiple_of(step * FF_TILE, FF_TILE), FF_TILE)
    down_ref[...] = down_all_ref[here, :].astype(BF)

    normed = normed_ref[...]
    gate = dot_nn(normed, gate_ref[...])
    up = dot_nn(normed, up_ref[...])
    grad_act = dot_nt(out_cot_ref[...], down_ref[...])
    scale = 0.7978845608028654
    square = gate * gate
    bent = jnp.tanh(scale * (gate + 0.044715 * (square * gate)))
    half = 0.5 * (1.0 + bent)
    curved = gate * half
    slope = half + 0.5 * gate * (1.0 - bent * bent) * (scale * (1.0 + 0.134145 * square))
    activated = (curved * up).astype(BF)
    grad_gate = (grad_act * up * slope).astype(BF)
    grad_up = (grad_act * curved).astype(BF)
    branch_ref[...] += dot_nn(activated, down_ref[...])
    back_ref[...] += dot_nt(grad_gate, gate_ref[...]) + dot_nt(grad_up, up_ref[...])
    gate_grad_ref[...] = dot_nn(turned_ref[...], grad_gate).astype(gate_grad_ref.dtype)
    part_pieces(gate_grad_ref, gate_sent_ref, gate_kept_ref, device, scatter_order[0])
    up_grad_ref[...] = dot_nn(turned_ref[...], grad_up).astype(up_grad_ref.dtype)
    part_pieces(up_grad_ref, up_sent_ref, up_kept_ref, device, scatter_order[1])
    down_all_ref[here, :] = dot_tn(activated, out_cot_ref[...])

    @pl.when(step == pl.num_programs(0) - 1)
    def _():
        part_pieces(
            down_all_ref, down_sent_ref, down_kept_ref, down_device, scatter_order[2]
        )
        gain = gain_ref[0:1, :]
        gain_grad_ref[...] = jnp.zeros_like(gain_grad_ref)
        lane = lax.broadcasted_iota(jnp.int32, (ROWS, 128), 1)

        @pl.loop(0, mid_ref.shape[0] // ROWS)
        def _(block):
            rows = pl.ds(pl.multiple_of(block * ROWS, ROWS), ROWS)
            middle = mid_ref[rows, :]
            final = middle + branch_ref[rows, :]
            layer_ref[rows, :] = final.astype(BF)
            mid_sum = jnp.sum(middle * middle, -1, keepdims=True)
            final_sum = jnp.sum(final * final, -1, keepdims=True)
            sums = jnp.where(lane == 1, mid_sum, jnp.where(lane == 2, final_sum, 1.0))
            gain_grad_ref[1:2, :128] += jnp.sum(keep_ref[rows, :] * sums, 0, keepdims=True)
            inverse = lax.rsqrt(mid_sum * (1.0 / D) + EPS)
            unit = middle * inverse
            grad_normed = back_ref[rows, :]
            weighted = grad_normed * gain
            inner = jnp.mean(weighted * unit, -1, keepdims=True)
            grad_middle = out_cot_ref[rows, :].astype(F32) + inverse * (weighted - unit * inner)
            middle_grad_ref[rows, :] = grad_middle
            attn_grad_ref[rows, :] = grad_middle.astype(BF)
            gain_grad_ref[0:1, :] += jnp.sum(grad_normed * unit, 0, keepdims=True)


def feed_forward(scalars, normed_two, out_cot, middle, gain_two, keep, weights, down):
    tokens = normed_two.shape[0]
    ff = (weights.shape[1] - 4 * D) // 3
    half = lax.axis_size("row") * lax.axis_size("col") // 2
    down_rows = ff // (2 * half)
    rows = D // (2 * half)
    gate_at = 4 * D // FF_TILE
    up_at = gate_at + ff // FF_TILE
    once = pl.Buffered(1)
    full = lambda shape: pl.BlockSpec(shape, lambda i, c: (0,) * len(shape), pipeline_mode=once)
    tile = pl.BlockSpec((half, rows, FF_TILE), lambda i, c: (0, 0, i))
    shape = jax.ShapeDtypeStruct
    kernel = functools.partial(
        ffn_kernel,
        scatter_order=[scatter_masks(kind) for kind in range(3)],
    )
    return pl.pallas_call(
        kernel,
        grid_spec=pltpu.PrefetchScalarGridSpec(
            num_scalar_prefetch=1,
            grid=(ff // FF_TILE,),
            in_specs=[
                full((tokens, D)),
                full((tokens, D)),
                full((tokens, D)),
                full((8, D)),
                full((tokens, 128)),
                pl.BlockSpec((D, FF_TILE), lambda i, c: (0, gate_at + i)),
                pl.BlockSpec((D, FF_TILE), lambda i, c: (0, up_at + i)),
                pl.BlockSpec(memory_space=pl.ANY),
            ],
            out_specs=[
                tile,
                tile,
                tile,
                tile,
                full((half, down_rows, D)),
                full((half, down_rows, D)),
                full((tokens, D)),
                full((tokens, D)),
                full((tokens, D)),
                full((8, D)),
            ],
            scratch_shapes=[
                pltpu.VMEM((D, tokens), BF),
                pltpu.VMEM((tokens, D), F32),
                pltpu.VMEM((tokens, D), F32),
                pltpu.VMEM((ff, D), F32),
                pltpu.VMEM((D, FF_TILE), held_type(rows)),
                pltpu.VMEM((D, FF_TILE), held_type(rows)),
                pltpu.VMEM((FF_TILE, D), BF),
                pltpu.VMEM((ff, D) if down is not None else (D, ff), BF),
                pltpu.SemaphoreType.DMA(()),
            ],
        ),
        out_shape=[shape((half, rows, ff), BF)] * 4
        + [shape((half, down_rows, D), BF)] * 2
        + [
            shape((tokens, D), BF),
            shape((tokens, D), F32),
            shape((tokens, D), BF),
            shape((8, D), F32),
        ],
        compiler_params=pltpu.CompilerParams(vmem_limit_bytes=VMEM_LIMIT),
        cost_estimate=pl.CostEstimate(
            flops=27_000_000_000, bytes_accessed=44_000_000, transcendentals=1_500_000
        ),
        name="feed_forward",
    )(scalars, normed_two, out_cot, middle, gain_two, keep, weights, weights, weights if down is None else down)


def add_histogram(split_ref, grad_ref, hist_ref, chosen_ref, keys):
    heads = grad_ref.shape[0]
    cols = split_ref.shape[2]
    bucket = lax.broadcasted_iota(jnp.int32, (BUCKETS, cols), 0)

    @pl.loop(0, keys // HIST_ROWS)
    def _(block):
        base = pl.multiple_of(block * HIST_ROWS, HIST_ROWS)
        grads = grad_ref[:, pl.ds(base, HIST_ROWS), :]
        grads = grads.reshape(heads * HIST_ROWS, cols)
        for row in range(HIST_ROWS):
            for t in range(TABLES):
                at = (row * TABLES + t) * BUCKETS
                match = split_ref[t, pl.ds(base + row, 1), :] == bucket
                chosen_ref[at : at + BUCKETS, :] = match.astype(F32).astype(BF)
        hist_ref[...] += dot_nt(chosen_ref[...], grads)


def take_histogram(hist_ref, out_ref):
    height, width = out_ref.shape
    own = lax.broadcasted_iota(jnp.int32, (height, width), 1) & (HIST_ROWS - 1)
    total = jnp.zeros((height, width), F32)
    for row in range(HIST_ROWS):
        piece = hist_ref[row * height : (row + 1) * height, :]
        total = total + jnp.where(own == row, piece, 0.0)
    out_ref[...] = total


def backward_kernel(
    count_ref,
    attn_grad_ref,
    wo_ref,
    q_ref,
    k_ref,
    v_ref,
    lse_ref,
    prob_ref,
    codes_ref,
    table_ref,
    normed_ref,
    picked_ref,
    mixed_ref,
    dq_ref,
    dk_ref,
    dv_ref,
    grad_ref,
    hist_out_ref,
    sent_ref,
    kept_ref,
    back_ref,
    split_ref,
    long_grad_ref,
    turned_ref,
    dq_turned_ref,
    dk_sum_ref,
    dv_sum_ref,
    hist_ref,
    chosen_ref,
    joined_ref,
    *,
    first_head,
    scatter_order,
):
    step = pl.program_id(0)
    few = count_ref[0] <= FEW
    total_keys = k_ref.shape[0]
    heads = q_ref.shape[1] // HEAD_DIM

    @pl.when(step == 0)
    def _():
        back_ref[...] = dot_nt(attn_grad_ref[...], wo_ref[...]).astype(BF)
        dk_sum_ref[...] = jnp.zeros_like(dk_sum_ref)
        dv_sum_ref[...] = jnp.zeros_like(dv_sum_ref)
        hist_ref[...] = jnp.zeros_like(hist_ref)

    @pl.when(jnp.logical_and(step == 0, few))
    def _():
        turned_ref[:, 0:FEW] = k_ref[0:FEW, :].T

    @pl.when(jnp.logical_and(step == 0, jnp.logical_not(few)))
    def _():
        turned_ref[...] = k_ref[...].T

    here = pl.ds(pl.multiple_of(step * COLS, COLS), COLS)
    masks = head_masks()

    def turn_back(keys, short):
        def run(group):
            lanes = lanes_of(group)
            queries = stack_heads(q_ref[here, lanes], masks)
            grads = stack_heads(back_ref[here, lanes], masks)
            prob_grads = dot_nt(v_ref[0:keys, lanes], grads)
            if not short:
                scores = dot_nt(k_ref[0:keys, lanes], queries)
            score_grads = []
            probs = []
            for h in range(GROUP):
                cols = slice(h * COLS, (h + 1) * COLS)
                local = group * GROUP + h
                if short:
                    prob = prob_ref[local]
                else:
                    head = first_head + local
                    bias = bias_of(split_ref, table_ref, head, keys)
                    prob = jnp.exp(scores[:, cols] + bias - lse_ref[pl.ds(head, 1), :])
                weighted = prob * prob_grads[:, cols]
                inner = jnp.sum(weighted, 0, keepdims=True)
                score_grad = (weighted - prob * inner).astype(BF)
                if short:
                    grad_ref[local] = score_grad
                else:
                    long_grad_ref[local] = score_grad
                score_grads.append(score_grad)
                probs.append(prob.astype(BF))
            score_grads = jnp.concatenate(score_grads, 1)
            probs = jnp.concatenate(probs, 1)
            dq_turned_ref[lanes, here] = own_blocks(
                dot_nn(turned_ref[lanes, 0:keys], score_grads)
            ).astype(BF)
            dk_sum_ref[0:keys, lanes] += dot_nn(score_grads, queries)
            dv_sum_ref[0:keys, lanes] += dot_nn(probs, grads)

        if not short:
            unpack_codes(codes_ref, split_ref, keys)
        each_group(run, heads // GROUP, short)
        if not short:
            add_histogram(split_ref, long_grad_ref, hist_ref, chosen_ref, keys)

    pl.when(few)(lambda: turn_back(FEW, True))
    pl.when(jnp.logical_not(few))(lambda: turn_back(total_keys, False))

    def leave(number, gradient):
        joined_ref[...] = gradient.astype(joined_ref.dtype)
        at = number * joined_ref.shape[1]
        part_pieces(joined_ref, sent_ref, kept_ref, count_ref[1], scatter_order, at)

    def finish(keys):
        leave(1, dot_tn(picked_ref[0:keys, :], dk_ref[0:keys, :]))
        leave(2, dot_tn(picked_ref[0:keys, :], dv_ref[0:keys, :]))

    @pl.when(step == pl.num_programs(0) - 1)
    def _():
        dk_ref[...] = dk_sum_ref[...].astype(BF)
        dv_ref[...] = dv_sum_ref[...].astype(BF)
        dq_ref[...] = dq_turned_ref[...].T
        leave(0, dot_tn(normed_ref[...], dq_ref[...]))
        first = first_head * HEAD_DIM
        leave(3, dot_nn(mixed_ref[...], attn_grad_ref[:, first : first + heads * HEAD_DIM]))
        take_histogram(hist_ref, hist_out_ref)
        pl.when(few)(lambda: finish(FEW))
        pl.when(jnp.logical_not(few))(lambda: finish(total_keys))


def attention_backward(
    half,
    kind,
    count,
    attn_grad,
    weights,
    queries,
    keys,
    values,
    lse,
    probs,
    codes,
    table_lanes,
    normed,
    picked,
    mixed,
):
    tokens = queries.shape[0]
    device_count = lax.axis_size("row") * lax.axis_size("col")
    rows = D // device_count
    key_total = keys.shape[0]
    heads = HEADS // 2
    width = heads * HEAD_DIM
    full = lambda shape: pl.BlockSpec(shape, lambda i, c: (0, 0))
    side = lambda height: pl.BlockSpec((height, width), lambda i, c: (0, half))
    across = lambda height: pl.BlockSpec((height, COLS), lambda i, c: (0, i))
    shape = jax.ShapeDtypeStruct
    hist_shape = (TABLES * BUCKETS, heads * HIST_ROWS)
    return pl.pallas_call(
        functools.partial(
            backward_kernel,
            first_head=half * heads,
            scatter_order=scatter_masks(kind),
        ),
        grid_spec=pltpu.PrefetchScalarGridSpec(
            num_scalar_prefetch=1,
            grid=(tokens // COLS,),
            in_specs=[
                full((tokens, D)),
                pl.BlockSpec((width, D), lambda i, c: (half, 3)),
                side(tokens),
                side(key_total),
                side(key_total),
                across(HEADS),
                pl.BlockSpec((heads, FEW, COLS), lambda i, c: (half, 0, i)),
                across(key_total),
                full(table_lanes.shape),
                full((tokens, D)),
                full((key_total, D)),
                full((D, tokens)),
            ],
            out_specs=[
                full((tokens, width)),
                full((key_total, width)),
                full((key_total, width)),
                pl.BlockSpec((heads, FEW, COLS), lambda i, c: (0, 0, i)),
                full(hist_shape),
            ]
            + [
                pl.BlockSpec((device_count // 2, rows, 4 * width), lambda i, c: (0, 0, 0)),
            ]
            * 2,
            scratch_shapes=[
                pltpu.VMEM((tokens, width), BF),
                pltpu.VMEM((TABLES, key_total, COLS), jnp.int32),
                pltpu.VMEM((heads, key_total, COLS), BF),
                pltpu.VMEM((width, key_total), BF),
                pltpu.VMEM((width, tokens), BF),
                pltpu.VMEM((key_total, width), F32),
                pltpu.VMEM((key_total, width), F32),
                pltpu.VMEM((HIST_ROWS * hist_shape[0], hist_shape[1]), F32),
                pltpu.VMEM((HIST_ROWS * hist_shape[0], COLS), BF),
                pltpu.VMEM((D, width), held_type(rows)),
            ],
        ),
        out_shape=[
            shape((tokens, width), BF),
            shape((key_total, width), BF),
            shape((key_total, width), BF),
            shape((heads, FEW, tokens), BF),
            shape(hist_shape, F32),
        ]
        + [shape((device_count // 2, rows, 4 * width), BF)] * 2,
        compiler_params=pltpu.CompilerParams(vmem_limit_bytes=VMEM_LIMIT),
        cost_estimate=pl.CostEstimate(
            flops=15_000_000_000, bytes_accessed=30_000_000, transcendentals=0
        ),
        name="attention_backward",
    )(
        count,
        attn_grad,
        weights,
        queries,
        keys,
        values,
        lse,
        probs,
        codes,
        table_lanes,
        normed,
        picked,
        mixed,
    )


def histogram_kernel(
    count_ref, codes_ref, low_ref, high_ref, out_ref, split_ref, both_ref, hist_ref, chosen_ref
):
    out_ref[...] = jnp.zeros_like(out_ref)

    @pl.when(count_ref[0] <= FEW)
    def _():
        unpack_codes(codes_ref, split_ref, FEW)
        both_ref[: HEADS // 2] = low_ref[...]
        both_ref[HEADS // 2 :] = high_ref[...]
        hist_ref[...] = jnp.zeros_like(hist_ref)
        add_histogram(split_ref, both_ref, hist_ref, chosen_ref, FEW)
        take_histogram(hist_ref, out_ref)


def table_histogram(count, codes, low, high):
    tokens = codes.shape[1]
    hist_shape = (TABLES * BUCKETS, HEADS * HIST_ROWS)
    whole = lambda shape: pl.BlockSpec(shape, lambda i, c: (0,) * len(shape))
    return pl.pallas_call(
        histogram_kernel,
        grid_spec=pltpu.PrefetchScalarGridSpec(
            num_scalar_prefetch=1,
            grid=(1,),
            in_specs=[whole((FEW, tokens)), whole(low.shape), whole(high.shape)],
            out_specs=whole(hist_shape),
            scratch_shapes=[
                pltpu.VMEM((TABLES, FEW, tokens), jnp.int32),
                pltpu.VMEM((HEADS, FEW, tokens), BF),
                pltpu.VMEM((HIST_ROWS * hist_shape[0], hist_shape[1]), F32),
                pltpu.VMEM((HIST_ROWS * hist_shape[0], tokens), BF),
            ],
        ),
        out_shape=jax.ShapeDtypeStruct(hist_shape, F32),
        compiler_params=pltpu.CompilerParams(vmem_limit_bytes=VMEM_LIMIT),
        cost_estimate=pl.CostEstimate(
            flops=20_000_000_000, bytes_accessed=8_000_000, transcendentals=0
        ),
        name="table_histogram",
    )(count, codes, low, high)


def key_gradients_kernel(
    count_ref,
    dq_low_ref,
    dq_high_ref,
    dk_low_ref,
    dk_high_ref,
    dv_low_ref,
    dv_high_ref,
    wq_ref,
    wk_ref,
    wv_ref,
    pack_ref,
    x_ref,
    picked_ref,
    lent_ref,
    own_ref,
    gain_ref,
    both_ref,
):
    tokens = x_ref.shape[0]
    half = D // 2
    few = count_ref[0] <= FEW

    def unit(rows):
        rows = rows.astype(F32)
        return rows * lax.rsqrt(jnp.mean(rows * rows, -1, keepdims=True) + EPS)

    def product(low, high, weight_ref):
        return dot_nt(low, weight_ref[:, :half]) + dot_nt(high, weight_ref[:, half:])

    gain_ref[...] = jnp.zeros_like(gain_ref)
    own_ref[...] = product(dq_low_ref[...], dq_high_ref[...], wq_ref)

    @pl.loop(0, tokens // COLS)
    def _(block):
        rows = pl.ds(pl.multiple_of(block * COLS, COLS), COLS)
        gain_ref[0:1, :] += jnp.sum(own_ref[rows, :] * unit(x_ref[rows, :]), 0, keepdims=True)

    def spread(keys, step):
        @pl.loop(0, keys // step)
        def _(block):
            rows = pl.ds(pl.multiple_of(block * step, step), step)
            grads = product(dk_low_ref[rows, :], dk_high_ref[rows, :], wk_ref)
            grads = grads + product(dv_low_ref[rows, :], dv_high_ref[rows, :], wv_ref)
            gain_ref[0:1, :] += jnp.sum(grads * unit(picked_ref[rows, :]), 0, keepdims=True)
            high = grads.astype(BF)
            both_ref[0, rows, :] = high
            both_ref[1, rows, :] = (grads - high.astype(F32)).astype(BF)

        high = both_ref[0, 0:keys, :]
        chosen = pack_ref[0:tokens, 0:keys]
        own_ref[...] += dot_nn(chosen, high) + dot_nn(chosen, both_ref[1, 0:keys, :])
        lent_ref[...] = dot_nn(pack_ref[tokens:, 0:keys], high).astype(BF)

    pl.when(few)(lambda: spread(FEW, FEW))
    pl.when(jnp.logical_not(few))(lambda: spread(pack_ref.shape[1], COLS))


def key_gradients(count, low, high, weights, pack, x_block, picked_x):
    tokens = x_block.shape[0]
    keys = pack.shape[0]
    whole = lambda shape: pl.BlockSpec(shape, lambda i, c: (0, 0))
    weight = lambda at: pl.BlockSpec((D, D), lambda i, c: (0, at))
    shape = jax.ShapeDtypeStruct
    return pl.pallas_call(
        key_gradients_kernel,
        grid_spec=pltpu.PrefetchScalarGridSpec(
            num_scalar_prefetch=1,
            grid=(1,),
            in_specs=[
                whole((tokens, D // 2)),
                whole((tokens, D // 2)),
                whole((keys, D // 2)),
                whole((keys, D // 2)),
                whole((keys, D // 2)),
                whole((keys, D // 2)),
                weight(0),
                weight(1),
                weight(2),
                whole(pack.shape),
                whole((tokens, D)),
                whole((keys, D)),
            ],
            out_specs=[whole((keys - tokens, D)), whole((tokens, D)), whole((8, D))],
            scratch_shapes=[pltpu.VMEM((2, keys, D), BF)],
        ),
        out_shape=[
            shape((keys - tokens, D), BF),
            shape((tokens, D), F32),
            shape((8, D), F32),
        ],
        compiler_params=pltpu.CompilerParams(vmem_limit_bytes=VMEM_LIMIT),
        cost_estimate=pl.CostEstimate(
            flops=9_000_000_000, bytes_accessed=18_000_000, transcendentals=0
        ),
        name="key_gradients",
    )(count, low[0], high[0], low[1], high[1], low[2], high[2], weights, weights, weights, pack, x_block, picked_x)


def input_kernel(own_ref, owner_ref, returned_ref, x_ref, gain_ref, middle_ref, out_ref):
    grads = own_ref[...] + dot_nn(owner_ref[...], returned_ref[...])
    rows = x_ref[...].astype(F32)
    inverse = lax.rsqrt(jnp.mean(rows * rows, -1, keepdims=True) + EPS)
    unit = rows * inverse
    weighted = grads * gain_ref[0:1, :]
    inner = jnp.mean(weighted * unit, -1, keepdims=True)
    out_ref[...] = (middle_ref[...] + inverse * (weighted - unit * inner)).astype(BF)


def input_gradient(own, owner, returned, x_block, gain_one, grad_middle):
    tokens = own.shape[0]
    streamed = lambda width: pl.BlockSpec((COLS, width), lambda i: (i, 0))
    whole = lambda shape: pl.BlockSpec(shape, lambda i: (0, 0))
    return pl.pallas_call(
        input_kernel,
        grid=(tokens // COLS,),
        in_specs=[
            streamed(D),
            streamed(owner.shape[1]),
            whole(returned.shape),
            streamed(D),
            whole((8, D)),
            streamed(D),
        ],
        out_specs=streamed(D),
        out_shape=jax.ShapeDtypeStruct((tokens, D), BF),
        compiler_params=pltpu.CompilerParams(vmem_limit_bytes=VMEM_LIMIT),
        cost_estimate=pl.CostEstimate(
            flops=1_000_000_000, bytes_accessed=8_000_000, transcendentals=0
        ),
        name="input_gradient",
    )(own, owner, returned, x_block, gain_one, grad_middle)


def on_device(
    hidden_in,
    out_cotangent,
    query_weight,
    key_weight,
    value_weight,
    output_weight,
    attn_gain,
    relative_table,
    horiz_table,
    vert_table,
    ffn_gain,
    gate_weight,
    up_weight,
    down_weight,
    key_keep,
    halo_rows,
    relative_bucket,
    horiz_bucket,
    vert_bucket,
):
    tokens = hidden_in.shape[0]
    rows = gate_weight.shape[0]
    table_share = relative_table.shape[0]
    row_index = lax.axis_index("row")
    col_index = lax.axis_index("col")
    row_count = lax.axis_size("row")
    col_count = lax.axis_size("col")
    region = row_index * col_count + col_index
    device_count = row_count * col_count

    packed_weights = pack_shards(
        (query_weight, key_weight, value_weight, output_weight, gate_weight, up_weight),
        down_weight,
    )
    weights = lax.all_gather(packed_weights, ("row", "col"), axis=0, tiled=True)
    small = jnp.stack(
        [attn_gain, ffn_gain]
        + [jnp.pad(t, (0, rows - table_share)) for t in (relative_table, horiz_table, vert_table)],
        1,
    )
    small = after(jnp.pad(small, ((0, 0), (0, 128 - small.shape[1]))), packed_weights)
    small_gather = Gather(small, 0, True)

    def turn(gathers, *done):
        for gather in gathers:
            gather.land(*done)
        return [gather.send() for gather in gathers]

    sent = turn([small_gather])

    halo_rows, key_keep, x_early = after((halo_rows, key_keep, hidden_in), sent)
    own_lists = lax.dynamic_index_in_dim(halo_rows, region, 0, keepdims=False)
    rim = x_early[own_lists]
    sent = turn([small_gather], rim)
    rim = after(rim, sent)
    above, below = shifted(rim[0:2], "row")
    left, right = shifted(rim[2:4], "col")
    neighbours = jnp.stack([region - col_count, region + col_count, region - 1, region + 1])
    present = jnp.stack(
        [row_index > 0, row_index < row_count - 1, col_index > 0, col_index < col_count - 1]
    ).astype(jnp.int32)
    list_ids = jnp.array([1, 0, 3, 2], dtype=jnp.int32)
    clipped = jnp.clip(neighbours, 0, device_count - 1)
    their_lists = after(halo_rows, rim)[clipped, list_ids]
    halo_keep = key_keep[clipped[:, None] * tokens + their_lists] * present[:, None]
    own_keep = lax.dynamic_slice_in_dim(key_keep, region * tokens, tokens)
    key_mask = jnp.concatenate([own_keep, halo_keep.reshape(-1)])
    key_total = key_mask.shape[0]

    place = jnp.cumsum(key_mask) - 1
    count = place[-1:] + 1
    scalars = jnp.concatenate([count, region.reshape(1)])
    slots = jnp.arange(key_total, dtype=jnp.int32)
    pack = ((place[:, None] == slots) & (key_mask[:, None] > 0)).astype(BF)

    sent = turn([small_gather], pack)
    packed_by, relative_bucket = after((pack, relative_bucket), sent)
    found = [
        lax.dot_general(
            packed_by, bucket.astype(BF), (((0,), (1,)), ((), ())), preferred_element_type=F32
        ).astype(jnp.int32)
        for bucket in (relative_bucket, horiz_bucket, vert_bucket)
    ]
    found_vert = jnp.where(slots[:, None] < count, found[2], BUCKETS)
    codes = found[0] + found[1] * BUCKETS + found_vert * (BUCKETS * BUCKETS)

    sent = turn([small_gather], codes)
    packed_by, above = after((pack, above), sent, codes)
    x_keys = jnp.concatenate([hidden_in, above, below, left, right], 0)
    picked_x = dot_nn(packed_by.T, x_keys).astype(BF)
    turn([small_gather], picked_x)
    while small_gather.flight is not None:
        turn([small_gather])
    small_masks = [0]
    for stage in stages_of(0)[::-1]:
        small_masks = small_masks + [mask ^ mask_of(stage) for mask in small_masks]
    place_of = [0] * device_count
    for at, mask in enumerate(small_masks):
        place_of[mask] = at
    devices = jnp.arange(device_count, dtype=jnp.int32)
    small_all = small_gather.held[jnp.array(place_of, jnp.int32)[devices ^ region]]
    gain_attn, gain_ffn = [small_all[:, :, i].reshape(-1) for i in range(2)]
    table_rows = [
        small_all[:, :table_share, 2 + t].reshape(BUCKETS, HEADS).T for t in range(TABLES)
    ]
    table_lanes = jnp.pad(
        jnp.stack(table_rows).astype(F32), ((0, 0), (0, 0), (0, 128 - BUCKETS))
    )
    table_lanes = table_lanes.at[2, :, BUCKETS].set(masked_score).reshape(TABLES * HEADS, 128)
    gain_one = gain_attn.astype(F32)
    gain_two = jnp.broadcast_to(gain_ffn.astype(F32), (8, D))

    low_bias = layout_bias(codes, table_lanes, 0)
    high_bias = layout_bias(after(codes, low_bias), table_lanes, HEADS // 2)
    x_input = hidden_in.astype(F32)
    normed_one = norm_rows(x_input, gain_one).astype(BF)
    picked = norm_rows(picked_x.astype(F32), gain_one).astype(BF)
    owner_lists = own_lists.reshape(-1)
    owner = (jnp.arange(tokens, dtype=jnp.int32)[:, None] == owner_lists).astype(BF)
    x_sum = jnp.sum(x_input * x_input, -1, keepdims=True)
    lanes = jnp.arange(128, dtype=jnp.int32)
    keep = own_keep.astype(F32)[:, None] * jnp.where(lanes == 0, x_sum, 1.0)
    weights = after(weights, high_bias, normed_one, picked, owner, keep)
    queries, keys, values, mixed, lse, probs, x_middle, normed_two = attention_forward(
        scalars,
        normed_one,
        picked,
        weights,
        codes,
        table_lanes,
        (low_bias, high_bias),
        hidden_in,
        gain_two,
    )
    uneven = down_weight.shape[0] % 8 != 0 or rows * 256 != 8 * D
    down = weights[:, weights.shape[1] - gate_weight.shape[1] :].reshape(-1, D) if uneven else None
    (
        gate_sent,
        gate_kept,
        up_sent,
        up_kept,
        down_sent,
        down_kept,
        layer_out,
        grad_middle,
        grad_attn,
        ffn_small,
    ) = feed_forward(
        scalars, normed_two, out_cotangent, x_middle, gain_two, keep, weights, down
    )
    if down_weight.shape[0] % 8 != 0:
        down_kept, down_sent = reordered(down_kept, down_sent, scatter_masks(2), region)
    ffn_chains = [
        Scatter(gate_sent, gate_kept, 0),
        Scatter(up_sent, up_kept, 1),
        Scatter(down_sent, down_kept, 2),
    ]
    rounds = Rounds()
    rounds.chains += ffn_chains

    def backward(half, kind, grad_attn):
        return attention_backward(
            half,
            kind,
            scalars,
            grad_attn,
            weights,
            queries,
            keys,
            values,
            lse,
            probs,
            codes,
            table_lanes,
            normed_one,
            picked,
            mixed,
        )

    sent = rounds.send()
    low_half = backward(0, 3, after(grad_attn, sent))
    low_chain = Scatter(low_half[5], low_half[6], 3)
    rounds.land(low_half[0])
    rounds.chains.append(low_chain)
    sent = rounds.send()
    high_half = backward(1, 0, after(grad_attn, low_half[0], sent))
    high_chain = Scatter(high_half[5], high_half[6], 0)
    rounds.land(high_half[0])
    rounds.chains.append(high_chain)
    sent = rounds.send()
    short_hist = table_histogram(
        scalars, after(codes, high_half[0], sent), low_half[3], high_half[3]
    )
    sent = rounds.turn(short_hist)
    lent, own_grads, attn_gain_part = key_gradients(
        scalars,
        low_half[:3],
        high_half[:3],
        weights,
        after(pack, short_hist, sent),
        hidden_in,
        picked_x,
    )
    hist = short_hist + jnp.concatenate([low_half[4], high_half[4]], 1)
    grad_table = jnp.sum(hist.reshape(TABLES * BUCKETS, HEADS, HIST_ROWS), -1)
    small_part = jnp.concatenate(
        [
            ffn_small[1, :128],
            ffn_small[0],
            attn_gain_part[0],
            grad_table.reshape(-1),
        ]
    ).reshape(-1, 128)
    small_rows = small_part.shape[0]
    small_part = jnp.pad(small_part, ((0, 128 - small_rows), (0, 0)))
    landed = rounds.land(lent)
    small_parts = lax.all_gather(after(small_part, landed), ("row", "col"), axis=0, tiled=True)
    rounds.send()
    rounds.land()
    sent = rounds.send()
    lent = after(lent, sent).reshape(4, -1, D)
    back_above, back_below = shifted(lent[0:2], "row")
    back_left, back_right = shifted(lent[2:4], "col")
    returned = jnp.concatenate([back_above, back_below, back_left, back_right], 0)
    sent = rounds.turn()
    input_grad = input_gradient(
        own_grads,
        owner,
        after(returned, sent),
        hidden_in,
        jnp.broadcast_to(gain_one, (8, D)),
        grad_middle,
    )
    rounds.turn(input_grad)
    while rounds.chains:
        rounds.turn()
    summed = jnp.sum(small_parts.reshape(device_count, 128, 128)[:, :small_rows], 0).reshape(-1)

    residual_rms = jnp.sqrt(summed[:3] / (summed[3] * D))
    own_part = lambda at, size: lax.dynamic_slice_in_dim(summed, at + region * size, size)
    ffn_gain_grad = own_part(128, rows)
    attn_gain_grad = own_part(128 + D, rows)
    table_at = 128 + 2 * D
    table_grads = [own_part(table_at + t * BUCKETS * HEADS, table_share) for t in range(TABLES)]
    gate_grad, up_grad, down_grad = [
        total[0] for total in piece_sums([[chain] for chain in ffn_chains], False, F32)
    ]
    query_grad, key_grad, value_grad, output_grad = side_totals(low_chain, high_chain)
    return (
        layer_out,
        input_grad,
        query_grad,
        key_grad,
        value_grad,
        output_grad,
        attn_gain_grad,
        table_grads[0],
        table_grads[1],
        table_grads[2],
        ffn_gain_grad,
        gate_grad,
        up_grad,
        down_grad,
        residual_rms,
    )


def solution(mesh):
    split = P(("row", "col"), None)
    line = P(("row", "col"))
    return jax.shard_map(
        on_device,
        mesh=mesh,
        in_specs=(split,) * 6 + (line,) * 5 + (split,) * 3 + (P(), P()) + (split,) * 3,
        out_specs=(split,) * 6 + (line,) * 5 + (split,) * 3 + (P(),),
        check_vma=False,
    )
```

```python
import functools

import jax
import jax.numpy as jnp
from jax import lax
from jax.experimental import pallas as pl
from jax.experimental.pallas import tpu as pltpu
from jax.sharding import PartitionSpec as P

D = 1024
HEADS = 16
HEAD_DIM = 64
BUCKETS = 32
TABLES = 3

EPS = 1e-06
masked_score = -1e30
FEW = 384
COLS = 128
ROWS = 64
GROUP = 4
WIDE = GROUP * HEAD_DIM
HIST_ROWS = 16
FF_TILE = 256
VMEM_LIMIT = 56 * 1024 * 1024
BF = jnp.bfloat16
F32 = jnp.float32


def shifted(block, axis):
    count = lax.axis_size(axis)
    forward = [(i, i + 1) for i in range(count - 1)]
    backward = [(target, source) for source, target in forward]
    return (
        lax.ppermute(block[1], axis, forward),
        lax.ppermute(block[0], axis, backward),
    )


def norm_rows(values, gain_row):
    return values * lax.rsqrt(jnp.mean(values * values, -1, keepdims=True) + EPS) * gain_row


def stages_of(kind):
    row_bits = [("row", bit) for bit in range(lax.axis_size("row").bit_length() - 1)]
    col_bits = [("col", bit) for bit in range(lax.axis_size("col").bit_length() - 1)]
    if kind == 0:
        return row_bits[:1] + col_bits + row_bits[1:]
    if kind == 1:
        return row_bits[:1] + col_bits[::-1] + row_bits[1:]
    if kind == 2:
        return row_bits[:2] + col_bits[:1] + row_bits[2:] + col_bits[1:]
    return row_bits[:2] + col_bits[::-1] + row_bits[2:]


def mask_of(stage):
    axis, bit = stage
    return (lax.axis_size("col") if axis == "row" else 1) << bit


def scatter_masks(kind):
    masks = [0]
    for stage in stages_of(kind)[::-1]:
        masks = masks + [mask ^ mask_of(stage) for mask in masks]
    return tuple(masks)


def gather_masks(kind):
    masks = [0]
    for stage in stages_of(kind)[:0:-1]:
        masks = masks + [mask ^ mask_of(stage) for mask in masks]
    return tuple(masks), mask_of(("row", 0))


def exchange(values, stage):
    axis, bit = stage
    pairs = [(i, i ^ (1 << bit)) for i in range(lax.axis_size(axis))]
    return lax.ppermute(values, axis, pairs)


def after(values, *earlier):
    return lax.optimization_barrier((values, earlier))[0]


class Gather:
    def __init__(self, shard, kind, both=False):
        self.held = shard[None]
        self.stages = stages_of(kind)[::-1] if both else stages_of(kind)[:0:-1]
        self.flight = None

    def send(self):
        if self.stages:
            self.flight = exchange(self.held, self.stages.pop(0))
        return self.held

    def land(self, *done):
        if self.flight is not None:
            if done:
                self.flight = after(self.flight, *done)
            self.held = jnp.concatenate([self.held, self.flight], 0)
            self.flight = None


class Scatter:
    def __init__(self, sent, kept, kind):
        self.stages = stages_of(kind)
        self.first = sent
        self.parts = [(kept, 0)]
        self.pieces, self.rows, self.width = sent.shape


class Rounds:
    def __init__(self):
        self.chains = []
        self.flights = []

    def land(self, *done):
        landed = [flight for chains, flight in self.flights]
        for chains, flight in self.flights:
            if done:
                flight = after(flight, *done)
            for number, chain in enumerate(chains):
                chain.parts.append((flight, number * chain.width))
        self.flights = []
        self.chains = [chain for chain in self.chains if chain.stages]
        return landed

    def send(self):
        sums, firsts = {}, []
        for chain in self.chains:
            stage = chain.stages.pop(0)
            if chain.first is not None:
                firsts.append(([chain], stage, chain.first))
                chain.first = None
            else:
                chain.pieces //= 2
                alike = (stage, chain.pieces, chain.rows, chain.width)
                sums.setdefault(alike, []).append(chain)
        sent = firsts
        if sums:
            values = piece_sums(list(sums.values()), True, BF)
            sent = sent + [
                (chains, alike[0], value)
                for (alike, chains), value in zip(sums.items(), values)
            ]
        for chains, stage, value in sent:
            self.flights.append((chains, exchange(value, stage)))
        return [value for chains, stage, value in sent]

    def turn(self, *done):
        self.land(*done)
        return self.send()


def sum_kernel(*refs, shares):
    refs = list(refs)
    outputs = refs[len(refs) - len(shares) :]
    for out_ref, (counts, width) in zip(outputs, shares):
        for number, count in enumerate(counts):
            total = refs.pop(0)[...].astype(F32)
            for _ in range(count - 1):
                total = total + refs.pop(0)[...].astype(F32)
            out_ref[:, :, number * width : (number + 1) * width] = total.astype(out_ref.dtype)


def piece_sums(groups, upper, dtype):
    steps = min([4] + [chains[0].pieces for chains in groups]) if upper else 1
    arrays, in_specs, out_specs, out_shape, shares = [], [], [], [], []
    for chains in groups:
        pieces, rows, width = chains[0].pieces, chains[0].rows, chains[0].width
        block = pieces // steps if upper else 1
        for chain in chains:
            for array, column in chain.parts:
                arrays.append(array)
                place = lambda i, lane=column // width: (steps + i if upper else 0, 0, lane)
                in_specs.append(pl.BlockSpec((block, rows, width), place))
        total = len(chains) * width
        out_specs.append(pl.BlockSpec((block, rows, total), lambda i: (i, 0, 0)))
        out_shape.append(jax.ShapeDtypeStruct((block * steps, rows, total), dtype))
        shares.append(([len(chain.parts) for chain in chains], width))
    moved = sum(2 * spec.block_shape[0] * spec.block_shape[1] * spec.block_shape[2] * steps for spec in in_specs)
    return pl.pallas_call(
        functools.partial(sum_kernel, shares=shares),
        grid=(steps,),
        in_specs=in_specs,
        out_specs=out_specs,
        out_shape=out_shape,
        compiler_params=pltpu.CompilerParams(vmem_limit_bytes=VMEM_LIMIT),
        cost_estimate=pl.CostEstimate(flops=moved, bytes_accessed=2 * moved, transcendentals=0),
        name="piece_sums",
    )(*arrays)


def totals_kernel(*refs, low_count):
    *parts, a_ref, b_ref, c_ref, d_ref = refs
    width = a_ref.shape[1] // 2
    for side, side_parts in enumerate((parts[:low_count], parts[low_count:])):
        total = side_parts[0][0].astype(F32)
        for part in side_parts[1:]:
            total = total + part[0].astype(F32)
        for number, out_ref in enumerate((a_ref, b_ref, c_ref, d_ref)):
            taken = total[:, number * width : (number + 1) * width]
            out_ref[:, side * width : (side + 1) * width] = taken


def side_totals(low, high):
    parts = low.parts + high.parts
    specs = [
        pl.BlockSpec((1, low.rows, low.width), lambda i, lane=column // low.width: (0, 0, lane))
        for array, column in parts
    ]
    return pl.pallas_call(
        functools.partial(totals_kernel, low_count=len(low.parts)),
        grid=(1,),
        in_specs=specs,
        out_specs=[pl.BlockSpec((low.rows, D), lambda i: (0, 0))] * 4,
        out_shape=[jax.ShapeDtypeStruct((low.rows, D), F32)] * 4,
        compiler_params=pltpu.CompilerParams(vmem_limit_bytes=VMEM_LIMIT),
        name="side_totals",
    )(*[array for array, column in parts])


def dot_nn(left, right):
    return lax.dot_general(left, right, (((1,), (0,)), ((), ())), preferred_element_type=F32)


def dot_nt(left, right):
    return lax.dot_general(left, right, (((1,), (1,)), ((), ())), preferred_element_type=F32)


def dot_tn(left, right):
    return lax.dot_general(left, right, (((0,), (0,)), ((), ())), preferred_element_type=F32)


def pack_kernel(*refs):
    *sources, down_ref, out_ref = refs
    at = 0
    for source_ref in sources:
        width = source_ref.shape[1]
        out_ref[:, at : at + width] = source_ref[...]
        at += width
    down = down_ref[...].astype(F32)
    for b in range(down.shape[0] // 8):
        blocks = [down[8 * b : 8 * b + 8, a * 256 : (a + 1) * 256] for a in range(D // 256)]
        out_ref[:, at + b * 256 : at + (b + 1) * 256] = jnp.concatenate(blocks, 0).astype(BF)


def pack_shards(sources, down):
    rows = sources[0].shape[0]
    widths = [source.shape[1] for source in sources]
    total = sum(widths) + down.shape[0] * D // rows
    if down.shape[0] % 8 != 0 or rows * 256 != 8 * D:
        return jnp.concatenate(list(sources) + [down.reshape(rows, -1)], 1)
    return pl.pallas_call(
        pack_kernel,
        out_shape=jax.ShapeDtypeStruct((rows, total), BF),
        compiler_params=pltpu.CompilerParams(vmem_limit_bytes=VMEM_LIMIT),
        name="pack_shards",
    )(*sources, down)


LANE_GATHER = lax.GatherDimensionNumbers(
    offset_dims=(),
    collapsed_slice_dims=(1,),
    start_index_map=(1,),
    operand_batching_dims=(0,),
    start_indices_batching_dims=(0,),
)


def lane_gather(rows, index):
    return lax.gather(
        rows,
        index[:, :, None],
        LANE_GATHER,
        (1, 1),
        mode=lax.GatherScatterMode.PROMISE_IN_BOUNDS,
    )


def lanes_of(group):
    if isinstance(group, int):
        return pl.ds(group * WIDE, WIDE)
    return pl.ds(pl.multiple_of(group * WIDE, WIDE), WIDE)


def held_type(height):
    return BF if height % 16 == 0 else F32


def reordered(low, high, masks, device):
    place = [0] * len(masks)
    for at, mask in enumerate(masks):
        place[mask] = at
    index = jnp.array(place, jnp.int32)[jnp.array(masks, jnp.int32) ^ device]
    both = jnp.concatenate([low, high], 0)[index]
    return both[: len(masks) // 2], both[len(masks) // 2 :]


def placed(owner, height):
    start = owner * height
    if isinstance(start, int):
        return pl.ds(start, height)
    if height % 8 == 0:
        start = pl.multiple_of(start, height & -height)
    return pl.ds(start, height)


def join_pieces(own_ref, other_ref, joined_ref, device, masks, core_mask, at=0):
    height = own_ref.shape[1]
    lanes = slice(at, at + own_ref.shape[2])
    for p, mask in enumerate(masks):
        joined_ref[placed(device ^ mask, height), lanes] = own_ref[p].astype(joined_ref.dtype)
        joined_ref[placed(device ^ mask ^ core_mask, height), lanes] = other_ref[p].astype(
            joined_ref.dtype
        )


def part_pieces(joined_ref, sent_ref, kept_ref, device, masks, at=0, source=0):
    half, height, width = kept_ref.shape
    width = min(width, joined_ref.shape[1])
    lanes = slice(at, at + width)
    taken = slice(source, source + width)
    for p, mask in enumerate(masks):
        target_ref = kept_ref if p < half else sent_ref
        target_ref[p % half, :, lanes] = joined_ref[placed(device ^ mask, height), taken].astype(BF)


def head_masks():
    lane = lax.broadcasted_iota(jnp.int32, (1, WIDE), 1) >> 6
    return [(lane == h).astype(F32).astype(BF) for h in range(GROUP)]


def stack_heads(block, masks):
    return jnp.concatenate([block * mask for mask in masks], 0)


def unpack_codes(codes_ref, split_ref, keys):
    code = codes_ref[:keys, :]
    split_ref[0, :keys, :] = code & 31
    split_ref[1, :keys, :] = (code >> 5) & 31
    split_ref[2, :keys, :] = code >> 10


def bias_of(split_ref, table_ref, head, keys):
    spread = [
        jnp.broadcast_to(table_ref[pl.ds(t * HEADS + head, 1), :], (keys, COLS))
        for t in range(TABLES)
    ]
    found = [lane_gather(spread[t], split_ref[t, :keys, :]) for t in range(TABLES)]
    return found[0] + found[1] + found[2]


def bias_kernel(codes_ref, table_ref, bias_ref, split_ref, *, first_head):
    unpack_codes(codes_ref, split_ref, FEW)

    @pl.loop(0, bias_ref.shape[0])
    def _(head):
        bias_ref[head] = bias_of(split_ref, table_ref, first_head + head, FEW)


def layout_bias(codes, table_lanes, first_head):
    tokens = codes.shape[1]
    return pl.pallas_call(
        functools.partial(bias_kernel, first_head=first_head),
        grid=(tokens // COLS,),
        in_specs=[
            pl.BlockSpec((FEW, COLS), lambda i: (0, i)),
            pl.BlockSpec(table_lanes.shape, lambda i: (0, 0)),
        ],
        out_specs=pl.BlockSpec((HEADS // 2, FEW, COLS), lambda i: (0, 0, i)),
        out_shape=jax.ShapeDtypeStruct((HEADS // 2, FEW, tokens), F32),
        scratch_shapes=[pltpu.VMEM((TABLES, FEW, COLS), jnp.int32)],
        compiler_params=pltpu.CompilerParams(vmem_limit_bytes=VMEM_LIMIT),
        cost_estimate=pl.CostEstimate(
            flops=16_000_000_000, bytes_accessed=7_000_000, transcendentals=0
        ),
        name="layout_bias",
    )(codes, table_lanes)


def each_group(run, groups, short):
    if short:
        for group in range(groups):
            run(group)
    else:
        lax.fori_loop(0, groups, lambda group, carry: (run(group), carry)[1], 0)


def own_blocks(turned):
    return jnp.concatenate(
        [
            turned[h * HEAD_DIM : (h + 1) * HEAD_DIM, h * COLS : (h + 1) * COLS]
            for h in range(GROUP)
        ],
        0,
    )


def attend_kernel(
    count_ref,
    normed_ref,
    picked_ref,
    wq_ref,
    wk_ref,
    wv_ref,
    wo_ref,
    codes_ref,
    table_ref,
    low_bias_ref,
    high_bias_ref,
    x_ref,
    gain_ref,
    q_ref,
    k_ref,
    v_ref,
    mixed_ref,
    lse_ref,
    prob_ref,
    mid_ref,
    normed_two_ref,
    split_ref,
    turned_ref,
    attended_ref,
):
    step = pl.program_id(0)
    few = count_ref[0] <= FEW
    total_keys = picked_ref.shape[0]

    def project(rows):
        picked = picked_ref[rows, :]
        k_ref[rows, :] = dot_nn(picked, wk_ref[...]).astype(BF)
        values = dot_nn(picked, wv_ref[...]).astype(BF)
        v_ref[rows, :] = values
        turned_ref[:, rows] = values.T

    @pl.when(step == 0)
    def _():
        q_ref[...] = dot_nn(normed_ref[...], wq_ref[...]).astype(BF)

    @pl.when(jnp.logical_and(step == 0, few))
    def _():
        project(pl.ds(0, FEW))

    @pl.when(jnp.logical_and(step == 0, jnp.logical_not(few)))
    def _():
        @pl.loop(0, total_keys // 256)
        def _(block):
            project(pl.ds(pl.multiple_of(block * 256, 256), 256))

    here = pl.ds(pl.multiple_of(step * COLS, COLS), COLS)
    masks = head_masks()

    def attend(keys, short):
        def run(group):
            lanes = lanes_of(group)
            queries = stack_heads(q_ref[here, lanes], masks)
            scores = dot_nt(k_ref[0:keys, lanes], queries)
            pieces = []
            for h in range(GROUP):
                head = group * GROUP + h
                if short:
                    half = HEADS // 2
                    bias = low_bias_ref[head] if head < half else high_bias_ref[head - half]
                else:
                    bias = bias_of(split_ref, table_ref, head, keys)
                score = scores[:, h * COLS : (h + 1) * COLS] + bias
                top = jnp.max(score, 0, keepdims=True)
                grown = jnp.exp(score - top)
                total = jnp.sum(grown, 0, keepdims=True)
                prob = grown * (1.0 / total)
                if short:
                    prob_ref[head] = prob
                lse_ref[pl.ds(head, 1), :] = top + jnp.log(total)
                pieces.append(prob.astype(BF))
            mixed = dot_nn(turned_ref[lanes, 0:keys], jnp.concatenate(pieces, 1))
            mixed_ref[lanes, here] = own_blocks(mixed).astype(BF)

        if not short:
            unpack_codes(codes_ref, split_ref, keys)
        each_group(run, HEADS // GROUP, short)

    pl.when(few)(lambda: attend(FEW, True))
    pl.when(jnp.logical_not(few))(lambda: attend(total_keys, False))

    @pl.when(step == pl.num_programs(0) - 1)
    def _():
        gain = gain_ref[0:1, :]
        attended_ref[...] = mixed_ref[...].T

        @pl.loop(0, x_ref.shape[0] // 256)
        def _(block):
            rows = pl.ds(pl.multiple_of(block * 256, 256), 256)
            middle = x_ref[rows, :].astype(F32) + dot_nn(attended_ref[rows, :], wo_ref[...])
            mid_ref[rows, :] = middle
            normed_two_ref[rows, :] = norm_rows(middle, gain).astype(BF)


def attention_forward(count, normed, picked, weights, codes, table_lanes, bias, x_block, gain_two):
    tokens = normed.shape[0]
    keys = picked.shape[0]
    full = lambda shape: pl.BlockSpec(shape, lambda i, c: (0, 0))
    weight = lambda at: pl.BlockSpec((D, D), lambda i, c: (0, at), pipeline_mode=pl.Buffered(1))
    across = lambda height: pl.BlockSpec((height, COLS), lambda i, c: (0, i))
    headed = pl.BlockSpec((HEADS, FEW, COLS), lambda i, c: (0, 0, i))
    shape = jax.ShapeDtypeStruct
    return pl.pallas_call(
        attend_kernel,
        grid_spec=pltpu.PrefetchScalarGridSpec(
            num_scalar_prefetch=1,
            grid=(tokens // COLS,),
            in_specs=[
                full((tokens, D)),
                full((keys, D)),
                weight(0),
                weight(1),
                weight(2),
                weight(3),
                across(keys),
                full(table_lanes.shape),
                pl.BlockSpec((HEADS // 2, FEW, COLS), lambda i, c: (0, 0, i)),
                pl.BlockSpec((HEADS // 2, FEW, COLS), lambda i, c: (0, 0, i)),
                full((tokens, D)),
                full((8, D)),
            ],
            out_specs=[
                full((tokens, D)),
                full((keys, D)),
                full((keys, D)),
                full((D, tokens)),
                across(HEADS),
                headed,
                full((tokens, D)),
                full((tokens, D)),
            ],
            scratch_shapes=[
                pltpu.VMEM((TABLES, keys, COLS), jnp.int32),
                pltpu.VMEM((D, keys), BF),
                pltpu.VMEM((tokens, D), BF),
            ],
        ),
        out_shape=[
            shape((tokens, D), BF),
            shape((keys, D), BF),
            shape((keys, D), BF),
            shape((D, tokens), BF),
            shape((HEADS, tokens), F32),
            shape((HEADS, FEW, tokens), F32),
            shape((tokens, D), F32),
            shape((tokens, D), BF),
        ],
        compiler_params=pltpu.CompilerParams(vmem_limit_bytes=VMEM_LIMIT),
        cost_estimate=pl.CostEstimate(
            flops=20_000_000_000, bytes_accessed=50_000_000, transcendentals=3_000_000
        ),
        name="attention_forward",
    )(count, normed, picked, weights, weights, weights, weights, codes, table_lanes, *bias, x_block, gain_two)


def ffn_kernel(
    scalar_ref,
    normed_ref,
    out_cot_ref,
    mid_ref,
    gain_ref,
    keep_ref,
    gate_ref,
    up_ref,
    packed_ref,
    gate_sent_ref,
    gate_kept_ref,
    up_sent_ref,
    up_kept_ref,
    down_sent_ref,
    down_kept_ref,
    layer_ref,
    middle_grad_ref,
    attn_grad_ref,
    gain_grad_ref,
    turned_ref,
    branch_ref,
    back_ref,
    down_all_ref,
    gate_grad_ref,
    up_grad_ref,
    down_ref,
    landed_ref,
    landed_sem,
    *,
    scatter_order,
):
    step = pl.program_id(0)
    device = scalar_ref[1]
    down_device = device if down_kept_ref.shape[1] % 8 == 0 else 0

    @pl.when(step == 0)
    def _():
        if landed_ref.shape[0] == D:
            at = packed_ref.shape[1] - landed_ref.shape[1]
            source_ref = packed_ref.at[:, at:]
        else:
            source_ref = packed_ref
        copy = pltpu.make_async_copy(source_ref, landed_ref, landed_sem)
        copy.start()
        turned_ref[...] = normed_ref[...].T
        copy.wait()
        if landed_ref.shape[0] != D:
            down_all_ref[...] = landed_ref[...].astype(F32)
        else:
            height = landed_ref.shape[1] // 32
            for d in range(D // 32):
                for b in range(height // 8):
                    block = landed_ref[d * 32 : (d + 1) * 32, b * 256 : (b + 1) * 256].astype(F32)
                    rows = slice(d * height + 8 * b, d * height + 8 * b + 8)
                    for a in range(D // 256):
                        lanes = slice(a * 256, (a + 1) * 256)
                        down_all_ref[rows, lanes] = block[8 * a : 8 * a + 8]
        branch_ref[...] = jnp.zeros_like(branch_ref)
        back_ref[...] = jnp.zeros_like(back_ref)

    here = pl.ds(pl.multiple_of(step * FF_TILE, FF_TILE), FF_TILE)
    down_ref[...] = down_all_ref[here, :].astype(BF)

    normed = normed_ref[...]
    gate = dot_nn(normed, gate_ref[...])
    up = dot_nn(normed, up_ref[...])
    grad_act = dot_nt(out_cot_ref[...], down_ref[...])
    scale = 0.7978845608028654
    square = gate * gate
    bent = jnp.tanh(scale * (gate + 0.044715 * (square * gate)))
    half = 0.5 * (1.0 + bent)
    curved = gate * half
    slope = half + 0.5 * gate * (1.0 - bent * bent) * (scale * (1.0 + 0.134145 * square))
    activated = (curved * up).astype(BF)
    grad_gate = (grad_act * up * slope).astype(BF)
    grad_up = (grad_act * curved).astype(BF)
    branch_ref[...] += dot_nn(activated, down_ref[...])
    back_ref[...] += dot_nt(grad_gate, gate_ref[...]) + dot_nt(grad_up, up_ref[...])
    gate_grad_ref[...] = dot_nn(turned_ref[...], grad_gate).astype(gate_grad_ref.dtype)
    part_pieces(gate_grad_ref, gate_sent_ref, gate_kept_ref, device, scatter_order[0])
    up_grad_ref[...] = dot_nn(turned_ref[...], grad_up).astype(up_grad_ref.dtype)
    part_pieces(up_grad_ref, up_sent_ref, up_kept_ref, device, scatter_order[1])
    down_all_ref[here, :] = dot_tn(activated, out_cot_ref[...])

    @pl.when(step == pl.num_programs(0) - 1)
    def _():
        part_pieces(
            down_all_ref, down_sent_ref, down_kept_ref, down_device, scatter_order[2]
        )
        gain = gain_ref[0:1, :]
        gain_grad_ref[...] = jnp.zeros_like(gain_grad_ref)
        lane = lax.broadcasted_iota(jnp.int32, (ROWS, 128), 1)

        @pl.loop(0, mid_ref.shape[0] // ROWS)
        def _(block):
            rows = pl.ds(pl.multiple_of(block * ROWS, ROWS), ROWS)
            middle = mid_ref[rows, :]
            final = middle + branch_ref[rows, :]
            layer_ref[rows, :] = final.astype(BF)
            mid_sum = jnp.sum(middle * middle, -1, keepdims=True)
            final_sum = jnp.sum(final * final, -1, keepdims=True)
            sums = jnp.where(lane == 1, mid_sum, jnp.where(lane == 2, final_sum, 1.0))
            gain_grad_ref[1:2, :128] += jnp.sum(keep_ref[rows, :] * sums, 0, keepdims=True)
            inverse = lax.rsqrt(mid_sum * (1.0 / D) + EPS)
            unit = middle * inverse
            grad_normed = back_ref[rows, :]
            weighted = grad_normed * gain
            inner = jnp.mean(weighted * unit, -1, keepdims=True)
            grad_middle = out_cot_ref[rows, :].astype(F32) + inverse * (weighted - unit * inner)
            middle_grad_ref[rows, :] = grad_middle
            attn_grad_ref[rows, :] = grad_middle.astype(BF)
            gain_grad_ref[0:1, :] += jnp.sum(grad_normed * unit, 0, keepdims=True)


def feed_forward(scalars, normed_two, out_cot, middle, gain_two, keep, weights, down):
    tokens = normed_two.shape[0]
    ff = (weights.shape[1] - 4 * D) // 3
    half = lax.axis_size("row") * lax.axis_size("col") // 2
    down_rows = ff // (2 * half)
    rows = D // (2 * half)
    gate_at = 4 * D // FF_TILE
    up_at = gate_at + ff // FF_TILE
    once = pl.Buffered(1)
    full = lambda shape: pl.BlockSpec(shape, lambda i, c: (0,) * len(shape), pipeline_mode=once)
    tile = pl.BlockSpec((half, rows, FF_TILE), lambda i, c: (0, 0, i))
    shape = jax.ShapeDtypeStruct
    kernel = functools.partial(
        ffn_kernel,
        scatter_order=[scatter_masks(kind) for kind in range(3)],
    )
    return pl.pallas_call(
        kernel,
        grid_spec=pltpu.PrefetchScalarGridSpec(
            num_scalar_prefetch=1,
            grid=(ff // FF_TILE,),
            in_specs=[
                full((tokens, D)),
                full((tokens, D)),
                full((tokens, D)),
                full((8, D)),
                full((tokens, 128)),
                pl.BlockSpec((D, FF_TILE), lambda i, c: (0, gate_at + i)),
                pl.BlockSpec((D, FF_TILE), lambda i, c: (0, up_at + i)),
                pl.BlockSpec(memory_space=pl.ANY),
            ],
            out_specs=[
                tile,
                tile,
                tile,
                tile,
                full((half, down_rows, D)),
                full((half, down_rows, D)),
                full((tokens, D)),
                full((tokens, D)),
                full((tokens, D)),
                full((8, D)),
            ],
            scratch_shapes=[
                pltpu.VMEM((D, tokens), BF),
                pltpu.VMEM((tokens, D), F32),
                pltpu.VMEM((tokens, D), F32),
                pltpu.VMEM((ff, D), F32),
                pltpu.VMEM((D, FF_TILE), held_type(rows)),
                pltpu.VMEM((D, FF_TILE), held_type(rows)),
                pltpu.VMEM((FF_TILE, D), BF),
                pltpu.VMEM((ff, D) if down is not None else (D, ff), BF),
                pltpu.SemaphoreType.DMA(()),
            ],
        ),
        out_shape=[shape((half, rows, ff), BF)] * 4
        + [shape((half, down_rows, D), BF)] * 2
        + [
            shape((tokens, D), BF),
            shape((tokens, D), F32),
            shape((tokens, D), BF),
            shape((8, D), F32),
        ],
        compiler_params=pltpu.CompilerParams(vmem_limit_bytes=VMEM_LIMIT),
        cost_estimate=pl.CostEstimate(
            flops=27_000_000_000, bytes_accessed=44_000_000, transcendentals=1_500_000
        ),
        name="feed_forward",
    )(scalars, normed_two, out_cot, middle, gain_two, keep, weights, weights, weights if down is None else down)


def add_histogram(split_ref, grad_ref, hist_ref, chosen_ref, keys):
    heads = grad_ref.shape[0]
    cols = split_ref.shape[2]
    bucket = lax.broadcasted_iota(jnp.int32, (BUCKETS, cols), 0)

    @pl.loop(0, keys // HIST_ROWS)
    def _(block):
        base = pl.multiple_of(block * HIST_ROWS, HIST_ROWS)
        grads = grad_ref[:, pl.ds(base, HIST_ROWS), :]
        grads = grads.reshape(heads * HIST_ROWS, cols)
        for row in range(HIST_ROWS):
            for t in range(TABLES):
                at = (row * TABLES + t) * BUCKETS
                match = split_ref[t, pl.ds(base + row, 1), :] == bucket
                chosen_ref[at : at + BUCKETS, :] = match.astype(F32).astype(BF)
        hist_ref[...] += dot_nt(chosen_ref[...], grads)


def take_histogram(hist_ref, out_ref):
    height, width = out_ref.shape
    own = lax.broadcasted_iota(jnp.int32, (height, width), 1) & (HIST_ROWS - 1)
    total = jnp.zeros((height, width), F32)
    for row in range(HIST_ROWS):
        piece = hist_ref[row * height : (row + 1) * height, :]
        total = total + jnp.where(own == row, piece, 0.0)
    out_ref[...] = total


def backward_kernel(
    count_ref,
    attn_grad_ref,
    wo_ref,
    q_ref,
    k_ref,
    v_ref,
    lse_ref,
    prob_ref,
    codes_ref,
    table_ref,
    normed_ref,
    picked_ref,
    mixed_ref,
    dq_ref,
    dk_ref,
    dv_ref,
    grad_ref,
    hist_out_ref,
    sent_ref,
    kept_ref,
    back_ref,
    split_ref,
    long_grad_ref,
    turned_ref,
    dq_turned_ref,
    dk_sum_ref,
    dv_sum_ref,
    hist_ref,
    chosen_ref,
    joined_ref,
    *,
    first_head,
    scatter_order,
):
    step = pl.program_id(0)
    few = count_ref[0] <= FEW
    total_keys = k_ref.shape[0]
    heads = q_ref.shape[1] // HEAD_DIM

    @pl.when(step == 0)
    def _():
        back_ref[...] = dot_nt(attn_grad_ref[...], wo_ref[...]).astype(BF)

    @pl.when(jnp.logical_and(step == 0, few))
    def _():
        turned_ref[:, 0:FEW] = k_ref[0:FEW, :].T
        dk_sum_ref[0:FEW, :] = jnp.zeros_like(dk_sum_ref[0:FEW, :])
        dv_sum_ref[0:FEW, :] = jnp.zeros_like(dv_sum_ref[0:FEW, :])

    @pl.when(jnp.logical_and(step == 0, jnp.logical_not(few)))
    def _():
        turned_ref[...] = k_ref[...].T
        dk_sum_ref[...] = jnp.zeros_like(dk_sum_ref)
        dv_sum_ref[...] = jnp.zeros_like(dv_sum_ref)
        hist_ref[...] = jnp.zeros_like(hist_ref)

    here = pl.ds(pl.multiple_of(step * COLS, COLS), COLS)
    masks = head_masks()

    def turn_back(keys, short):
        def run(group):
            lanes = lanes_of(group)
            queries = stack_heads(q_ref[here, lanes], masks)
            grads = stack_heads(back_ref[here, lanes], masks)
            prob_grads = dot_nt(v_ref[0:keys, lanes], grads)
            if not short:
                scores = dot_nt(k_ref[0:keys, lanes], queries)
            score_grads = []
            probs = []
            for h in range(GROUP):
                cols = slice(h * COLS, (h + 1) * COLS)
                local = group * GROUP + h
                if short:
                    prob = prob_ref[local]
                else:
                    head = first_head + local
                    bias = bias_of(split_ref, table_ref, head, keys)
                    prob = jnp.exp(scores[:, cols] + bias - lse_ref[pl.ds(head, 1), :])
                weighted = prob * prob_grads[:, cols]
                inner = jnp.sum(weighted, 0, keepdims=True)
                score_grad = (weighted - prob * inner).astype(BF)
                if short:
                    grad_ref[local] = score_grad
                else:
                    long_grad_ref[local] = score_grad
                score_grads.append(score_grad)
                probs.append(prob.astype(BF))
            score_grads = jnp.concatenate(score_grads, 1)
            probs = jnp.concatenate(probs, 1)
            dq_turned_ref[lanes, here] = own_blocks(
                dot_nn(turned_ref[lanes, 0:keys], score_grads)
            ).astype(BF)
            dk_sum_ref[0:keys, lanes] += dot_nn(score_grads, queries)
            dv_sum_ref[0:keys, lanes] += dot_nn(probs, grads)

        if not short:
            unpack_codes(codes_ref, split_ref, keys)
        each_group(run, heads // GROUP, short)
        if not short:
            add_histogram(split_ref, long_grad_ref, hist_ref, chosen_ref, keys)

    pl.when(few)(lambda: turn_back(FEW, True))
    pl.when(jnp.logical_not(few))(lambda: turn_back(total_keys, False))

    def leave(number, gradient):
        joined_ref[...] = gradient.astype(joined_ref.dtype)
        at = number * joined_ref.shape[1]
        part_pieces(joined_ref, sent_ref, kept_ref, count_ref[1], scatter_order, at)

    def finish(keys):
        dk_ref[0:keys, :] = dk_sum_ref[0:keys, :].astype(BF)
        dv_ref[0:keys, :] = dv_sum_ref[0:keys, :].astype(BF)
        if keys == total_keys:
            take_histogram(hist_ref, hist_out_ref)
        else:
            hist_out_ref[...] = jnp.zeros_like(hist_out_ref)
        leave(1, dot_tn(picked_ref[0:keys, :], dk_ref[0:keys, :]))
        leave(2, dot_tn(picked_ref[0:keys, :], dv_ref[0:keys, :]))

    @pl.when(step == pl.num_programs(0) - 1)
    def _():
        dq_ref[...] = dq_turned_ref[...].T
        leave(0, dot_tn(normed_ref[...], dq_ref[...]))
        first = first_head * HEAD_DIM
        leave(3, dot_nn(mixed_ref[...], attn_grad_ref[:, first : first + heads * HEAD_DIM]))
        pl.when(few)(lambda: finish(FEW))
        pl.when(jnp.logical_not(few))(lambda: finish(total_keys))


def attention_backward(
    half,
    kind,
    count,
    attn_grad,
    weights,
    queries,
    keys,
    values,
    lse,
    probs,
    codes,
    table_lanes,
    normed,
    picked,
    mixed,
):
    tokens = queries.shape[0]
    device_count = lax.axis_size("row") * lax.axis_size("col")
    rows = D // device_count
    key_total = keys.shape[0]
    heads = HEADS // 2
    width = heads * HEAD_DIM
    full = lambda shape: pl.BlockSpec(shape, lambda i, c: (0, 0))
    side = lambda height: pl.BlockSpec((height, width), lambda i, c: (0, half))
    across = lambda height: pl.BlockSpec((height, COLS), lambda i, c: (0, i))
    shape = jax.ShapeDtypeStruct
    hist_shape = (TABLES * BUCKETS, heads * HIST_ROWS)
    return pl.pallas_call(
        functools.partial(
            backward_kernel,
            first_head=half * heads,
            scatter_order=scatter_masks(kind),
        ),
        grid_spec=pltpu.PrefetchScalarGridSpec(
            num_scalar_prefetch=1,
            grid=(tokens // COLS,),
            in_specs=[
                full((tokens, D)),
                pl.BlockSpec((width, D), lambda i, c: (half, 3)),
                side(tokens),
                side(key_total),
                side(key_total),
                across(HEADS),
                pl.BlockSpec((heads, FEW, COLS), lambda i, c: (half, 0, i)),
                across(key_total),
                full(table_lanes.shape),
                full((tokens, D)),
                full((key_total, D)),
                full((D, tokens)),
            ],
            out_specs=[
                full((tokens, width)),
                full((key_total, width)),
                full((key_total, width)),
                pl.BlockSpec((heads, FEW, COLS), lambda i, c: (0, 0, i)),
                full(hist_shape),
            ]
            + [
                pl.BlockSpec((device_count // 2, rows, 4 * width), lambda i, c: (0, 0, 0)),
            ]
            * 2,
            scratch_shapes=[
                pltpu.VMEM((tokens, width), BF),
                pltpu.VMEM((TABLES, key_total, COLS), jnp.int32),
                pltpu.VMEM((heads, key_total, COLS), BF),
                pltpu.VMEM((width, key_total), BF),
                pltpu.VMEM((width, tokens), BF),
                pltpu.VMEM((key_total, width), F32),
                pltpu.VMEM((key_total, width), F32),
                pltpu.VMEM((HIST_ROWS * hist_shape[0], hist_shape[1]), F32),
                pltpu.VMEM((HIST_ROWS * hist_shape[0], COLS), BF),
                pltpu.VMEM((D, width), held_type(rows)),
            ],
        ),
        out_shape=[
            shape((tokens, width), BF),
            shape((key_total, width), BF),
            shape((key_total, width), BF),
            shape((heads, FEW, tokens), BF),
            shape(hist_shape, F32),
        ]
        + [shape((device_count // 2, rows, 4 * width), BF)] * 2,
        compiler_params=pltpu.CompilerParams(vmem_limit_bytes=VMEM_LIMIT),
        cost_estimate=pl.CostEstimate(
            flops=15_000_000_000, bytes_accessed=30_000_000, transcendentals=0
        ),
        name="attention_backward",
    )(
        count,
        attn_grad,
        weights,
        queries,
        keys,
        values,
        lse,
        probs,
        codes,
        table_lanes,
        normed,
        picked,
        mixed,
    )


def histogram_kernel(
    count_ref, codes_ref, low_ref, high_ref, out_ref, split_ref, both_ref, hist_ref, chosen_ref
):
    out_ref[...] = jnp.zeros_like(out_ref)

    @pl.when(count_ref[0] <= FEW)
    def _():
        unpack_codes(codes_ref, split_ref, FEW)
        both_ref[: HEADS // 2] = low_ref[...]
        both_ref[HEADS // 2 :] = high_ref[...]
        hist_ref[...] = jnp.zeros_like(hist_ref)
        add_histogram(split_ref, both_ref, hist_ref, chosen_ref, FEW)
        take_histogram(hist_ref, out_ref)


def table_histogram(count, codes, low, high):
    tokens = codes.shape[1]
    hist_shape = (TABLES * BUCKETS, HEADS * HIST_ROWS)
    whole = lambda shape: pl.BlockSpec(shape, lambda i, c: (0,) * len(shape))
    return pl.pallas_call(
        histogram_kernel,
        grid_spec=pltpu.PrefetchScalarGridSpec(
            num_scalar_prefetch=1,
            grid=(1,),
            in_specs=[whole((FEW, tokens)), whole(low.shape), whole(high.shape)],
            out_specs=whole(hist_shape),
            scratch_shapes=[
                pltpu.VMEM((TABLES, FEW, tokens), jnp.int32),
                pltpu.VMEM((HEADS, FEW, tokens), BF),
                pltpu.VMEM((HIST_ROWS * hist_shape[0], hist_shape[1]), F32),
                pltpu.VMEM((HIST_ROWS * hist_shape[0], tokens), BF),
            ],
        ),
        out_shape=jax.ShapeDtypeStruct(hist_shape, F32),
        compiler_params=pltpu.CompilerParams(vmem_limit_bytes=VMEM_LIMIT),
        cost_estimate=pl.CostEstimate(
            flops=20_000_000_000, bytes_accessed=8_000_000, transcendentals=0
        ),
        name="table_histogram",
    )(count, codes, low, high)


def key_gradients_kernel(
    count_ref,
    dq_low_ref,
    dq_high_ref,
    dk_low_ref,
    dk_high_ref,
    dv_low_ref,
    dv_high_ref,
    wq_ref,
    wk_ref,
    wv_ref,
    pack_ref,
    x_ref,
    picked_ref,
    lent_ref,
    own_ref,
    gain_ref,
    both_ref,
):
    tokens = x_ref.shape[0]
    half = D // 2
    few = count_ref[0] <= FEW

    def unit(rows):
        rows = rows.astype(F32)
        return rows * lax.rsqrt(jnp.mean(rows * rows, -1, keepdims=True) + EPS)

    def product(low, high, weight_ref):
        return dot_nt(low, weight_ref[:, :half]) + dot_nt(high, weight_ref[:, half:])

    gain_ref[...] = jnp.zeros_like(gain_ref)
    own_ref[...] = product(dq_low_ref[...], dq_high_ref[...], wq_ref)

    @pl.loop(0, tokens // COLS)
    def _(block):
        rows = pl.ds(pl.multiple_of(block * COLS, COLS), COLS)
        gain_ref[0:1, :] += jnp.sum(own_ref[rows, :] * unit(x_ref[rows, :]), 0, keepdims=True)

    def spread(keys, step):
        @pl.loop(0, keys // step)
        def _(block):
            rows = pl.ds(pl.multiple_of(block * step, step), step)
            grads = product(dk_low_ref[rows, :], dk_high_ref[rows, :], wk_ref)
            grads = grads + product(dv_low_ref[rows, :], dv_high_ref[rows, :], wv_ref)
            gain_ref[0:1, :] += jnp.sum(grads * unit(picked_ref[rows, :]), 0, keepdims=True)
            high = grads.astype(BF)
            both_ref[0, rows, :] = high
            both_ref[1, rows, :] = (grads - high.astype(F32)).astype(BF)

        high = both_ref[0, 0:keys, :]
        chosen = pack_ref[0:tokens, 0:keys]
        own_ref[...] += dot_nn(chosen, high) + dot_nn(chosen, both_ref[1, 0:keys, :])
        lent_ref[...] = dot_nn(pack_ref[tokens:, 0:keys], high).astype(BF)

    pl.when(few)(lambda: spread(FEW, FEW))
    pl.when(jnp.logical_not(few))(lambda: spread(pack_ref.shape[1], COLS))


def key_gradients(count, low, high, weights, pack, x_block, picked_x):
    tokens = x_block.shape[0]
    keys = pack.shape[0]
    whole = lambda shape: pl.BlockSpec(shape, lambda i, c: (0, 0))
    weight = lambda at: pl.BlockSpec((D, D), lambda i, c: (0, at))
    shape = jax.ShapeDtypeStruct
    return pl.pallas_call(
        key_gradients_kernel,
        grid_spec=pltpu.PrefetchScalarGridSpec(
            num_scalar_prefetch=1,
            grid=(1,),
            in_specs=[
                whole((tokens, D // 2)),
                whole((tokens, D // 2)),
                whole((keys, D // 2)),
                whole((keys, D // 2)),
                whole((keys, D // 2)),
                whole((keys, D // 2)),
                weight(0),
                weight(1),
                weight(2),
                whole(pack.shape),
                whole((tokens, D)),
                whole((keys, D)),
            ],
            out_specs=[whole((keys - tokens, D)), whole((tokens, D)), whole((8, D))],
            scratch_shapes=[pltpu.VMEM((2, keys, D), BF)],
        ),
        out_shape=[
            shape((keys - tokens, D), BF),
            shape((tokens, D), F32),
            shape((8, D), F32),
        ],
        compiler_params=pltpu.CompilerParams(vmem_limit_bytes=VMEM_LIMIT),
        cost_estimate=pl.CostEstimate(
            flops=9_000_000_000, bytes_accessed=18_000_000, transcendentals=0
        ),
        name="key_gradients",
    )(count, low[0], high[0], low[1], high[1], low[2], high[2], weights, weights, weights, pack, x_block, picked_x)


def input_kernel(own_ref, owner_ref, returned_ref, x_ref, gain_ref, middle_ref, out_ref):
    grads = own_ref[...] + dot_nn(owner_ref[...], returned_ref[...])
    rows = x_ref[...].astype(F32)
    inverse = lax.rsqrt(jnp.mean(rows * rows, -1, keepdims=True) + EPS)
    unit = rows * inverse
    weighted = grads * gain_ref[0:1, :]
    inner = jnp.mean(weighted * unit, -1, keepdims=True)
    out_ref[...] = (middle_ref[...] + inverse * (weighted - unit * inner)).astype(BF)


def input_gradient(own, owner, returned, x_block, gain_one, grad_middle):
    tokens = own.shape[0]
    streamed = lambda width: pl.BlockSpec((COLS, width), lambda i: (i, 0))
    whole = lambda shape: pl.BlockSpec(shape, lambda i: (0, 0))
    return pl.pallas_call(
        input_kernel,
        grid=(tokens // COLS,),
        in_specs=[
            streamed(D),
            streamed(owner.shape[1]),
            whole(returned.shape),
            streamed(D),
            whole((8, D)),
            streamed(D),
        ],
        out_specs=streamed(D),
        out_shape=jax.ShapeDtypeStruct((tokens, D), BF),
        compiler_params=pltpu.CompilerParams(vmem_limit_bytes=VMEM_LIMIT),
        cost_estimate=pl.CostEstimate(
            flops=1_000_000_000, bytes_accessed=8_000_000, transcendentals=0
        ),
        name="input_gradient",
    )(own, owner, returned, x_block, gain_one, grad_middle)


def on_device(
    hidden_in,
    out_cotangent,
    query_weight,
    key_weight,
    value_weight,
    output_weight,
    attn_gain,
    relative_table,
    horiz_table,
    vert_table,
    ffn_gain,
    gate_weight,
    up_weight,
    down_weight,
    key_keep,
    halo_rows,
    relative_bucket,
    horiz_bucket,
    vert_bucket,
):
    tokens = hidden_in.shape[0]
    rows = gate_weight.shape[0]
    table_share = relative_table.shape[0]
    row_index = lax.axis_index("row")
    col_index = lax.axis_index("col")
    row_count = lax.axis_size("row")
    col_count = lax.axis_size("col")
    region = row_index * col_count + col_index
    device_count = row_count * col_count

    packed_weights = pack_shards(
        (query_weight, key_weight, value_weight, output_weight, gate_weight, up_weight),
        down_weight,
    )
    weights = lax.all_gather(packed_weights, ("row", "col"), axis=0, tiled=True)
    small = jnp.stack(
        [attn_gain, ffn_gain]
        + [jnp.pad(t, (0, rows - table_share)) for t in (relative_table, horiz_table, vert_table)],
        1,
    )
    small = after(jnp.pad(small, ((0, 0), (0, 128 - small.shape[1]))), packed_weights)
    small_gather = Gather(small, 0, True)

    def turn(gathers, *done):
        for gather in gathers:
            gather.land(*done)
        return [gather.send() for gather in gathers]

    sent = turn([small_gather])

    halo_rows, key_keep, x_early = after((halo_rows, key_keep, hidden_in), sent)
    own_lists = lax.dynamic_index_in_dim(halo_rows, region, 0, keepdims=False)
    rim = x_early[own_lists]
    sent = turn([small_gather], rim)
    rim = after(rim, sent)
    above, below = shifted(rim[0:2], "row")
    left, right = shifted(rim[2:4], "col")
    neighbours = jnp.stack([region - col_count, region + col_count, region - 1, region + 1])
    present = jnp.stack(
        [row_index > 0, row_index < row_count - 1, col_index > 0, col_index < col_count - 1]
    ).astype(jnp.int32)
    list_ids = jnp.array([1, 0, 3, 2], dtype=jnp.int32)
    clipped = jnp.clip(neighbours, 0, device_count - 1)
    their_lists = after(halo_rows, rim)[clipped, list_ids]
    halo_keep = key_keep[clipped[:, None] * tokens + their_lists] * present[:, None]
    own_keep = lax.dynamic_slice_in_dim(key_keep, region * tokens, tokens)
    key_mask = jnp.concatenate([own_keep, halo_keep.reshape(-1)])
    key_total = key_mask.shape[0]

    place = jnp.cumsum(key_mask) - 1
    count = place[-1:] + 1
    scalars = jnp.concatenate([count, region.reshape(1)])
    slots = jnp.arange(key_total, dtype=jnp.int32)
    pack = ((place[:, None] == slots) & (key_mask[:, None] > 0)).astype(BF)

    sent = turn([small_gather], pack)
    packed_by, relative_bucket = after((pack, relative_bucket), sent)
    found = [
        lax.dot_general(
            packed_by, bucket.astype(BF), (((0,), (1,)), ((), ())), preferred_element_type=F32
        ).astype(jnp.int32)
        for bucket in (relative_bucket, horiz_bucket, vert_bucket)
    ]
    found_vert = jnp.where(slots[:, None] < count, found[2], BUCKETS)
    codes = found[0] + found[1] * BUCKETS + found_vert * (BUCKETS * BUCKETS)

    sent = turn([small_gather], codes)
    packed_by, above = after((pack, above), sent, codes)
    x_keys = jnp.concatenate([hidden_in, above, below, left, right], 0)
    picked_x = dot_nn(packed_by.T, x_keys).astype(BF)
    turn([small_gather], picked_x)
    while small_gather.flight is not None:
        turn([small_gather])
    small_masks = [0]
    for stage in stages_of(0)[::-1]:
        small_masks = small_masks + [mask ^ mask_of(stage) for mask in small_masks]
    place_of = [0] * device_count
    for at, mask in enumerate(small_masks):
        place_of[mask] = at
    devices = jnp.arange(device_count, dtype=jnp.int32)
    small_all = small_gather.held[jnp.array(place_of, jnp.int32)[devices ^ region]]
    gain_attn, gain_ffn = [small_all[:, :, i].reshape(-1) for i in range(2)]
    table_rows = [
        small_all[:, :table_share, 2 + t].reshape(BUCKETS, HEADS).T for t in range(TABLES)
    ]
    table_lanes = jnp.pad(
        jnp.stack(table_rows).astype(F32), ((0, 0), (0, 0), (0, 128 - BUCKETS))
    )
    table_lanes = table_lanes.at[2, :, BUCKETS].set(masked_score).reshape(TABLES * HEADS, 128)
    gain_one = gain_attn.astype(F32)
    gain_two = jnp.broadcast_to(gain_ffn.astype(F32), (8, D))

    low_bias = layout_bias(codes, table_lanes, 0)
    high_bias = layout_bias(after(codes, low_bias), table_lanes, HEADS // 2)
    x_input = hidden_in.astype(F32)
    normed_one = norm_rows(x_input, gain_one).astype(BF)
    picked = norm_rows(picked_x.astype(F32), gain_one).astype(BF)
    owner_lists = own_lists.reshape(-1)
    owner = (jnp.arange(tokens, dtype=jnp.int32)[:, None] == owner_lists).astype(BF)
    x_sum = jnp.sum(x_input * x_input, -1, keepdims=True)
    lanes = jnp.arange(128, dtype=jnp.int32)
    keep = own_keep.astype(F32)[:, None] * jnp.where(lanes == 0, x_sum, 1.0)
    weights = after(weights, high_bias, normed_one, picked, owner, keep)
    queries, keys, values, mixed, lse, probs, x_middle, normed_two = attention_forward(
        scalars,
        normed_one,
        picked,
        weights,
        codes,
        table_lanes,
        (low_bias, high_bias),
        hidden_in,
        gain_two,
    )
    uneven = down_weight.shape[0] % 8 != 0 or rows * 256 != 8 * D
    down = weights[:, weights.shape[1] - gate_weight.shape[1] :].reshape(-1, D) if uneven else None
    (
        gate_sent,
        gate_kept,
        up_sent,
        up_kept,
        down_sent,
        down_kept,
        layer_out,
        grad_middle,
        grad_attn,
        ffn_small,
    ) = feed_forward(
        scalars, normed_two, out_cotangent, x_middle, gain_two, keep, weights, down
    )
    if down_weight.shape[0] % 8 != 0:
        down_kept, down_sent = reordered(down_kept, down_sent, scatter_masks(2), region)
    ffn_chains = [
        Scatter(gate_sent, gate_kept, 0),
        Scatter(up_sent, up_kept, 1),
        Scatter(down_sent, down_kept, 2),
    ]
    rounds = Rounds()
    rounds.chains += ffn_chains

    def backward(half, kind, grad_attn):
        return attention_backward(
            half,
            kind,
            scalars,
            grad_attn,
            weights,
            queries,
            keys,
            values,
            lse,
            probs,
            codes,
            table_lanes,
            normed_one,
            picked,
            mixed,
        )

    sent = rounds.send()
    low_half = backward(0, 3, after(grad_attn, sent))
    low_chain = Scatter(low_half[5], low_half[6], 3)
    rounds.land(low_half[0])
    rounds.chains.append(low_chain)
    sent = rounds.send()
    high_half = backward(1, 0, after(grad_attn, low_half[0], sent))
    high_chain = Scatter(high_half[5], high_half[6], 0)
    rounds.land(high_half[0])
    rounds.chains.append(high_chain)
    sent = rounds.send()
    short_hist = table_histogram(
        scalars, after(codes, high_half[0], sent), low_half[3], high_half[3]
    )
    sent = rounds.turn(short_hist)
    lent, own_grads, attn_gain_part = key_gradients(
        scalars,
        low_half[:3],
        high_half[:3],
        weights,
        after(pack, short_hist, sent),
        hidden_in,
        picked_x,
    )
    hist = short_hist + jnp.concatenate([low_half[4], high_half[4]], 1)
    grad_table = jnp.sum(hist.reshape(TABLES * BUCKETS, HEADS, HIST_ROWS), -1)
    small_part = jnp.concatenate(
        [
            ffn_small[1, :128],
            ffn_small[0],
            attn_gain_part[0],
            grad_table.reshape(-1),
        ]
    ).reshape(-1, 128)
    small_rows = small_part.shape[0]
    small_part = jnp.pad(small_part, ((0, 128 - small_rows), (0, 0)))
    landed = rounds.land(lent)
    small_parts = lax.all_gather(after(small_part, landed[:1]), ("row", "col"), axis=0, tiled=True)
    rounds.send()
    rounds.land()
    sent = rounds.send()
    lent = after(lent, sent).reshape(4, -1, D)
    back_above, back_below = shifted(lent[0:2], "row")
    back_left, back_right = shifted(lent[2:4], "col")
    returned = jnp.concatenate([back_above, back_below, back_left, back_right], 0)
    sent = rounds.turn()
    input_grad = input_gradient(
        own_grads,
        owner,
        after(returned, sent),
        hidden_in,
        jnp.broadcast_to(gain_one, (8, D)),
        grad_middle,
    )
    rounds.turn(input_grad)
    while rounds.chains:
        rounds.turn()
    summed = jnp.sum(small_parts.reshape(device_count, 128, 128)[:, :small_rows], 0).reshape(-1)

    residual_rms = jnp.sqrt(summed[:3] / (summed[3] * D))
    own_part = lambda at, size: lax.dynamic_slice_in_dim(summed, at + region * size, size)
    ffn_gain_grad = own_part(128, rows)
    attn_gain_grad = own_part(128 + D, rows)
    table_at = 128 + 2 * D
    table_grads = [own_part(table_at + t * BUCKETS * HEADS, table_share) for t in range(TABLES)]
    gate_grad, up_grad, down_grad = [
        total[0] for total in piece_sums([[chain] for chain in ffn_chains], False, F32)
    ]
    query_grad, key_grad, value_grad, output_grad = side_totals(low_chain, high_chain)
    return (
        layer_out,
        input_grad,
        query_grad,
        key_grad,
        value_grad,
        output_grad,
        attn_gain_grad,
        table_grads[0],
        table_grads[1],
        table_grads[2],
        ffn_gain_grad,
        gate_grad,
        up_grad,
        down_grad,
        residual_rms,
    )


def solution(mesh):
    split = P(("row", "col"), None)
    line = P(("row", "col"))
    return jax.shard_map(
        on_device,
        mesh=mesh,
        in_specs=(split,) * 6 + (line,) * 5 + (split,) * 3 + (P(), P()) + (split,) * 3,
        out_specs=(split,) * 6 + (line,) * 5 + (split,) * 3 + (P(),),
        check_vma=False,
    )
```
